32 devices in a mesh: dp: 8 (over z, y), tensor: 4 (over x, core).
Axes of the slice: x: 2, y: 2, z: 4, core: 2. Of those that a mesh axis runs over, the one named last changes fastest.
Arguments:
- hidden: bfloat16 [8, 2048, 768], P('dp', None, 'tensor'), may hold values from -6 to 6
- segments: int32 [8, 2048], P('dp'), may hold values from 0 to 15, never falling along the last dimension, each value on 1 to 1024 neighbouring positions
- norm_gain: float32 [768], replicated, may hold values from 0.1 to 1.9
- gate_weight: bfloat16 [768, 1536], P(None, 'tensor'), may hold values from -0.21875 to 0.21875
- inner_weight: bfloat16 [768, 1536], P(None, 'tensor'), may hold values from -0.21875 to 0.21875
- state_weight: bfloat16 [768, 256], replicated, may hold values from -0.21875 to 0.21875
- step_weight: bfloat16 [768, 24], P(None, 'tensor'), may hold values from -0.21875 to 0.21875
- inner_taps: float32 [4, 1536], P(None, 'tensor'), may hold values from -3 to 3
- inner_offset: float32 [1536], P('tensor'), may hold values from -0.5 to 0.5
- state_taps: float32 [4, 256], replicated, may hold values from -3 to 3
- state_offset: float32 [256], replicated, may hold values from -0.5 to 0.5
- step_bias: float32 [24], P('tensor'), may hold values from -4 to -1
- decay_log: float32 [24], P('tensor'), may hold values from -1 to 2.77
- skip_weight: float32 [24], P('tensor'), may hold values from 0.3 to 3
- out_gain: float32 [1536], P('tensor'), may hold values from 0.1 to 1.9
- out_weight: bfloat16 [1536, 768], P('tensor'), may hold values from -0.15625 to 0.15625
- cotangent: bfloat16 [8, 2048, 768], P('dp', None, 'tensor'), may hold values from -6 to 6
Outputs:
- output: bfloat16 [8, 2048, 768], P('dp', None, 'tensor')
- input_grad: float32 [8, 2048, 768], P('dp', None, 'tensor')
- norm_gain_grad: float32 [768], replicated
- gate_weight_grad: float32 [768, 1536], P(None, 'tensor')
- inner_weight_grad: float32 [768, 1536], P(None, 'tensor')
- state_weight_grad: float32 [768, 256], replicated
- step_weight_grad: float32 [768, 24], P(None, 'tensor')
- inner_taps_grad: float32 [4, 1536], P(None, 'tensor')
- inner_offset_grad: float32 [1536], P('tensor')
- state_taps_grad: float32 [4, 256], replicated
- state_offset_grad: float32 [256], replicated
- step_bias_grad: float32 [24], P('tensor')
- decay_log_grad: float32 [24], P('tensor')
- skip_weight_grad: float32 [24], P('tensor')
- out_gain_grad: float32 [1536], P('tensor')
- out_weight_grad: float32 [1536, 768], P('tensor')
The draws below stay inside these ranges and needn't reach their ends.
Inputs may be any that keep to these rules, and one draw needn't show every extreme that they name: `segments`: document numbers never fall along a sequence; each document has 1 to 1024 tokens and some has exactly 1024.
All inputs are finite; a program needn't handle non-finite values.
Results may differ from the reference program's by a relative error of at most 0.0096.
Values may be sent and summed in bfloat16 or wider, within the bound.
No kernel may reach another device: no remote copies, remote signals or barrier semaphores. Data moves between devices by JAX's collectives and lax.ppermute only.
A program may use at most 128 MiB of HBM per device.

```python
import math
from functools import partial
import jax
import jax.numpy as jnp
import numpy as np
from jax import lax

D = 768
HEADS = 24
NS = 128
KW = 4
BLOCK = 256
TOK_DEV = 2048
DI = 1536
SEQS = 8
DOCS = 16
MOST_DOC = 1024


def block_levels(stream_key, dims, shards, smallest, top_value):
    def one(axis_at, blocks):
        heights = jax.random.uniform(jax.random.fold_in(jax.random.fold_in(stream_key, 6), axis_at), (blocks,), jnp.float32, smallest / len(shards), top_value / len(shards))
        return jnp.repeat(jnp.exp(heights), dims[axis_at] // blocks).reshape((-1,) + (1,) * (len(dims) - axis_at - 1))

    level = one(*shards[0])
    for cut in shards[1:]:
        level = level * one(*cut)
    return level


def split_up(amount, total, limit, lean):
    portions = [(1 << 20) // math.isqrt(rank ** lean) + 1 for rank in range(2, amount + 1)]
    rest, holding = total - limit - (amount - 1), [1] * (amount - 1)
    while rest > 0:
        movable = [i for i in range(amount - 1) if holding[i] < limit]
        whole, left = sum([portions[i] for i in movable]), rest
        for i in movable:
            more = min(limit - holding[i], max(1, left * portions[i] // whole), rest)
            holding[i] = holding[i] + more
            rest = rest - more
    return np.array([limit] + holding)


def ragged_sizes(own_key, amount, total, most, skew):
    if amount == 2:
        one = jax.random.randint(own_key, (), max(1, total - most), min(most, total - 1) + 1)
        return jnp.stack([one, total - one])
    sizes = jnp.asarray(split_up(amount, total, most, skew), jnp.int32)
    couples = (amount - 1) // 2
    donor, receiver = sizes[1:1 + 2 * couples:2], sizes[2:2 + 2 * couples:2]
    slack = jnp.minimum(donor - 1, most - receiver)
    shifted = jax.random.randint(jax.random.fold_in(own_key, 1), (couples,), 0, 1 << 20) % (slack + 1)
    sizes = sizes.at[1:1 + 2 * couples:2].set(donor - shifted).at[2:2 + 2 * couples:2].set(receiver + shifted)
    return sizes[jax.random.permutation(jax.random.fold_in(own_key, 2), amount)]


def bell_draw(rng, dims, width, limit, cuts=(), kind=jnp.bfloat16):
    entries = jax.random.normal(rng, dims, jnp.float32) * width
    if len(cuts) > 0:
        entries = block_levels(rng, dims, cuts, -0.22, 0.18) * entries
    return jnp.clip(entries, min=-limit, max=limit).astype(kind)


def setup_inputs(seed: int = 0) -> dict:
    streams_of = jax.random.split(jax.random.key(seed), 18)
    hidden = bell_draw(streams_of[0], (SEQS, TOK_DEV, D), 1.0, 6.0, ((0, 8), (2, 4)))
    segments = jax.vmap(lambda own: jnp.searchsorted(jnp.cumsum(ragged_sizes(own, DOCS, TOK_DEV, MOST_DOC, 1)), jnp.arange(TOK_DEV), side="right"))(jax.random.split(streams_of[1], SEQS)).reshape((SEQS, TOK_DEV)).astype(jnp.int32)
    norm_gain = jnp.clip(1.0 + 0.18 * jax.random.normal(streams_of[2], (D,), jnp.float32), 0.1, 1.9)
    gate_weight = bell_draw(streams_of[3], (D, DI), D ** -0.5, 0.21875, ((1, 4),))
    inner_weight = bell_draw(streams_of[4], (D, DI), D ** -0.5, 0.21875, ((1, 4),))
    state_weight = bell_draw(streams_of[5], (D, 2 * NS), D ** -0.5, 0.21875)
    step_weight = bell_draw(streams_of[6], (D, HEADS), D ** -0.5, 0.21875, ((1, 4),))
    inner_taps = bell_draw(streams_of[7], (KW, DI), 0.5, 3.0, ((1, 4),), jnp.float32)
    inner_offset = jnp.clip(jax.random.uniform(streams_of[8], (DI,), jnp.float32, -0.5, 0.5) * block_levels(streams_of[8], (DI,), ((0, 4),), -0.4, 0.0), -0.5, 0.5)
    state_taps = bell_draw(streams_of[9], (KW, 2 * NS), 0.5, 3.0, (), jnp.float32)
    state_offset = jnp.clip(jax.random.uniform(streams_of[10], (2 * NS,), jnp.float32, -0.5, 0.5), -0.5, 0.5)
    step_bias = jnp.clip(-4.0 + 3.0 * jax.random.uniform(streams_of[11], (HEADS,), jnp.float32) ** block_levels(streams_of[11], (HEADS,), ((0, 4),), -0.2, 0.2), -4.0, -1.0)
    decay_log = jnp.clip(-1.0 + 3.77 * jax.random.uniform(streams_of[12], (HEADS,), jnp.float32) ** block_levels(streams_of[12], (HEADS,), ((0, 4),), -0.2, 0.2), -1.0, 2.77)
    skip_weight = jnp.clip(jnp.exp(math.log(3.0) - 2.3025851 * jax.random.uniform(streams_of[13], (HEADS,), jnp.float32) ** block_levels(streams_of[13], (HEADS,), ((0, 4),), -0.2, 0.2)), 0.3, 3.0)
    out_gain = jnp.clip(1.0 + 0.18 * jax.random.normal(streams_of[14], (DI,), jnp.float32), 0.1, 1.9)
    out_weight = bell_draw(streams_of[15], (DI, D), DI ** -0.5, 0.15625, ((0, 4),))
    cotangent = bell_draw(streams_of[16], (SEQS, TOK_DEV, D), 1.0, 6.0, ((0, 8), (2, 4)))
    return {"hidden": hidden, "segments": segments, "norm_gain": norm_gain, "gate_weight": gate_weight, "inner_weight": inner_weight, "state_weight": state_weight, "step_weight": step_weight, "inner_taps": inner_taps, "inner_offset": inner_offset, "state_taps": state_taps, "state_offset": state_offset, "step_bias": step_bias, "decay_log": decay_log, "skip_weight": skip_weight, "out_gain": out_gain, "out_weight": out_weight, "cotangent": cotangent}


@jax.custom_vjp
def low(v):
    return lax.optimization_barrier(v.astype(jnp.bfloat16)).astype(jnp.float32)

@jax.custom_vjp
def low_back(v):
    return v

def low_keep(v):
    return (low(v), None)

def low_pass(kept, grad):
    return (grad,)

def back_keep(v):
    return (v, None)

def back_low(kept, grad):
    return (low(grad),)
low.defvjp(low_keep, low_pass)
low_back.defvjp(back_keep, back_low)
EPSILON = 1e-05
HIGHEST_PRECISION = lax.Precision.HIGHEST

def rms_normed(values, gain):
    factor = lax.rsqrt(lax.optimization_barrier(jnp.mean(values * values, axis=-1, keepdims=True)) + EPSILON)
    return values * factor * gain

def causal_conv(values, kernel, offset, segment):
    kernel_width = kernel.shape[0]
    row_count = values.shape[0]
    padded = jnp.pad(values, ((kernel_width - 1, 0), (0, 0)))
    padded_seg = jnp.pad(segment, (kernel_width - 1, 0), constant_values=-1)
    summed = jnp.zeros_like(values) + offset
    for tap_index in range(kernel_width):
        same_doc = (padded_seg[tap_index:tap_index + row_count] == segment).astype(values.dtype)
        summed = summed + kernel[tap_index] * padded[tap_index:tap_index + row_count] * same_doc[:, None]
    return summed

def advance(running, pieces):
    factor, incoming = pieces
    return (factor[:, None, None] * running + incoming, running)

def scan_states(carried, fresh_states):
    zero_state = jnp.zeros_like(fresh_states[0])
    _, entering = lax.scan(jax.checkpoint(advance), zero_state, (carried, fresh_states))
    return entering

def state_space(inner, write_keys, read_keys, step_size, log_decay, segment, skip_weight, block_len):
    token_count, head_count, head_width = inner.shape
    block_count = token_count // block_len
    inner_blocks = inner.reshape(block_count, block_len, head_count, head_width)
    write_blocks = write_keys.reshape(block_count, block_len, -1)
    read_blocks = read_keys.reshape(block_count, block_len, -1)
    step_blocks = step_size.reshape(block_count, block_len, head_count)
    cumulated = jnp.cumsum(log_decay.reshape(block_count, block_len, head_count), axis=1)
    seg_blocks = segment.reshape(block_count, block_len)
    positions = jnp.arange(block_len)
    causal = positions[:, None] >= positions[None, :]
    allowed = causal[None] & (seg_blocks[:, :, None] == seg_blocks[:, None, :])
    scores = jnp.einsum('ctn,csn->cts', read_blocks, write_blocks, precision=HIGHEST_PRECISION)
    spread = cumulated[:, :, None, :] - cumulated[:, None, :, :]
    weights = jnp.exp(jnp.where(allowed[..., None], spread, -1e+30)) * scores[..., None] * step_blocks[:, None, :, :]
    within = jnp.einsum('ctsh,cshp->cthp', weights, inner_blocks, precision=HIGHEST_PRECISION)
    last_seg = seg_blocks[:, -1]
    keep_last = (seg_blocks == last_seg[:, None]).astype(inner.dtype)
    toward = jnp.exp(cumulated[:, -1:, :] - cumulated) * step_blocks * keep_last[..., None]
    fresh_states = jnp.einsum('csh,csn,cshp->chpn', toward, write_blocks, inner_blocks, precision=HIGHEST_PRECISION)
    previous = jnp.concatenate([jnp.full((1,), -1, jnp.int32), last_seg[:-1].astype(jnp.int32)])
    carried = jnp.exp(cumulated[:, -1, :]) * (last_seg == previous).astype(inner.dtype)[:, None]
    entering = scan_states(carried, fresh_states)
    reach_back = jnp.exp(cumulated) * (seg_blocks == previous[:, None]).astype(inner.dtype)[..., None]
    across = jnp.einsum('ctn,chpn->cthp', read_blocks, entering, precision=HIGHEST_PRECISION) * reach_back[..., None]
    mixed = (within + across).reshape(token_count, head_count, head_width)
    return mixed + skip_weight[None, :, None] * inner

def block_forward(params, row_values, segment):
    norm_gain, gate_weight, inner_weight, state_weight, step_weight, inner_taps, inner_offset, state_taps, state_offset, step_bias, decay_log, skip_weight, out_gain, out_weight = params
    token_count = row_values.shape[0]
    normed = low(rms_normed(row_values, norm_gain))
    gate_pre = low_back(jnp.dot(normed, gate_weight, precision=HIGHEST_PRECISION))
    inner_pre = low_back(jnp.dot(normed, inner_weight, precision=HIGHEST_PRECISION))
    state_pre = low_back(jnp.dot(normed, state_weight, precision=HIGHEST_PRECISION))
    steps_raw = low_back(jnp.dot(normed, step_weight, precision=HIGHEST_PRECISION))
    active = low(jax.nn.silu(causal_conv(inner_pre, inner_taps, inner_offset, segment)))
    pairs = low(jax.nn.silu(causal_conv(state_pre, state_taps, state_offset, segment)))
    step_size = jax.nn.softplus(steps_raw + step_bias)
    log_decay = -step_size * jnp.exp(decay_log)
    head_count = step_size.shape[1]
    mixed = state_space(active.reshape(token_count, head_count, -1), pairs[:, :NS], pairs[:, NS:], step_size, log_decay, segment, skip_weight, BLOCK)
    gated = mixed.reshape(token_count, -1) * jax.nn.silu(gate_pre)
    row_scale = lax.rsqrt(lax.optimization_barrier(jnp.mean(gated * gated, axis=-1, keepdims=True)) + EPSILON)
    gated_normed = low(gated * row_scale * out_gain)
    return jnp.dot(gated_normed, out_weight, precision=HIGHEST_PRECISION)

def reference(hidden, segments, norm_gain, gate_weight, inner_weight, state_weight, step_weight, inner_taps, inner_offset, state_taps, state_offset, step_bias, decay_log, skip_weight, out_gain, out_weight, cotangent):
    params = tuple((value.astype(jnp.float32) for value in (norm_gain, gate_weight, inner_weight, state_weight, step_weight, inner_taps, inner_offset, state_taps, state_offset, step_bias, decay_log, skip_weight, out_gain, out_weight)))
    zeros = tuple((jnp.zeros_like(value) for value in params))

    def one_sequence(totals, pieces):
        row_values, segment, upstream = pieces
        rows_wide = row_values.astype(jnp.float32)
        upstream_wide = upstream.astype(jnp.float32)
        result, pullback = jax.vjp(partial(block_forward, segment=segment), params, rows_wide)
        param_grads, rows_grad = pullback(upstream_wide)
        output = (rows_wide + result).astype(jnp.bfloat16)
        input_grad = upstream_wide + rows_grad
        totals = tuple((total + extra for total, extra in zip(totals, param_grads)))
        return (totals, (output, input_grad))
    totals, (output, input_grad) = lax.scan(one_sequence, zeros, (hidden, segments, cotangent))
    return (output, input_grad, totals[0], totals[1], totals[2], totals[3], totals[4], totals[5], totals[6], totals[7], totals[8], totals[9], totals[10], totals[11], totals[12], totals[13])
```

```python
import functools

import jax
import jax.numpy as jnp
from jax import lax
from jax.experimental import pallas as pl
from jax.experimental.pallas import tpu as pltpu
from jax.sharding import PartitionSpec as P

BLOCK = 256
EPSILON = 1e-05
HEAD = 64
F32 = jnp.float32
LOW = jnp.bfloat16
EXACT = lax.Precision.HIGHEST
VMEM_BYTES = 48 * 1024 * 1024


def mm(left, right):
    return jnp.dot(left, right, preferred_element_type=F32)


def mm_nt(left, right):
    return lax.dot_general(left, right, (((1,), (1,)), ((), ())), preferred_element_type=F32)


def mm_tn(left, right):
    return lax.dot_general(left, right, (((0,), (0,)), ((), ())), preferred_element_type=F32)


def iota(shape, axis):
    return lax.broadcasted_iota(jnp.int32, shape, axis)


def sigmoid(values):
    return 1.0 / (1.0 + jnp.exp(-values))


def softplus(values):
    return jnp.maximum(values, 0.0) + jnp.log1p(jnp.exp(-jnp.abs(values)))


def expand(columns, width):
    first = iota((1, 2 * HEAD), 1) < HEAD
    parts = []
    for pair in range(width // (2 * HEAD)):
        left = columns[:, 2 * pair : 2 * pair + 1]
        right = columns[:, 2 * pair + 1 : 2 * pair + 2]
        parts.append(jnp.where(first, left, right))
    return jnp.concatenate(parts, axis=1)


def collapse(values, lanes):
    width = values.shape[1]
    pick = (iota((width, lanes), 0) // HEAD == iota((width, lanes), 1)).astype(LOW)
    high = values.astype(LOW)
    rest = (values - high.astype(F32)).astype(LOW)
    return mm(high, pick) + mm(rest, pick)


def to_row(column):
    return jnp.broadcast_to(column, (column.shape[0], 128)).T[0:1]


def to_column(row):
    return jnp.broadcast_to(row, (128, row.shape[1])).T[:, 0:1]


def join_pieces(me, pieces):
    one, two = (me & 1) == 1, (me & 2) == 2
    values = [piece[...].astype(F32) for piece in pieces]
    a, b, c, d = values
    a, b, c, d = (
        jnp.where(one, b, a),
        jnp.where(one, a, b),
        jnp.where(one, d, c),
        jnp.where(one, c, d),
    )
    a, b, c, d = (
        jnp.where(two, c, a),
        jnp.where(two, d, b),
        jnp.where(two, a, c),
        jnp.where(two, b, d),
    )
    return jnp.concatenate([a, b, c, d], axis=1)


def store_pieces(me, values, keep_ref, give_ref):
    half = values.shape[0] // 2
    width = values.shape[1] // 4
    for dest in range(4):
        piece = values[:, dest * width : (dest + 1) * width]
        packed = jnp.concatenate([piece[:half], piece[half:]], axis=1).astype(LOW)[None]
        relative = me ^ dest

        @pl.when((relative & 1) == 0)
        def _():
            keep_ref[pl.ds(relative >> 1, 1)] = packed

        @pl.when((relative & 1) == 1)
        def _():
            give_ref[pl.ds(relative >> 1, 1)] = packed


def unpack(packed):
    width = packed.shape[1] // 2
    return jnp.concatenate([packed[:, :width], packed[:, width:]], axis=0)


def block_conv(ext, values, taps, offset, aux):
    rows = values.shape[0]
    total = offset + taps[3:4] * values
    for back in range(1, 4):
        total = total + taps[3 - back : 4 - back] * (
            aux[:, back - 1 : back] * ext[8 - back : 8 - back + rows]
        )
    return total


def conv_back(dpre, carry_ref, taps, values, aux):
    rows = dpre.shape[0]
    grad = taps[3:4] * dpre
    taps_grads = [jnp.sum(values * dpre, axis=0, keepdims=True)]
    for back in range(1, 4):
        masked = dpre * aux[:, back - 1 : back]
        ext = jnp.concatenate([masked, carry_ref[back - 1]], axis=0)
        carry_ref[back - 1] = masked[0:8]
        shifted = ext[back : back + rows]
        grad = grad + taps[3 - back : 4 - back] * shifted
        taps_grads.insert(0, jnp.sum(values * shifted, axis=0, keepdims=True))
    return grad, taps_grads


def scan_parts(raw, step_bias, rate, aux, seg_row):
    length, lanes = raw.shape
    shifted = raw + step_bias
    step = softplus(shifted)
    log_decay = -step * rate
    lower = (iota((length, length), 0) >= iota((length, length), 1)).astype(F32)
    cum = jnp.dot(lower, log_decay, precision=EXACT, preferred_element_type=F32)
    allowed = (iota((length, length), 0) >= iota((length, length), 1)) & (aux[:, 5:6] == seg_row)
    last = cum[length - 1 : length]
    reach = jnp.exp(cum) * aux[:, 4:5]
    fade = jnp.exp(last - cum) * aux[:, 3:4]
    return shifted, step, log_decay, cum, allowed, last, reach, fade


def forward_kernel(
    me_ref, x0, x1, x2, x3, gain, gate_w, inner_w, state_w, step_w, taps_i, off_i, taps_s, off_s,
    step_bias, rate, skip, aux_ref, seg_row, carry_mask, run_in, ci_in, cs_in,
    normed_out, gate_out, inner_v, inner_c, state_v, state_c, pairs_out, raw_out, y_out, enter_out,
    scale_out, run_out, ci_out, cs_out,
    run, carry_i, carry_s,
):
    at = pl.program_id(0)

    @pl.when(at == 0)
    def _():
        run[...] = run_in[...]
        carry_i[...] = ci_in[...]
        carry_s[...] = cs_in[...]

    aux = aux_ref[...]
    rows = join_pieces(me_ref[0], (x0, x1, x2, x3))
    factor = lax.rsqrt(jnp.mean(rows * rows, axis=1, keepdims=True) + EPSILON)
    normed = (rows * factor * gain[...]).astype(LOW)
    normed_out[...] = normed
    scale_out[0] = to_row(factor)
    gate_out[...] = mm(normed, gate_w[...])
    inner = mm(normed, inner_w[...])
    state = mm(normed, state_w[...])
    raw = mm(normed, step_w[...])
    raw_out[...] = raw
    inner_v[...] = inner.astype(LOW)
    state_v[...] = state.astype(LOW)
    inner_pre = block_conv(
        jnp.concatenate([carry_i[...], inner], axis=0), inner, taps_i[...], off_i[...], aux
    )
    state_pre = block_conv(
        jnp.concatenate([carry_s[...], state], axis=0), state, taps_s[...], off_s[...], aux
    )
    carry_i[...] = inner[-8:]
    carry_s[...] = state[-8:]
    inner_c[...] = inner_pre
    state_c[...] = state_pre
    active = (inner_pre * sigmoid(inner_pre)).astype(LOW)
    pairs = (state_pre * sigmoid(state_pre)).astype(LOW)
    pairs_out[...] = pairs
    half = pairs.shape[1] // 2
    write, read = pairs[:, :half], pairs[:, half:]
    shifted, step, log_decay, cum, allowed, last, reach, fade = scan_parts(
        raw, step_bias[...], rate[...], aux, seg_row[0]
    )
    cum_t, step_t = cum.T, step.T
    scores = mm_nt(read, write)
    width = active.shape[1]
    first = iota((1, 2 * HEAD), 1) < HEAD
    parts = []
    for pair in range(width // (2 * HEAD)):
        values = active[:, pair * 2 * HEAD : (pair + 1) * 2 * HEAD]
        got = []
        for head in (2 * pair, 2 * pair + 1):
            spread = cum[:, head : head + 1] - cum_t[head : head + 1]
            weights = jnp.exp(jnp.where(allowed, spread, -1e30)) * scores * step_t[head : head + 1]
            got.append(mm(weights.astype(LOW), values))
        parts.append(jnp.where(first, got[0], got[1]))
    within = jnp.concatenate(parts, axis=1)
    entering = run[...]
    entering_low = entering.astype(LOW)
    enter_out[0] = entering_low
    active_wide = active.astype(F32)
    across = mm(read, entering_low) * expand(reach, width)
    y_out[...] = within + across + skip[...] * active_wide
    fresh = mm_tn(write, (expand(fade * step, width) * active_wide).astype(LOW))
    run[...] = expand(jnp.exp(last) * carry_mask[0], width) * entering + fresh

    @pl.when(at == pl.num_programs(0) - 1)
    def _():
        run_out[...] = run[...]
        ci_out[...] = carry_i[...]
        cs_out[...] = carry_s[...]


def sums_kernel(me_ref, u0, u1, u2, u3, gate, y, out_w, out_gain, up_out, sums_out):
    upstream = join_pieces(me_ref[0], (u0, u1, u2, u3)).astype(LOW)
    up_out[...] = upstream
    z = gate[...]
    gated = y[...] * (z * sigmoid(z))
    weighted = mm_nt(upstream, out_w[...]) * out_gain[...]
    square = jnp.sum(gated * gated, axis=1, keepdims=True)
    cross = jnp.sum(weighted * gated, axis=1, keepdims=True)
    lane = iota((gated.shape[0], 128), 1)
    sums_out[0] = jnp.where(lane == 0, square, cross).T[0:2]


def output_kernel(
    full_width, me_ref, sums, upstream_ref, gate, y_ref, normed, out_w, out_gain,
    keep, give, out_w_grad, out_gain_grad, gate_low, dy_out, gate_w_grad, total_o, total_g,
):
    at = pl.program_id(0)

    @pl.when(at == 0)
    def _():
        total_o[...] = jnp.zeros_like(total_o)
        total_g[...] = jnp.zeros_like(total_g)
        out_gain_grad[...] = jnp.zeros_like(out_gain_grad)

    upstream = upstream_ref[...]
    pair = jnp.concatenate([sums[0], jnp.zeros((126, sums.shape[2]), F32)], axis=0).T
    square, cross = pair[:, 0:1], pair[:, 1:2]
    z, y = gate[...], y_ref[...]
    sig = sigmoid(z)
    swish = z * sig
    gated = y * swish
    scale = lax.rsqrt(square / full_width + EPSILON)
    gated_normed = (gated * scale * out_gain[...]).astype(LOW)
    store_pieces(me_ref[0], mm(gated_normed, out_w[...]), keep, give)
    total_o[...] += mm_tn(gated_normed, upstream)
    normal_grad = mm_nt(upstream, out_w[...])
    out_gain_grad[...] += jnp.sum(normal_grad * gated * scale, axis=0, keepdims=True)
    weighted = normal_grad * out_gain[...]
    gated_grad = scale * weighted - gated * (scale * scale * scale * (cross / full_width))
    dy_out[...] = gated_grad * swish
    low = (gated_grad * y * (sig * (1.0 + z * (1.0 - sig)))).astype(LOW)
    gate_low[...] = low
    total_g[...] += mm_tn(normed[...], low)

    @pl.when(at == pl.num_programs(0) - 1)
    def _():
        out_w_grad[...] = total_o[...].astype(LOW)
        gate_w_grad[...] = total_g[...].astype(LOW)


def backward_kernel(
    me_ref, pairs_ref, inner_c, inner_v, raw_ref, dy_ref, enter_ref, aux_ref, seg_row, carry_mask,
    taps_i, step_bias, rate, skip, state_in, carry_in,
    inner_low, keep, give, steps_low, rows_out, heads_out, state_out, carry_out,
    back, carry_z,
):
    at = pl.program_id(0)

    @pl.when(at == 0)
    def _():
        back[...] = state_in[...]
        carry_z[...] = carry_in[...]
        rows_out[...] = jnp.zeros_like(rows_out)
        heads_out[...] = jnp.zeros_like(heads_out)

    aux = aux_ref[...]
    pre = inner_c[...]
    sig = sigmoid(pre)
    active = (pre * sig).astype(LOW)
    active_wide = active.astype(F32)
    width = active.shape[1]
    pairs = pairs_ref[...]
    half = pairs.shape[1] // 2
    write, read = pairs[:, :half], pairs[:, half:]
    shifted, step, log_decay, cum, allowed, last, reach, fade = scan_parts(
        raw_ref[...], step_bias[...], rate[...], aux, seg_row[0]
    )
    length, lanes = cum.shape
    cum_t, step_t = cum.T, step.T
    scores = mm_nt(read, write)
    dy = dy_ref[...]
    dy_low = dy.astype(LOW)
    entering_low = enter_ref[0]
    reach_wide = expand(reach, width)
    toward_wide = expand(fade * step, width)
    dy_reach = dy * reach_wide
    dy_reach_low = dy_reach.astype(LOW)
    from_state = mm(read, entering_low)
    dcum = collapse(dy_reach * from_state, lanes)
    dread = mm_nt(dy_reach_low, entering_low)
    dentering = mm_tn(read, dy_reach_low)
    grad_state = back[...]
    grad_low = grad_state.astype(LOW)
    from_grad = mm(write, grad_low)
    dwrite = mm_nt((toward_wide * active_wide).astype(LOW), grad_low)
    dtoward = collapse(active_wide * from_grad, lanes)
    dfade = dtoward * (fade * step)
    dcum = dcum - dfade
    dstep = dtoward * fade
    keep_factor = jnp.exp(last) * carry_mask[0]
    kept = jnp.sum(grad_state * entering_low.astype(F32), axis=0, keepdims=True)
    kept = collapse(jnp.broadcast_to(kept, (8, width)), lanes)[0:1]
    dlast = jnp.sum(dfade, axis=0, keepdims=True) + keep_factor * kept
    back[...] = expand(keep_factor, width) * grad_state + dentering

    first = iota((1, 2 * HEAD), 1) < HEAD
    lane = iota((length, lanes), 1)
    dscores = jnp.zeros((length, length), F32)
    row_sums = jnp.zeros((length, lanes), F32)
    column_sums = []
    parts = []
    for pair in range(width // (2 * HEAD)):
        values = active[:, pair * 2 * HEAD : (pair + 1) * 2 * HEAD]
        grads = dy_low[:, pair * 2 * HEAD : (pair + 1) * 2 * HEAD]
        got = []
        for head in (2 * pair, 2 * pair + 1):
            own = jnp.where(first == (head % 2 == 0), grads, jnp.zeros_like(grads))
            steps_row = step_t[head : head + 1]
            spread = cum[:, head : head + 1] - cum_t[head : head + 1]
            decays = jnp.exp(jnp.where(allowed, spread, -1e30))
            dweights = mm_nt(own, values) * decays
            with_scores = dweights * scores
            dscores = dscores + dweights * steps_row
            column_sums.append(jnp.sum(with_scores, axis=0, keepdims=True))
            total = jnp.sum(with_scores * steps_row, axis=1, keepdims=True)
            row_sums = jnp.where(lane == head, total, row_sums)
            weights = (decays * scores * steps_row).astype(LOW)
            got.append(mm_tn(weights, grads))
        parts.append(jnp.where(first, got[0], got[1]))
    column_sums.append(jnp.zeros((lanes - len(column_sums), length), F32))
    columns = jnp.concatenate(column_sums, axis=0).T
    dscores_low = dscores.astype(LOW)
    dread = dread + mm(dscores_low, write)
    dwrite = dwrite + mm_tn(dscores_low, read)
    dstep = dstep + columns
    dcum = dcum + row_sums - step * columns
    dcum = dcum + jnp.where(iota((length, 1), 0) == length - 1, dlast, 0.0)
    upper = (iota((length, length), 0) <= iota((length, length), 1)).astype(F32)
    dlog = jnp.dot(upper, dcum, precision=EXACT, preferred_element_type=F32)
    dstep = dstep - dlog * rate[...]
    draw = dstep * sigmoid(shifted)
    steps_low[...] = draw.astype(LOW)
    heads_out[0:1] += jnp.sum(draw, axis=0, keepdims=True)
    heads_out[1:2] += jnp.sum(dlog * log_decay, axis=0, keepdims=True)

    dactive = jnp.concatenate(parts, axis=1) + skip[...] * dy + toward_wide * from_grad
    dpre = dactive * (sig * (1.0 + pre * (1.0 - sig)))
    grad, taps_grads = conv_back(dpre, carry_z, taps_i[...], inner_v[...].astype(F32), aux)
    inner_low[...] = grad.astype(LOW)
    for tap in range(4):
        rows_out[tap : tap + 1] += taps_grads[tap]
    rows_out[4:5] += jnp.sum(dpre, axis=0, keepdims=True)
    rows_out[5:6] += jnp.sum(dy * active_wide, axis=0, keepdims=True)
    store_pieces(me_ref[0], jnp.concatenate([dwrite, dread], axis=1), keep, give)

    @pl.when(at == pl.num_programs(0) - 1)
    def _():
        state_out[...] = back[...]
        carry_out[...] = carry_z[...]


def return_kernel(
    gate_low, inner_low, steps_low, normed, gate_w, inner_w, step_w,
    local, inner_w_grad, step_w_grad, total_i, total_s,
):
    at = pl.program_id(0)

    @pl.when(at == 0)
    def _():
        total_i[...] = jnp.zeros_like(total_i)
        total_s[...] = jnp.zeros_like(total_s)

    total_i[...] += mm_tn(normed[...], inner_low[...])
    total_s[...] += mm_tn(normed[...], steps_low[...])
    local[...] = (
        mm_nt(gate_low[...], gate_w[...])
        + mm_nt(inner_low[...], inner_w[...])
        + mm_nt(steps_low[...], step_w[...])
    )

    @pl.when(at == pl.num_programs(0) - 1)
    def _():
        inner_w_grad[...] = total_i[...].astype(LOW)
        step_w_grad[...] = total_s[...].astype(LOW)


def state_kernel(
    me_ref, part_a, part_b, part_c, state_c, state_v, normed_ref, local_ref, aux_ref, taps, state_w,
    keep, give, row_dot, state_w_grad, rows_out, gain_out, carry_z, total,
):
    at = pl.program_id(0)
    me = me_ref[0]

    @pl.when(at == 0)
    def _():
        carry_z[...] = jnp.zeros_like(carry_z)
        total[...] = jnp.zeros_like(total)
        rows_out[...] = jnp.zeros_like(rows_out)
        gain_out[...] = jnp.zeros_like(gain_out)

    def own(values):
        values = values.astype(F32)
        width = values.shape[1] // 4
        picked = jnp.where((me & 2) == 2, values[:, 2 * width :], values[:, : 2 * width])
        return jnp.where((me & 1) == 1, picked[:, width:], picked[:, :width])

    dpairs = unpack(
        part_a[0].astype(F32) + part_b[0].astype(F32) + part_c[...].astype(F32)
    )
    pre = own(state_c[...])
    sig = sigmoid(pre)
    dpre = dpairs * (sig * (1.0 + pre * (1.0 - sig)))
    grad, taps_grads = conv_back(dpre, carry_z, taps[...], own(state_v[...]), aux_ref[...])
    low = grad.astype(LOW)
    for tap in range(4):
        rows_out[tap : tap + 1] += taps_grads[tap]
    rows_out[4:5] += jnp.sum(dpre, axis=0, keepdims=True)
    normed = normed_ref[...]
    total[...] += mm_tn(normed, low)
    values = local_ref[...] + mm_nt(low, state_w[...])
    store_pieces(me, values, keep, give)
    product = values * normed.astype(F32)
    row_dot[0] = to_row(jnp.sum(product, axis=1, keepdims=True))
    gain_out[0:1] += jnp.sum(product, axis=0, keepdims=True)

    @pl.when(at == pl.num_programs(0) - 1)
    def _():
        state_w_grad[...] = total[...].astype(LOW)


def output_sum_kernel(part_a, part_b, part_c, hidden, out):
    branch = unpack(part_a[0].astype(F32) + part_b[0].astype(F32) + part_c[...].astype(F32))
    out[...] = (hidden[...].astype(F32) + branch).astype(LOW)


def input_grad_kernel(features, part_a, part_b, part_c, hidden, upstream, scale, row_dot, gain, out):
    grad = unpack(part_a[0].astype(F32) + part_b[0].astype(F32) + part_c[...].astype(F32))
    factor, dot = to_column(scale[0]), to_column(row_dot[0])
    out[...] = upstream[...].astype(F32) + (
        factor * (grad * gain[...]) - hidden[...].astype(F32) * (factor * factor * dot / features)
    )


def rows(columns, index):
    return pl.BlockSpec((BLOCK, columns), lambda i: (index(i), 0))


def slab(shape, index):
    return pl.BlockSpec((1, *shape), lambda i: (index(i),) + (0,) * len(shape))


def whole(shape):
    return pl.BlockSpec(shape, lambda i: (0,) * len(shape))


def packed(count, columns, index):
    return pl.BlockSpec((count, BLOCK // 2, columns), lambda i: (0, index(i), 0))


def half_rows(columns, index):
    return pl.BlockSpec((BLOCK // 2, columns), lambda i: (index(i), 0))


SCALAR = pl.BlockSpec(memory_space=pltpu.SMEM)


def call(kernel, blocks, ins, outs, scratch, flops):
    arrays = [array for array, _ in ins]
    shapes = [jax.ShapeDtypeStruct(shape, dtype) for shape, dtype, _ in outs]
    moved = sum(a.size * a.dtype.itemsize for a in [*arrays, *shapes])
    return pl.pallas_call(
        kernel,
        grid=(blocks,),
        in_specs=[spec for _, spec in ins],
        out_specs=[spec for _, _, spec in outs],
        out_shape=shapes,
        scratch_shapes=scratch,
        compiler_params=pltpu.CompilerParams(
            dimension_semantics=("arbitrary",), vmem_limit_bytes=VMEM_BYTES
        ),
        cost_estimate=pl.CostEstimate(flops=flops, bytes_accessed=moved, transcendentals=0),
    )(*arrays)


def swap(values, axis, bit):
    size = lax.axis_size(axis)
    return lax.ppermute(values, axis, [(i, i ^ bit) for i in range(size)])


def small_sum(values, axis):
    size = lax.axis_size(axis)
    if size & (size - 1):
        return lax.psum(values, axis)
    bit = 1
    while bit < size:
        values = values + swap(values, axis, bit)
        bit *= 2
    return values


def gather_pieces(values):
    across = swap(values, "tensor", 2)
    return values, swap(values, "tensor", 1), across, swap(across, "tensor", 1)


def scatter_sum(keep, give):
    got = swap(give, "tensor", 1)
    middle = (keep[1].astype(F32) + got[1].astype(F32)).astype(LOW)
    return keep, got, swap(middle, "tensor", 2)


def body(
    hidden, segments, norm_gain, gate_weight, inner_weight, state_weight, step_weight, inner_taps,
    inner_offset, state_taps, state_offset, step_bias, decay_log, skip_weight, out_gain, out_weight,
    cotangent,
):
    tensor_index = lax.axis_index("tensor")
    me = tensor_index.astype(jnp.int32)[None]
    own_hidden, own_upstream, segment = hidden[0], cotangent[0], segments[0]
    tokens, part = own_hidden.shape
    features, channels = gate_weight.shape
    heads = step_weight.shape[1]
    states = state_weight.shape[1]
    half = states // 2
    own_states = states // 4
    blocks = tokens // BLOCK
    lanes = 128
    full_width = channels * lax.axis_size("tensor")
    ahead = lambda i: i
    behind = lambda i: blocks - 1 - i
    zero = lambda i: 0

    hidden_pieces = gather_pieces(own_hidden)
    upstream_pieces = gather_pieces(own_upstream)

    seg_blocks = segment.reshape(blocks, BLOCK)
    last_seg = seg_blocks[:, -1]
    previous = jnp.concatenate([jnp.full((1,), -1, jnp.int32), last_seg[:-1]])
    columns = []
    for back in range(1, 4):
        padded = jnp.pad(segment, (back, 0), constant_values=-1)[:tokens]
        columns.append(padded == segment)
    columns.append((seg_blocks == last_seg[:, None]).reshape(tokens))
    columns.append((seg_blocks == previous[:, None]).reshape(tokens))
    columns.append(segment)
    aux = jnp.stack([c.astype(F32) for c in columns] + [jnp.zeros((tokens,), F32)] * 2, axis=1)
    seg_rows = seg_blocks.astype(F32)[:, None, :]
    carry_mask = jnp.broadcast_to(
        (last_seg == previous).astype(F32)[:, None, None], (blocks, 1, lanes)
    )
    pad_heads = lambda v: jnp.pad(v, (0, lanes - heads))[None]
    step_w = jnp.pad(step_weight, ((0, 0), (0, lanes - heads)))
    bias_row = pad_heads(step_bias)
    rate_row = pad_heads(jnp.exp(decay_log))
    skip_row = jnp.repeat(skip_weight, HEAD)[None]
    gain_row = norm_gain[None]
    out_gain_row = out_gain[None]

    weight_spec = whole((features, channels))
    (
        normed, gate, inner_v, inner_c, state_v, state_c, pairs, raw, y, entering, scale, _, _, _,
    ) = call(
        forward_kernel,
        blocks,
        [
            (me, SCALAR),
            *[(piece, rows(part, ahead)) for piece in hidden_pieces],
            (gain_row, whole((1, features))),
            (gate_weight, weight_spec),
            (inner_weight, weight_spec),
            (state_weight, whole((features, states))),
            (step_w, whole((features, lanes))),
            (inner_taps, whole((4, channels))),
            (inner_offset[None], whole((1, channels))),
            (state_taps, whole((4, states))),
            (state_offset[None], whole((1, states))),
            (bias_row, whole((1, lanes))),
            (rate_row, whole((1, lanes))),
            (skip_row, whole((1, channels))),
            (aux, rows(8, ahead)),
            (seg_rows, slab((1, BLOCK), ahead)),
            (carry_mask, slab((1, lanes), ahead)),
            (jnp.zeros((half, channels), F32), whole((half, channels))),
            (jnp.zeros((8, channels), F32), whole((8, channels))),
            (jnp.zeros((8, states), F32), whole((8, states))),
        ],
        [
            ((tokens, features), LOW, rows(features, ahead)),
            ((tokens, channels), F32, rows(channels, ahead)),
            ((tokens, channels), LOW, rows(channels, ahead)),
            ((tokens, channels), F32, rows(channels, ahead)),
            ((tokens, states), LOW, rows(states, ahead)),
            ((tokens, states), F32, rows(states, ahead)),
            ((tokens, states), LOW, rows(states, ahead)),
            ((tokens, lanes), F32, rows(lanes, ahead)),
            ((tokens, channels), F32, rows(channels, ahead)),
            ((blocks, half, channels), LOW, slab((half, channels), ahead)),
            ((blocks, 1, BLOCK), F32, slab((1, BLOCK), ahead)),
            ((half, channels), F32, whole((half, channels))),
            ((8, channels), F32, whole((8, channels))),
            ((8, states), F32, whole((8, states))),
        ],
        [
            pltpu.VMEM((half, channels), F32),
            pltpu.VMEM((8, channels), F32),
            pltpu.VMEM((8, states), F32),
        ],
        40_000_000_000,
    )

    upstream, sums = call(
        sums_kernel,
        blocks,
        [
            (me, SCALAR),
            *[(piece, rows(part, ahead)) for piece in upstream_pieces],
            (gate, rows(channels, ahead)),
            (y, rows(channels, ahead)),
            (out_weight, whole((channels, features))),
            (out_gain_row, whole((1, channels))),
        ],
        [
            ((tokens, features), LOW, rows(features, ahead)),
            ((blocks, 2, BLOCK), F32, slab((2, BLOCK), ahead)),
        ],
        [],
        4_000_000_000,
    )
    sums = small_sum(sums, "tensor")

    piece_shape = (2, tokens // 2, 2 * part)
    keep_o, give_o, out_w_grad, out_gain_grad, gate_low, dy, gate_w_grad = call(
        functools.partial(output_kernel, full_width),
        blocks,
        [
            (me, SCALAR),
            (sums, slab((2, BLOCK), ahead)),
            (upstream, rows(features, ahead)),
            (gate, rows(channels, ahead)),
            (y, rows(channels, ahead)),
            (normed, rows(features, ahead)),
            (out_weight, whole((channels, features))),
            (out_gain_row, whole((1, channels))),
        ],
        [
            (piece_shape, LOW, packed(2, 2 * part, ahead)),
            (piece_shape, LOW, packed(2, 2 * part, ahead)),
            ((channels, features), LOW, whole((channels, features))),
            ((1, channels), F32, whole((1, channels))),
            ((tokens, channels), LOW, rows(channels, ahead)),
            ((tokens, channels), F32, rows(channels, ahead)),
            ((features, channels), LOW, weight_spec),
        ],
        [pltpu.VMEM((channels, features), F32), pltpu.VMEM((features, channels), F32)],
        16_000_000_000,
    )
    branch_parts = scatter_sum(keep_o, give_o)
    out_w_grad, gate_w_grad = lax.psum((out_w_grad, gate_w_grad), "dp")

    pair_shape = (2, tokens // 2, 2 * own_states)
    inner_low, keep_p, give_p, steps_low, row_grads, head_grads, _, _ = call(
        backward_kernel,
        blocks,
        [
            (me, SCALAR),
            (pairs, rows(states, behind)),
            (inner_c, rows(channels, behind)),
            (inner_v, rows(channels, behind)),
            (raw, rows(lanes, behind)),
            (dy, rows(channels, behind)),
            (entering, slab((half, channels), behind)),
            (aux, rows(8, behind)),
            (seg_rows, slab((1, BLOCK), behind)),
            (carry_mask, slab((1, lanes), behind)),
            (inner_taps, whole((4, channels))),
            (bias_row, whole((1, lanes))),
            (rate_row, whole((1, lanes))),
            (skip_row, whole((1, channels))),
            (jnp.zeros((half, channels), F32), whole((half, channels))),
            (jnp.zeros((3, 8, channels), F32), whole((3, 8, channels))),
        ],
        [
            ((tokens, channels), LOW, rows(channels, behind)),
            (pair_shape, LOW, packed(2, 2 * own_states, behind)),
            (pair_shape, LOW, packed(2, 2 * own_states, behind)),
            ((tokens, lanes), LOW, rows(lanes, behind)),
            ((8, channels), F32, whole((8, channels))),
            ((8, lanes), F32, whole((8, lanes))),
            ((half, channels), F32, whole((half, channels))),
            ((3, 8, channels), F32, whole((3, 8, channels))),
        ],
        [pltpu.VMEM((half, channels), F32), pltpu.VMEM((3, 8, channels), F32)],
        60_000_000_000,
    )
    pair_parts = scatter_sum(keep_p, give_p)

    local, inner_w_grad, step_w_grad = call(
        return_kernel,
        blocks,
        [
            (gate_low, rows(channels, ahead)),
            (inner_low, rows(channels, ahead)),
            (steps_low, rows(lanes, ahead)),
            (normed, rows(features, ahead)),
            (gate_weight, weight_spec),
            (inner_weight, weight_spec),
            (step_w, whole((features, lanes))),
        ],
        [
            ((tokens, features), F32, rows(features, ahead)),
            ((features, channels), LOW, weight_spec),
            ((features, lanes), LOW, whole((features, lanes))),
        ],
        [pltpu.VMEM((features, channels), F32), pltpu.VMEM((features, lanes), F32)],
        10_000_000_000,
    )
    inner_w_grad, step_w_grad, gate_w_grad = lax.optimization_barrier(
        (inner_w_grad, step_w_grad[:, :heads], gate_w_grad)
    )
    inner_w_grad, step_w_grad = lax.psum((inner_w_grad, step_w_grad), "dp")

    own_start = tensor_index * own_states
    own_taps = lax.dynamic_slice_in_dim(state_taps, own_start, own_states, 1)
    own_state_w = lax.dynamic_slice_in_dim(state_weight, own_start, own_states, 1)
    keep_n, give_n, row_dot, state_w_grad, state_rows, gain_sum = call(
        state_kernel,
        blocks,
        [
            (me, SCALAR),
            (pair_parts[0], packed(1, 2 * own_states, behind)),
            (pair_parts[1], packed(1, 2 * own_states, behind)),
            (pair_parts[2], half_rows(2 * own_states, behind)),
            (state_c, rows(states, behind)),
            (state_v, rows(states, behind)),
            (normed, rows(features, behind)),
            (local, rows(features, behind)),
            (aux, rows(8, behind)),
            (own_taps, whole((4, own_states))),
            (own_state_w, whole((features, own_states))),
        ],
        [
            (piece_shape, LOW, packed(2, 2 * part, behind)),
            (piece_shape, LOW, packed(2, 2 * part, behind)),
            ((blocks, 1, BLOCK), F32, slab((1, BLOCK), behind)),
            ((features, own_states), LOW, whole((features, own_states))),
            ((8, own_states), F32, whole((8, own_states))),
            ((8, features), F32, whole((8, features))),
        ],
        [pltpu.VMEM((3, 8, own_states), F32), pltpu.VMEM((features, own_states), F32)],
        4_000_000_000,
    )
    grad_parts = scatter_sum(keep_n, give_n)
    row_dot = small_sum(row_dot, "tensor")

    output = call(
        output_sum_kernel,
        blocks,
        [
            (branch_parts[0], packed(1, 2 * part, ahead)),
            (branch_parts[1], packed(1, 2 * part, ahead)),
            (branch_parts[2], half_rows(2 * part, ahead)),
            (own_hidden, rows(part, ahead)),
        ],
        [((tokens, part), LOW, rows(part, ahead))],
        [],
        1_000_000,
    )[0]
    own_gain = lax.dynamic_slice_in_dim(norm_gain, tensor_index * part, part, 0)
    input_grad = call(
        functools.partial(input_grad_kernel, features),
        blocks,
        [
            (grad_parts[0], packed(1, 2 * part, ahead)),
            (grad_parts[1], packed(1, 2 * part, ahead)),
            (grad_parts[2], half_rows(2 * part, ahead)),
            (own_hidden, rows(part, ahead)),
            (own_upstream, rows(part, ahead)),
            (scale, slab((1, BLOCK), ahead)),
            (row_dot, slab((1, BLOCK), ahead)),
            (own_gain[None], whole((1, part))),
        ],
        [((tokens, part), F32, rows(part, ahead))],
        [],
        1_000_000,
    )[0]

    state_w_grad, inner_w_grad = lax.optimization_barrier((state_w_grad, inner_w_grad))
    state_w_grad = lax.psum(state_w_grad, "dp")
    state_w_grad = lax.all_gather(state_w_grad, "tensor", axis=1, tiled=True)

    early = jnp.concatenate(
        [row_grads[:6].reshape(-1), out_gain_grad.reshape(-1), head_grads[:2].reshape(-1)]
    ).reshape(-1, lanes)
    early = small_sum(early, "dp").reshape(-1)
    cut = 6 * channels
    row_grads = early[:cut].reshape(6, channels)
    out_gain_grad = early[cut : cut + channels]
    head_grads = early[cut + channels :].reshape(2, lanes)

    placed = lax.dynamic_update_slice_in_dim(
        jnp.zeros((5, states), F32), state_rows[:5], own_start, 1
    )
    late = jnp.concatenate([placed.reshape(-1), gain_sum[0]]).reshape(-1, lanes)
    late = small_sum(small_sum(late, "tensor"), "dp").reshape(-1)
    state_rows = late[: 5 * states].reshape(5, states)
    norm_gain_grad = late[5 * states :] / norm_gain

    return (
        output[None],
        input_grad[None],
        norm_gain_grad,
        gate_w_grad.astype(F32),
        inner_w_grad.astype(F32),
        state_w_grad.astype(F32),
        step_w_grad.astype(F32),
        row_grads[:4],
        row_grads[4],
        state_rows[:4],
        state_rows[4],
        head_grads[0, :heads],
        head_grads[1, :heads],
        jnp.sum(row_grads[5].reshape(heads, HEAD), axis=1),
        out_gain_grad,
        out_w_grad.astype(F32),
    )


def solution(mesh):
    rows_spec = P("dp", None, "tensor")
    columns_spec = P(None, "tensor")
    in_specs = (
        rows_spec, P("dp", None), P(), columns_spec, columns_spec, P(), columns_spec, columns_spec,
        P("tensor"), P(), P(), P("tensor"), P("tensor"), P("tensor"), P("tensor"),
        P("tensor", None), rows_spec,
    )
    out_specs = (
        rows_spec, rows_spec, P(), columns_spec, columns_spec, P(), columns_spec, columns_spec,
        P("tensor"), P(), P(), P("tensor"), P("tensor"), P("tensor"), P("tensor"),
        P("tensor", None),
    )
    return jax.shard_map(body, mesh=mesh, in_specs=in_specs, out_specs=out_specs, check_vma=False)
```

```python
import functools

import jax
import jax.numpy as jnp
from jax import lax
from jax.experimental import pallas as pl
from jax.experimental.pallas import tpu as pltpu
from jax.sharding import PartitionSpec as P

BLOCK = 256
EPSILON = 1e-05
HEAD = 64
F32 = jnp.float32
LOW = jnp.bfloat16
EXACT = lax.Precision.HIGHEST
VMEM_BYTES = 48 * 1024 * 1024


def mm(left, right):
    return jnp.dot(left, right, preferred_element_type=F32)


def mm_nt(left, right):
    return lax.dot_general(left, right, (((1,), (1,)), ((), ())), preferred_element_type=F32)


def mm_tn(left, right):
    return lax.dot_general(left, right, (((0,), (0,)), ((), ())), preferred_element_type=F32)


def iota(shape, axis):
    return lax.broadcasted_iota(jnp.int32, shape, axis)


def sigmoid(values):
    return 1.0 / (1.0 + jnp.exp(-values))


def softplus(values):
    return jnp.maximum(values, 0.0) + jnp.log1p(jnp.exp(-jnp.abs(values)))


def expand(columns, width):
    first = iota((1, 2 * HEAD), 1) < HEAD
    parts = []
    for pair in range(width // (2 * HEAD)):
        left = columns[:, 2 * pair : 2 * pair + 1]
        right = columns[:, 2 * pair + 1 : 2 * pair + 2]
        parts.append(jnp.where(first, left, right))
    return jnp.concatenate(parts, axis=1)


def collapse(values, lanes):
    width = values.shape[1]
    pick = (iota((width, lanes), 0) // HEAD == iota((width, lanes), 1)).astype(LOW)
    high = values.astype(LOW)
    rest = (values - high.astype(F32)).astype(LOW)
    return mm(high, pick) + mm(rest, pick)


def join_pieces(me, pieces, joined):
    for relative, piece in enumerate(pieces):
        joined[pl.ds(me ^ relative, 1)] = piece[...][None]
    return joined[...].reshape(joined.shape[0] * joined.shape[1], joined.shape[2])


def store_pieces(me, values, keep_ref, give_ref):
    width = values.shape[0] // 4
    for dest in range(4):
        piece = values[dest * width : (dest + 1) * width].astype(LOW)[None]
        relative = me ^ dest

        @pl.when((relative & 1) == 0)
        def _():
            keep_ref[pl.ds(relative >> 1, 1)] = piece

        @pl.when((relative & 1) == 1)
        def _():
            give_ref[pl.ds(relative >> 1, 1)] = piece


def block_conv(ext, values, taps, offset, aux):
    rows = values.shape[0]
    total = offset + taps[3:4] * values
    for back in range(1, 4):
        total = total + taps[3 - back : 4 - back] * (
            aux[:, back - 1 : back] * ext[8 - back : 8 - back + rows]
        )
    return total


def conv_back(dpre, carry_ref, taps, values, aux):
    rows = dpre.shape[0]
    grad = taps[3:4] * dpre
    taps_grads = [jnp.sum(values * dpre, axis=0, keepdims=True)]
    for back in range(1, 4):
        masked = dpre * aux[:, back - 1 : back]
        ext = jnp.concatenate([masked, carry_ref[back - 1]], axis=0)
        carry_ref[back - 1] = masked[0:8]
        shifted = ext[back : back + rows]
        grad = grad + taps[3 - back : 4 - back] * shifted
        taps_grads.insert(0, jnp.sum(values * shifted, axis=0, keepdims=True))
    return grad, taps_grads


def scan_parts(raw, step_bias, rate, aux, seg_row):
    length, lanes = raw.shape
    shifted = raw + step_bias
    step = softplus(shifted)
    log_decay = -step * rate
    lower = (iota((length, length), 0) >= iota((length, length), 1)).astype(F32)
    cum = jnp.dot(lower, log_decay, precision=EXACT, preferred_element_type=F32)
    allowed = (iota((length, length), 0) >= iota((length, length), 1)) & (aux[:, 5:6] == seg_row)
    last = cum[length - 1 : length]
    reach = jnp.exp(cum) * aux[:, 4:5]
    fade = jnp.exp(last - cum) * aux[:, 3:4]
    return shifted, step, log_decay, cum, allowed, last, reach, fade


def forward_kernel(
    me_ref, x0, x1, x2, x3, gain, gate_w, inner_w, state_w, step_w, taps_i, off_i, taps_s, off_s,
    step_bias, rate, skip, aux_ref, seg_row, carry_mask, run_in, ci_in, cs_in,
    normed_out, gate_out, inner_v, inner_c, state_v, state_c, pairs_out, raw_out, y_out, enter_out,
    scale_out, run_out, ci_out, cs_out,
    run, carry_i, carry_s, joined,
):
    at = pl.program_id(0)

    @pl.when(at == 0)
    def _():
        run[...] = run_in[...]
        carry_i[...] = ci_in[...]
        carry_s[...] = cs_in[...]

    aux = aux_ref[...]
    rows = join_pieces(me_ref[0], (x0, x1, x2, x3), joined).astype(F32)
    factor = lax.rsqrt(jnp.mean(rows * rows, axis=0, keepdims=True) + EPSILON)
    normed_t = (rows * factor * gain[...]).astype(LOW)
    normed_out[...] = normed_t
    scale_out[0] = factor
    normed = normed_t.T
    gate_out[...] = mm(normed, gate_w[...])
    inner = mm(normed, inner_w[...])
    state = mm(normed, state_w[...])
    raw = mm(normed, step_w[...])
    raw_out[...] = raw
    inner_v[...] = inner.astype(LOW)
    state_v[...] = state.astype(LOW)
    inner_pre = block_conv(
        jnp.concatenate([carry_i[...], inner], axis=0), inner, taps_i[...], off_i[...], aux
    )
    state_pre = block_conv(
        jnp.concatenate([carry_s[...], state], axis=0), state, taps_s[...], off_s[...], aux
    )
    carry_i[...] = inner[-8:]
    carry_s[...] = state[-8:]
    inner_c[...] = inner_pre
    state_c[...] = state_pre
    active = (inner_pre * sigmoid(inner_pre)).astype(LOW)
    pairs = (state_pre * sigmoid(state_pre)).astype(LOW)
    pairs_out[...] = pairs
    half = pairs.shape[1] // 2
    write, read = pairs[:, :half], pairs[:, half:]
    shifted, step, log_decay, cum, allowed, last, reach, fade = scan_parts(
        raw, step_bias[...], rate[...], aux, seg_row[0]
    )
    cum_t, step_t = cum.T, step.T
    scores = mm_nt(read, write)
    width = active.shape[1]
    first = iota((1, 2 * HEAD), 1) < HEAD
    parts = []
    for pair in range(width // (2 * HEAD)):
        values = active[:, pair * 2 * HEAD : (pair + 1) * 2 * HEAD]
        got = []
        for head in (2 * pair, 2 * pair + 1):
            spread = cum[:, head : head + 1] - cum_t[head : head + 1]
            weights = jnp.exp(jnp.where(allowed, spread, -1e30)) * scores * step_t[head : head + 1]
            got.append(mm(weights.astype(LOW), values))
        parts.append(jnp.where(first, got[0], got[1]))
    within = jnp.concatenate(parts, axis=1)
    entering = run[...]
    entering_low = entering.astype(LOW)
    enter_out[0] = entering_low
    active_wide = active.astype(F32)
    across = mm(read, entering_low) * expand(reach, width)
    y_out[...] = within + across + skip[...] * active_wide
    fresh = mm_tn(write, (expand(fade * step, width) * active_wide).astype(LOW))
    run[...] = expand(jnp.exp(last) * carry_mask[0], width) * entering + fresh

    @pl.when(at == pl.num_programs(0) - 1)
    def _():
        run_out[...] = run[...]
        ci_out[...] = carry_i[...]
        cs_out[...] = carry_s[...]


def sums_kernel(
    me_ref, u0, u1, u2, u3, gate, y, out_w_t, out_gain, up_out, grad_out, sums_out, joined
):
    upstream_t = join_pieces(me_ref[0], (u0, u1, u2, u3), joined)
    up_out[...] = upstream_t
    z = gate[...]
    gated = y[...] * (z * sigmoid(z))
    normal_grad = mm(upstream_t.T, out_w_t[...])
    grad_out[...] = normal_grad
    square = jnp.sum(gated * gated, axis=1, keepdims=True)
    cross = jnp.sum(normal_grad * out_gain[...] * gated, axis=1, keepdims=True)
    lane = iota((gated.shape[0], 128), 1)
    sums_out[0] = jnp.where(lane == 0, square, cross).T[0:2]


def output_kernel(
    full_width, me_ref, sums, upstream_t, gate, y_ref, grad_ref, normed_t, out_w_t, out_gain,
    keep, give, out_w_grad, out_gain_grad, gate_low, dy_out, gate_w_grad, total_o, total_g,
):
    at = pl.program_id(0)

    @pl.when(at == 0)
    def _():
        total_o[...] = jnp.zeros_like(total_o)
        total_g[...] = jnp.zeros_like(total_g)
        out_gain_grad[...] = jnp.zeros_like(out_gain_grad)

    pair = jnp.concatenate([sums[0], jnp.zeros((126, sums.shape[2]), F32)], axis=0).T
    square, cross = pair[:, 0:1], pair[:, 1:2]
    z, y = gate[...], y_ref[...]
    sig = sigmoid(z)
    swish = z * sig
    gated = y * swish
    scale = lax.rsqrt(square / full_width + EPSILON)
    gated_normed = (gated * scale * out_gain[...]).astype(LOW)
    store_pieces(me_ref[0], mm_nt(out_w_t[...], gated_normed), keep, give)
    total_o[...] += mm(upstream_t[...], gated_normed)
    normal_grad = grad_ref[...]
    out_gain_grad[...] += jnp.sum(normal_grad * gated * scale, axis=0, keepdims=True)
    weighted = normal_grad * out_gain[...]
    gated_grad = scale * weighted - gated * (scale * scale * scale * (cross / full_width))
    dy_out[...] = gated_grad * swish
    low = (gated_grad * y * (sig * (1.0 + z * (1.0 - sig)))).astype(LOW)
    gate_low[...] = low
    total_g[...] += mm(normed_t[...], low)

    @pl.when(at == pl.num_programs(0) - 1)
    def _():
        out_w_grad[...] = total_o[...].T.astype(LOW)
        gate_w_grad[...] = total_g[...].astype(LOW)


def backward_kernel(
    me_ref, pairs_ref, inner_c, inner_v, raw_ref, dy_ref, enter_ref, aux_ref, seg_row, carry_mask,
    taps_i, step_bias, rate, skip, state_in, carry_in,
    inner_low, keep, give, steps_low, rows_out, heads_out, state_out, carry_out,
    back, carry_z,
):
    at = pl.program_id(0)

    @pl.when(at == 0)
    def _():
        back[...] = state_in[...]
        carry_z[...] = carry_in[...]
        rows_out[...] = jnp.zeros_like(rows_out)
        heads_out[...] = jnp.zeros_like(heads_out)

    aux = aux_ref[...]
    pre = inner_c[...]
    sig = sigmoid(pre)
    active = (pre * sig).astype(LOW)
    active_wide = active.astype(F32)
    width = active.shape[1]
    pairs = pairs_ref[...]
    half = pairs.shape[1] // 2
    write, read = pairs[:, :half], pairs[:, half:]
    shifted, step, log_decay, cum, allowed, last, reach, fade = scan_parts(
        raw_ref[...], step_bias[...], rate[...], aux, seg_row[0]
    )
    length, lanes = cum.shape
    cum_t, step_t = cum.T, step.T
    scores = mm_nt(read, write)
    dy = dy_ref[...]
    dy_low = dy.astype(LOW)
    entering_low = enter_ref[0]
    reach_wide = expand(reach, width)
    toward_wide = expand(fade * step, width)
    dy_reach = dy * reach_wide
    dy_reach_low = dy_reach.astype(LOW)
    from_state = mm(read, entering_low)
    dcum = collapse(dy_reach * from_state, lanes)
    dread = mm_nt(dy_reach_low, entering_low)
    dentering = mm_tn(read, dy_reach_low)
    grad_state = back[...]
    grad_low = grad_state.astype(LOW)
    from_grad = mm(write, grad_low)
    dwrite = mm_nt((toward_wide * active_wide).astype(LOW), grad_low)
    dtoward = collapse(active_wide * from_grad, lanes)
    dfade = dtoward * (fade * step)
    dcum = dcum - dfade
    dstep = dtoward * fade
    keep_factor = jnp.exp(last) * carry_mask[0]
    kept = jnp.sum(grad_state * entering_low.astype(F32), axis=0, keepdims=True)
    kept = collapse(jnp.broadcast_to(kept, (8, width)), lanes)[0:1]
    dlast = jnp.sum(dfade, axis=0, keepdims=True) + keep_factor * kept
    back[...] = expand(keep_factor, width) * grad_state + dentering

    first = iota((1, 2 * HEAD), 1) < HEAD
    lane = iota((length, lanes), 1)
    dscores = jnp.zeros((length, length), F32)
    row_sums = jnp.zeros((length, lanes), F32)
    column_sums = []
    parts = []
    for pair in range(width // (2 * HEAD)):
        values = active[:, pair * 2 * HEAD : (pair + 1) * 2 * HEAD]
        grads = dy_low[:, pair * 2 * HEAD : (pair + 1) * 2 * HEAD]
        got = []
        for head in (2 * pair, 2 * pair + 1):
            own = jnp.where(first == (head % 2 == 0), grads, jnp.zeros_like(grads))
            steps_row = step_t[head : head + 1]
            spread = cum[:, head : head + 1] - cum_t[head : head + 1]
            decays = jnp.exp(jnp.where(allowed, spread, -1e30))
            dweights = mm_nt(own, values) * decays
            with_scores = dweights * scores
            dscores = dscores + dweights * steps_row
            column_sums.append(jnp.sum(with_scores, axis=0, keepdims=True))
            total = jnp.sum(with_scores * steps_row, axis=1, keepdims=True)
            row_sums = jnp.where(lane == head, total, row_sums)
            weights = (decays * scores * steps_row).astype(LOW)
            got.append(mm_tn(weights, grads))
        parts.append(jnp.where(first, got[0], got[1]))
    column_sums.append(jnp.zeros((lanes - len(column_sums), length), F32))
    columns = jnp.concatenate(column_sums, axis=0).T
    dscores_low = dscores.astype(LOW)
    dread = dread + mm(dscores_low, write)
    dwrite = dwrite + mm_tn(dscores_low, read)
    dstep = dstep + columns
    dcum = dcum + row_sums - step * columns
    dcum = dcum + jnp.where(iota((length, 1), 0) == length - 1, dlast, 0.0)
    upper = (iota((length, length), 0) <= iota((length, length), 1)).astype(F32)
    dlog = jnp.dot(upper, dcum, precision=EXACT, preferred_element_type=F32)
    dstep = dstep - dlog * rate[...]
    draw = dstep * sigmoid(shifted)
    steps_low[...] = draw.astype(LOW)
    heads_out[0:1] += jnp.sum(draw, axis=0, keepdims=True)
    heads_out[1:2] += jnp.sum(dlog * log_decay, axis=0, keepdims=True)

    dactive = jnp.concatenate(parts, axis=1) + skip[...] * dy + toward_wide * from_grad
    dpre = dactive * (sig * (1.0 + pre * (1.0 - sig)))
    grad, taps_grads = conv_back(dpre, carry_z, taps_i[...], inner_v[...].astype(F32), aux)
    inner_low[...] = grad.astype(LOW)
    for tap in range(4):
        rows_out[tap : tap + 1] += taps_grads[tap]
    rows_out[4:5] += jnp.sum(dpre, axis=0, keepdims=True)
    rows_out[5:6] += jnp.sum(dy * active_wide, axis=0, keepdims=True)
    store_pieces(me_ref[0], jnp.concatenate([dwrite, dread], axis=1).T, keep, give)

    @pl.when(at == pl.num_programs(0) - 1)
    def _():
        state_out[...] = back[...]
        carry_out[...] = carry_z[...]


def return_kernel(
    gate_low, inner_low, steps_low, normed_t, gate_w, inner_w, step_w,
    local, scan_w_grad, total_i, total_s,
):
    at = pl.program_id(0)

    @pl.when(at == 0)
    def _():
        total_i[...] = jnp.zeros_like(total_i)
        total_s[...] = jnp.zeros_like(total_s)

    total_i[...] += mm(normed_t[...], inner_low[...])
    total_s[...] += mm(normed_t[...], steps_low[...])
    local[...] = (
        mm_nt(gate_w[...], gate_low[...])
        + mm_nt(inner_w[...], inner_low[...])
        + mm_nt(step_w[...], steps_low[...])
    )

    @pl.when(at == pl.num_programs(0) - 1)
    def _():
        scan_w_grad[...] = jnp.concatenate([total_i[...], total_s[...]], axis=1).astype(LOW)


def state_kernel(
    me_ref, part_a, part_b, part_c, state_c, state_v, normed_ref, local_ref, aux_ref, taps, state_w,
    keep, give, row_dot, state_w_grad, rows_out, gain_out, carry_z, total, gain_total,
):
    at = pl.program_id(0)
    me = me_ref[0]

    @pl.when(at == 0)
    def _():
        carry_z[...] = jnp.zeros_like(carry_z)
        total[...] = jnp.zeros_like(total)
        rows_out[...] = jnp.zeros_like(rows_out)
        gain_total[...] = jnp.zeros_like(gain_total)

    def own(values):
        values = values.astype(F32)
        width = values.shape[1] // 4
        picked = jnp.where((me & 2) == 2, values[:, 2 * width :], values[:, : 2 * width])
        return jnp.where((me & 1) == 1, picked[:, width:], picked[:, :width])

    dpairs = (part_a[0].astype(F32) + part_b[0].astype(F32) + part_c[...].astype(F32)).T
    pre = own(state_c[...])
    sig = sigmoid(pre)
    dpre = dpairs * (sig * (1.0 + pre * (1.0 - sig)))
    grad, taps_grads = conv_back(dpre, carry_z, taps[...], own(state_v[...]), aux_ref[...])
    low = grad.astype(LOW)
    for tap in range(4):
        rows_out[tap : tap + 1] += taps_grads[tap]
    rows_out[4:5] += jnp.sum(dpre, axis=0, keepdims=True)
    normed_t = normed_ref[...]
    total[...] += mm(normed_t, low)
    values = local_ref[...] + mm_nt(state_w[...], low)
    store_pieces(me, values, keep, give)
    product = values * normed_t.astype(F32)
    row_dot[0] = jnp.sum(product, axis=0, keepdims=True)
    gain_total[...] += sum(
        product[:, at : at + 128] for at in range(0, product.shape[1], 128)
    )

    @pl.when(at == pl.num_programs(0) - 1)
    def _():
        state_w_grad[...] = total[...].T
        column = jnp.sum(gain_total[...], axis=1, keepdims=True)
        gain_out[...] = jnp.broadcast_to(column, gain_total.shape).T[0:8]


def rows(columns, index):
    return pl.BlockSpec((BLOCK, columns), lambda i: (index(i), 0))


def slab(shape, index):
    return pl.BlockSpec((1, *shape), lambda i: (index(i),) + (0,) * len(shape))


def whole(shape):
    return pl.BlockSpec(shape, lambda i: (0,) * len(shape))


def flat(features, index):
    return pl.BlockSpec((features, BLOCK), lambda i: (0, index(i)))


def packed(count, features, index):
    return pl.BlockSpec((count, features, BLOCK), lambda i: (0, 0, index(i)))


SCALAR = pl.BlockSpec(memory_space=pltpu.SMEM)


def call(kernel, blocks, ins, outs, scratch, flops):
    arrays = [array for array, _ in ins]
    shapes = [jax.ShapeDtypeStruct(shape, dtype) for shape, dtype, _ in outs]
    moved = sum(a.size * a.dtype.itemsize for a in [*arrays, *shapes])
    return pl.pallas_call(
        kernel,
        grid=(blocks,),
        in_specs=[spec for _, spec in ins],
        out_specs=[spec for _, _, spec in outs],
        out_shape=shapes,
        scratch_shapes=scratch,
        compiler_params=pltpu.CompilerParams(
            dimension_semantics=("arbitrary",), vmem_limit_bytes=VMEM_BYTES
        ),
        cost_estimate=pl.CostEstimate(flops=flops, bytes_accessed=moved, transcendentals=0),
    )(*arrays)


def swap(values, axis, bit):
    size = lax.axis_size(axis)
    return lax.ppermute(values, axis, [(i, i ^ bit) for i in range(size)])


def small_sum(values, axis):
    size = lax.axis_size(axis)
    if size & (size - 1):
        return lax.psum(values, axis)
    bit = 1
    while bit < size:
        values = values + swap(values, axis, bit)
        bit *= 2
    return values


def split_sum(values, axis):
    size = lax.axis_size(axis)
    if size & (size - 1) or values.shape[0] % size:
        return lax.psum(values, axis)
    index = lax.axis_index(axis)
    bits = [1 << k for k in range(size.bit_length() - 1)]
    for bit in bits:
        half = values.shape[0] // 2
        upper = (index & bit) // bit
        kept = lax.dynamic_slice_in_dim(values, upper * half, half, 0)
        given = lax.dynamic_slice_in_dim(values, (1 - upper) * half, half, 0)
        values = (kept.astype(F32) + swap(given, axis, bit).astype(F32)).astype(LOW)
    for bit in reversed(bits):
        got = swap(values, axis, bit)
        upper = (index & bit) > 0
        values = jnp.concatenate(
            [jnp.where(upper, got, values), jnp.where(upper, values, got)], axis=0
        )
    return values


def in_order(index, pieces):
    one, two = (index & 1) == 1, (index & 2) == 2
    a, b, c, d = pieces
    a, b, c, d = (
        jnp.where(one, b, a), jnp.where(one, a, b), jnp.where(one, d, c), jnp.where(one, c, d)
    )
    return (
        jnp.where(two, c, a), jnp.where(two, d, b), jnp.where(two, a, c), jnp.where(two, b, d)
    )


def gather_pieces(values):
    across = swap(values, "tensor", 2)
    return values, swap(values, "tensor", 1), across, swap(across, "tensor", 1)


def scatter_sum(keep, give):
    got = swap(give, "tensor", 1)
    middle = (keep[1].astype(F32) + got[1].astype(F32)).astype(LOW)
    return keep, got, swap(middle, "tensor", 2)


def body(
    hidden, segments, norm_gain, gate_weight, inner_weight, state_weight, step_weight, inner_taps,
    inner_offset, state_taps, state_offset, step_bias, decay_log, skip_weight, out_gain, out_weight,
    cotangent,
):
    tensor_index = lax.axis_index("tensor")
    me = tensor_index.astype(jnp.int32)[None]
    own_hidden, own_upstream, segment = hidden[0].T, cotangent[0].T, segments[0]
    part, tokens = own_hidden.shape
    features, channels = gate_weight.shape
    heads = step_weight.shape[1]
    states = state_weight.shape[1]
    half = states // 2
    own_states = states // 4
    blocks = tokens // BLOCK
    lanes = 128
    full_width = channels * lax.axis_size("tensor")
    ahead = lambda i: i
    behind = lambda i: blocks - 1 - i
    zero = lambda i: 0

    hidden_pieces = gather_pieces(own_hidden)
    upstream_pieces = gather_pieces(own_upstream)

    seg_blocks = segment.reshape(blocks, BLOCK)
    last_seg = seg_blocks[:, -1]
    previous = jnp.concatenate([jnp.full((1,), -1, jnp.int32), last_seg[:-1]])
    columns = []
    for back in range(1, 4):
        padded = jnp.pad(segment, (back, 0), constant_values=-1)[:tokens]
        columns.append(padded == segment)
    columns.append((seg_blocks == last_seg[:, None]).reshape(tokens))
    columns.append((seg_blocks == previous[:, None]).reshape(tokens))
    columns.append(segment)
    aux = jnp.stack([c.astype(F32) for c in columns] + [jnp.zeros((tokens,), F32)] * 2, axis=1)
    seg_rows = seg_blocks.astype(F32)[:, None, :]
    carry_mask = jnp.broadcast_to(
        (last_seg == previous).astype(F32)[:, None, None], (blocks, 1, lanes)
    )
    pad_heads = lambda v: jnp.pad(v, (0, lanes - heads))[None]
    step_w = jnp.pad(step_weight, ((0, 0), (0, lanes - heads)))
    bias_row = pad_heads(step_bias)
    rate_row = pad_heads(jnp.exp(decay_log))
    skip_row = jnp.repeat(skip_weight, HEAD)[None]
    gain_column = norm_gain[:, None]
    out_w_t = out_weight.T
    out_gain_row = out_gain[None]

    weight_spec = whole((features, channels))
    (
        normed, gate, inner_v, inner_c, state_v, state_c, pairs, raw, y, entering, scale, _, _, _,
    ) = call(
        forward_kernel,
        blocks,
        [
            (me, SCALAR),
            *[(piece, flat(part, ahead)) for piece in hidden_pieces],
            (gain_column, whole((features, 1))),
            (gate_weight, weight_spec),
            (inner_weight, weight_spec),
            (state_weight, whole((features, states))),
            (step_w, whole((features, lanes))),
            (inner_taps, whole((4, channels))),
            (inner_offset[None], whole((1, channels))),
            (state_taps, whole((4, states))),
            (state_offset[None], whole((1, states))),
            (bias_row, whole((1, lanes))),
            (rate_row, whole((1, lanes))),
            (skip_row, whole((1, channels))),
            (aux, rows(8, ahead)),
            (seg_rows, slab((1, BLOCK), ahead)),
            (carry_mask, slab((1, lanes), ahead)),
            (jnp.zeros((half, channels), F32), whole((half, channels))),
            (jnp.zeros((8, channels), F32), whole((8, channels))),
            (jnp.zeros((8, states), F32), whole((8, states))),
        ],
        [
            ((features, tokens), LOW, flat(features, ahead)),
            ((tokens, channels), F32, rows(channels, ahead)),
            ((tokens, channels), LOW, rows(channels, ahead)),
            ((tokens, channels), F32, rows(channels, ahead)),
            ((tokens, states), LOW, rows(states, ahead)),
            ((tokens, states), F32, rows(states, ahead)),
            ((tokens, states), LOW, rows(states, ahead)),
            ((tokens, lanes), F32, rows(lanes, ahead)),
            ((tokens, channels), F32, rows(channels, ahead)),
            ((blocks, half, channels), LOW, slab((half, channels), ahead)),
            ((blocks, 1, BLOCK), F32, slab((1, BLOCK), ahead)),
            ((half, channels), F32, whole((half, channels))),
            ((8, channels), F32, whole((8, channels))),
            ((8, states), F32, whole((8, states))),
        ],
        [
            pltpu.VMEM((half, channels), F32),
            pltpu.VMEM((8, channels), F32),
            pltpu.VMEM((8, states), F32),
            pltpu.VMEM((4, part, BLOCK), LOW),
        ],
        40_000_000_000,
    )

    upstream, normal_grad, sums = call(
        sums_kernel,
        blocks,
        [
            (me, SCALAR),
            *[(piece, flat(part, ahead)) for piece in upstream_pieces],
            (gate, rows(channels, ahead)),
            (y, rows(channels, ahead)),
            (out_w_t, weight_spec),
            (out_gain_row, whole((1, channels))),
        ],
        [
            ((features, tokens), LOW, flat(features, ahead)),
            ((tokens, channels), F32, rows(channels, ahead)),
            ((blocks, 2, BLOCK), F32, slab((2, BLOCK), ahead)),
        ],
        [pltpu.VMEM((4, part, BLOCK), LOW)],
        4_000_000_000,
    )
    sums = small_sum(sums, "tensor")

    piece_shape = (2, part, tokens)
    keep_o, give_o, out_w_grad, out_gain_grad, gate_low, dy, gate_w_grad = call(
        functools.partial(output_kernel, full_width),
        blocks,
        [
            (me, SCALAR),
            (sums, slab((2, BLOCK), ahead)),
            (upstream, flat(features, ahead)),
            (gate, rows(channels, ahead)),
            (y, rows(channels, ahead)),
            (normal_grad, rows(channels, ahead)),
            (normed, flat(features, ahead)),
            (out_w_t, weight_spec),
            (out_gain_row, whole((1, channels))),
        ],
        [
            (piece_shape, LOW, packed(2, part, ahead)),
            (piece_shape, LOW, packed(2, part, ahead)),
            ((channels, features), LOW, whole((channels, features))),
            ((1, channels), F32, whole((1, channels))),
            ((tokens, channels), LOW, rows(channels, ahead)),
            ((tokens, channels), F32, rows(channels, ahead)),
            ((features, channels), LOW, weight_spec),
        ],
        [pltpu.VMEM((features, channels), F32)] * 2,
        16_000_000_000,
    )
    branch_parts = scatter_sum(keep_o, give_o)
    out_w_grad, gate_w_grad = lax.psum((out_w_grad, gate_w_grad), "dp")

    pair_shape = (2, own_states, tokens)
    inner_low, keep_p, give_p, steps_low, row_grads, head_grads, _, _ = call(
        backward_kernel,
        blocks,
        [
            (me, SCALAR),
            (pairs, rows(states, behind)),
            (inner_c, rows(channels, behind)),
            (inner_v, rows(channels, behind)),
            (raw, rows(lanes, behind)),
            (dy, rows(channels, behind)),
            (entering, slab((half, channels), behind)),
            (aux, rows(8, behind)),
            (seg_rows, slab((1, BLOCK), behind)),
            (carry_mask, slab((1, lanes), behind)),
            (inner_taps, whole((4, channels))),
            (bias_row, whole((1, lanes))),
            (rate_row, whole((1, lanes))),
            (skip_row, whole((1, channels))),
            (jnp.zeros((half, channels), F32), whole((half, channels))),
            (jnp.zeros((3, 8, channels), F32), whole((3, 8, channels))),
        ],
        [
            ((tokens, channels), LOW, rows(channels, behind)),
            (pair_shape, LOW, packed(2, own_states, behind)),
            (pair_shape, LOW, packed(2, own_states, behind)),
            ((tokens, lanes), LOW, rows(lanes, behind)),
            ((8, channels), F32, whole((8, channels))),
            ((8, lanes), F32, whole((8, lanes))),
            ((half, channels), F32, whole((half, channels))),
            ((3, 8, channels), F32, whole((3, 8, channels))),
        ],
        [pltpu.VMEM((half, channels), F32), pltpu.VMEM((3, 8, channels), F32)],
        60_000_000_000,
    )
    pair_parts = scatter_sum(keep_p, give_p)

    local, scan_w_grad = call(
        return_kernel,
        blocks,
        [
            (gate_low, rows(channels, ahead)),
            (inner_low, rows(channels, ahead)),
            (steps_low, rows(lanes, ahead)),
            (normed, flat(features, ahead)),
            (gate_weight, weight_spec),
            (inner_weight, weight_spec),
            (step_w, whole((features, lanes))),
        ],
        [
            ((features, tokens), F32, flat(features, ahead)),
            ((features, channels + lanes), LOW, whole((features, channels + lanes))),
        ],
        [pltpu.VMEM((features, channels), F32), pltpu.VMEM((features, lanes), F32)],
        10_000_000_000,
    )
    scan_w_grad = split_sum(scan_w_grad, "dp")

    own_start = tensor_index * own_states
    own_taps = lax.dynamic_slice_in_dim(state_taps, own_start, own_states, 1)
    own_state_w = lax.dynamic_slice_in_dim(state_weight, own_start, own_states, 1)
    keep_n, give_n, row_dot, state_w_grad, state_rows, gain_sum = call(
        state_kernel,
        blocks,
        [
            (me, SCALAR),
            (pair_parts[0], packed(1, own_states, behind)),
            (pair_parts[1], packed(1, own_states, behind)),
            (pair_parts[2], flat(own_states, behind)),
            (state_c, rows(states, behind)),
            (state_v, rows(states, behind)),
            (normed, flat(features, behind)),
            (local, flat(features, behind)),
            (aux, rows(8, behind)),
            (own_taps, whole((4, own_states))),
            (own_state_w, whole((features, own_states))),
        ],
        [
            (piece_shape, LOW, packed(2, part, behind)),
            (piece_shape, LOW, packed(2, part, behind)),
            ((blocks, 1, BLOCK), F32, slab((1, BLOCK), behind)),
            ((own_states, features), F32, whole((own_states, features))),
            ((8, own_states), F32, whole((8, own_states))),
            ((8, features), F32, whole((8, features))),
        ],
        [
            pltpu.VMEM((3, 8, own_states), F32),
            pltpu.VMEM((features, own_states), F32),
            pltpu.VMEM((features, lanes), F32),
        ],
        4_000_000_000,
    )
    grad_parts = scatter_sum(keep_n, give_n)
    row_dot = small_sum(row_dot, "tensor")

    def total_of(parts):
        keep, got, last = parts
        return keep[0].astype(F32) + got[0].astype(F32) + last.astype(F32)

    output = (own_hidden.astype(F32) + total_of(branch_parts)).astype(LOW).T
    own_gain = lax.dynamic_slice_in_dim(norm_gain, tensor_index * part, part, 0)
    factor = scale.reshape(1, tokens)
    shrink = factor * factor * row_dot.reshape(1, tokens) / features
    input_grad = (
        own_upstream.astype(F32)
        + factor * (total_of(grad_parts) * own_gain[:, None])
        - own_hidden.astype(F32) * shrink
    ).T

    flat_size = 6 * channels + channels + 2 * lanes
    mine = jnp.concatenate(
        [row_grads[:6].reshape(-1), out_gain_grad.reshape(-1), head_grads[:2].reshape(-1)]
    )
    mine = jnp.pad(mine, (0, -flat_size % features)).reshape(-1, features)
    shared = jnp.concatenate([state_rows[:5].reshape(-1), jnp.zeros((-5 * own_states % features,), F32)])
    shared = jnp.concatenate([state_w_grad, shared.reshape(-1, features), gain_sum[:1]], axis=0)
    count = shared.shape[0]
    both = small_sum(jnp.concatenate([shared, mine], axis=0), "dp")
    shared, mine = both[:count], both[count:].reshape(-1)
    cut = 6 * channels
    row_grads = mine[:cut].reshape(6, channels)
    out_gain_grad = mine[cut : cut + channels]
    head_grads = mine[cut + channels : flat_size].reshape(2, lanes)

    members = in_order(tensor_index, gather_pieces(shared))
    state_w_grad = jnp.concatenate([m[:own_states] for m in members], axis=0).T
    state_rows = jnp.concatenate(
        [m[own_states:-1].reshape(-1)[: 5 * own_states].reshape(5, own_states) for m in members],
        axis=1,
    )
    norm_gain_grad = sum(m[-1] for m in members) / norm_gain

    return (
        output[None],
        input_grad[None],
        norm_gain_grad,
        gate_w_grad.astype(F32),
        scan_w_grad[:, :channels].astype(F32),
        state_w_grad,
        scan_w_grad[:, channels : channels + heads].astype(F32),
        row_grads[:4],
        row_grads[4],
        state_rows[:4],
        state_rows[4],
        head_grads[0, :heads],
        head_grads[1, :heads],
        jnp.sum(row_grads[5].reshape(heads, HEAD), axis=1),
        out_gain_grad,
        out_w_grad.astype(F32),
    )


def solution(mesh):
    rows_spec = P("dp", None, "tensor")
    columns_spec = P(None, "tensor")
    in_specs = (
        rows_spec, P("dp", None), P(), columns_spec, columns_spec, P(), columns_spec, columns_spec,
        P("tensor"), P(), P(), P("tensor"), P("tensor"), P("tensor"), P("tensor"),
        P("tensor", None), rows_spec,
    )
    out_specs = (
        rows_spec, rows_spec, P(), columns_spec, columns_spec, P(), columns_spec, columns_spec,
        P("tensor"), P(), P(), P("tensor"), P("tensor"), P("tensor"), P("tensor"),
        P("tensor", None),
    )
    return jax.shard_map(body, mesh=mesh, in_specs=in_specs, out_specs=out_specs, check_vma=False)
```

```python
import functools

import jax
import jax.numpy as jnp
from jax import lax
from jax.experimental import pallas as pl
from jax.experimental.pallas import tpu as pltpu
from jax.sharding import PartitionSpec as P

BLOCK = 256
EPSILON = 1e-05
HEAD = 64
F32 = jnp.float32
LOW = jnp.bfloat16
EXACT = lax.Precision.HIGHEST
VMEM_BYTES = 48 * 1024 * 1024


def mm(left, right):
    return jnp.dot(left, right, preferred_element_type=F32)


def mm_nt(left, right):
    return lax.dot_general(left, right, (((1,), (1,)), ((), ())), preferred_element_type=F32)


def mm_tn(left, right):
    return lax.dot_general(left, right, (((0,), (0,)), ((), ())), preferred_element_type=F32)


def iota(shape, axis):
    return lax.broadcasted_iota(jnp.int32, shape, axis)


def sigmoid(values):
    return 1.0 / (1.0 + jnp.exp(-values))


def softplus(values):
    return jnp.maximum(values, 0.0) + jnp.log1p(jnp.exp(-jnp.abs(values)))


def expand(columns, width):
    first = iota((1, 2 * HEAD), 1) < HEAD
    parts = []
    for pair in range(width // (2 * HEAD)):
        left = columns[:, 2 * pair : 2 * pair + 1]
        right = columns[:, 2 * pair + 1 : 2 * pair + 2]
        parts.append(jnp.where(first, left, right))
    return jnp.concatenate(parts, axis=1)


def collapse(values, lanes):
    width = values.shape[1]
    pick = (iota((width, lanes), 0) // HEAD == iota((width, lanes), 1)).astype(LOW)
    high = values.astype(LOW)
    rest = (values - high.astype(F32)).astype(LOW)
    return mm(high, pick) + mm(rest, pick)


def join_pieces(me, pieces, joined):
    for relative, piece in enumerate(pieces):
        joined[pl.ds(me ^ relative, 1)] = piece[...][None]
    return joined[...].reshape(joined.shape[0] * joined.shape[1], joined.shape[2])


def store_pieces(me, values, keep_ref, give_ref):
    width = values.shape[0] // 4
    for dest in range(4):
        piece = values[dest * width : (dest + 1) * width].astype(LOW)[None]
        relative = me ^ dest

        @pl.when((relative & 1) == 0)
        def _():
            keep_ref[pl.ds(relative >> 1, 1)] = piece

        @pl.when((relative & 1) == 1)
        def _():
            give_ref[pl.ds(relative >> 1, 1)] = piece


def block_conv(ext, values, taps, offset, aux):
    rows = values.shape[0]
    total = offset + taps[3:4] * values
    for back in range(1, 4):
        total = total + taps[3 - back : 4 - back] * (
            aux[:, back - 1 : back] * ext[8 - back : 8 - back + rows]
        )
    return total


def conv_back(dpre, carry_ref, taps, values, aux):
    rows = dpre.shape[0]
    grad = taps[3:4] * dpre
    taps_grads = [jnp.sum(values * dpre, axis=0, keepdims=True)]
    for back in range(1, 4):
        masked = dpre * aux[:, back - 1 : back]
        ext = jnp.concatenate([masked, carry_ref[back - 1]], axis=0)
        carry_ref[back - 1] = masked[0:8]
        shifted = ext[back : back + rows]
        grad = grad + taps[3 - back : 4 - back] * shifted
        taps_grads.insert(0, jnp.sum(values * shifted, axis=0, keepdims=True))
    return grad, taps_grads


def scan_parts(raw, step_bias, rate, aux, seg_row):
    length, lanes = raw.shape
    shifted = raw + step_bias
    step = softplus(shifted)
    log_decay = -step * rate
    lower = (iota((length, length), 0) >= iota((length, length), 1)).astype(F32)
    cum = jnp.dot(lower, log_decay, precision=EXACT, preferred_element_type=F32)
    allowed = (iota((length, length), 0) >= iota((length, length), 1)) & (aux[:, 5:6] == seg_row)
    last = cum[length - 1 : length]
    reach = jnp.exp(cum) * aux[:, 4:5]
    fade = jnp.exp(last - cum) * aux[:, 3:4]
    return shifted, step, log_decay, cum, allowed, last, reach, fade


def forward_kernel(
    me_ref, x0, x1, x2, x3, gain, gate_w, inner_w, state_w, step_w, taps_i, off_i, taps_s, off_s,
    step_bias, rate, skip, aux_ref, seg_row, carry_mask, run_in, ci_in, cs_in,
    normed_out, gate_out, inner_v, inner_c, state_v, state_c, pairs_out, raw_out, y_out, enter_out,
    scale_out, run_out, ci_out, cs_out,
    run, carry_i, carry_s, joined,
):
    at = pl.program_id(0)

    @pl.when(at == 0)
    def _():
        run[...] = run_in[...]
        carry_i[...] = ci_in[...]
        carry_s[...] = cs_in[...]

    aux = aux_ref[...]
    rows = join_pieces(me_ref[0], (x0, x1, x2, x3), joined).astype(F32)
    factor = lax.rsqrt(jnp.mean(rows * rows, axis=0, keepdims=True) + EPSILON)
    normed_t = (rows * factor * gain[...]).astype(LOW)
    normed_out[...] = normed_t
    scale_out[0] = factor
    normed = normed_t.T
    gate_out[...] = mm(normed, gate_w[...])
    inner = mm(normed, inner_w[...])
    state = mm(normed, state_w[...])
    raw = mm(normed, step_w[...])
    raw_out[...] = raw
    inner_v[...] = inner.astype(LOW)
    state_v[...] = state.astype(LOW)
    inner_pre = block_conv(
        jnp.concatenate([carry_i[...], inner], axis=0), inner, taps_i[...], off_i[...], aux
    )
    state_pre = block_conv(
        jnp.concatenate([carry_s[...], state], axis=0), state, taps_s[...], off_s[...], aux
    )
    carry_i[...] = inner[-8:]
    carry_s[...] = state[-8:]
    inner_c[...] = inner_pre
    state_c[...] = state_pre
    active = (inner_pre * sigmoid(inner_pre)).astype(LOW)
    pairs = (state_pre * sigmoid(state_pre)).astype(LOW)
    pairs_out[...] = pairs
    half = pairs.shape[1] // 2
    write, read = pairs[:, :half], pairs[:, half:]
    shifted, step, log_decay, cum, allowed, last, reach, fade = scan_parts(
        raw, step_bias[...], rate[...], aux, seg_row[0]
    )
    cum_t, step_t = cum.T, step.T
    scores = mm_nt(read, write)
    width = active.shape[1]
    first = iota((1, 2 * HEAD), 1) < HEAD
    parts = []
    for pair in range(width // (2 * HEAD)):
        values = active[:, pair * 2 * HEAD : (pair + 1) * 2 * HEAD]
        got = []
        for head in (2 * pair, 2 * pair + 1):
            spread = cum[:, head : head + 1] - cum_t[head : head + 1]
            weights = jnp.exp(jnp.where(allowed, spread, -1e30)) * scores * step_t[head : head + 1]
            got.append(mm(weights.astype(LOW), values))
        parts.append(jnp.where(first, got[0], got[1]))
    within = jnp.concatenate(parts, axis=1)
    entering = run[...]
    entering_low = entering.astype(LOW)
    enter_out[0] = entering_low
    active_wide = active.astype(F32)
    across = mm(read, entering_low) * expand(reach, width)
    y_out[...] = within + across + skip[...] * active_wide
    fresh = mm_tn(write, (expand(fade * step, width) * active_wide).astype(LOW))
    run[...] = expand(jnp.exp(last) * carry_mask[0], width) * entering + fresh

    @pl.when(at == pl.num_programs(0) - 1)
    def _():
        run_out[...] = run[...]
        ci_out[...] = carry_i[...]
        cs_out[...] = carry_s[...]


def sums_kernel(
    me_ref, u0, u1, u2, u3, gate, y, out_w_t, out_gain, up_out, grad_out, sums_out, joined
):
    upstream_t = join_pieces(me_ref[0], (u0, u1, u2, u3), joined)
    up_out[...] = upstream_t
    z = gate[...]
    gated = y[...] * (z * sigmoid(z))
    normal_grad = mm(upstream_t.T, out_w_t[...])
    grad_out[...] = normal_grad
    square = jnp.sum(gated * gated, axis=1, keepdims=True)
    cross = jnp.sum(normal_grad * out_gain[...] * gated, axis=1, keepdims=True)
    lane = iota((gated.shape[0], 128), 1)
    sums_out[0] = jnp.where(lane == 0, square, cross).T[0:2]


def output_kernel(
    full_width, me_ref, sums, upstream_t, gate, y_ref, grad_ref, normed_t, out_w_t, out_gain,
    keep, give, early_grad, out_gain_grad, gate_low, dy_out, total_o, total_g,
):
    at = pl.program_id(0)

    @pl.when(at == 0)
    def _():
        total_o[...] = jnp.zeros_like(total_o)
        total_g[...] = jnp.zeros_like(total_g)
        out_gain_grad[...] = jnp.zeros_like(out_gain_grad)

    pair = jnp.concatenate([sums[0], jnp.zeros((126, sums.shape[2]), F32)], axis=0).T
    square, cross = pair[:, 0:1], pair[:, 1:2]
    z, y = gate[...], y_ref[...]
    sig = sigmoid(z)
    swish = z * sig
    gated = y * swish
    scale = lax.rsqrt(square / full_width + EPSILON)
    gated_normed = (gated * scale * out_gain[...]).astype(LOW)
    store_pieces(me_ref[0], mm_nt(out_w_t[...], gated_normed), keep, give)
    total_o[...] += mm(upstream_t[...], gated_normed)
    normal_grad = grad_ref[...]
    out_gain_grad[...] += jnp.sum(normal_grad * gated * scale, axis=0, keepdims=True)
    weighted = normal_grad * out_gain[...]
    gated_grad = scale * weighted - gated * (scale * scale * scale * (cross / full_width))
    dy_out[...] = gated_grad * swish
    low = (gated_grad * y * (sig * (1.0 + z * (1.0 - sig)))).astype(LOW)
    gate_low[...] = low
    total_g[...] += mm(normed_t[...], low)

    @pl.when(at == pl.num_programs(0) - 1)
    def _():
        early_grad[0 : total_o.shape[0]] = total_o[...].astype(LOW)
        early_grad[total_o.shape[0] :] = total_g[...].astype(LOW)


def backward_kernel(
    me_ref, pairs_ref, inner_c, inner_v, raw_ref, dy_ref, enter_ref, aux_ref, seg_row, carry_mask,
    taps_i, step_bias, rate, skip, normed_t, state_in, carry_in, rows_in, heads_in, inner_in, steps_in,
    inner_low, keep, give, steps_low, state_out, carry_out, rows_out, heads_out, inner_out, steps_out,
    back, carry_z,
):
    at = pl.program_id(0)

    @pl.when(at == 0)
    def _():
        back[...] = state_in[...]
        carry_z[...] = carry_in[...]
        rows_out[...] = rows_in[...]
        heads_out[...] = heads_in[...]
        inner_out[...] = inner_in[...]
        steps_out[...] = steps_in[...]

    aux = aux_ref[...]
    pre = inner_c[...]
    sig = sigmoid(pre)
    active = (pre * sig).astype(LOW)
    active_wide = active.astype(F32)
    width = active.shape[1]
    pairs = pairs_ref[...]
    half = pairs.shape[1] // 2
    write, read = pairs[:, :half], pairs[:, half:]
    shifted, step, log_decay, cum, allowed, last, reach, fade = scan_parts(
        raw_ref[...], step_bias[...], rate[...], aux, seg_row[0]
    )
    length, lanes = cum.shape
    cum_t, step_t = cum.T, step.T
    scores = mm_nt(read, write)
    dy = dy_ref[...]
    dy_low = dy.astype(LOW)
    entering_low = enter_ref[0]
    reach_wide = expand(reach, width)
    toward_wide = expand(fade * step, width)
    dy_reach = dy * reach_wide
    dy_reach_low = dy_reach.astype(LOW)
    from_state = mm(read, entering_low)
    dcum = collapse(dy_reach * from_state, lanes)
    dread = mm_nt(dy_reach_low, entering_low)
    dentering = mm_tn(read, dy_reach_low)
    grad_state = back[...]
    grad_low = grad_state.astype(LOW)
    from_grad = mm(write, grad_low)
    dwrite = mm_nt((toward_wide * active_wide).astype(LOW), grad_low)
    dtoward = collapse(active_wide * from_grad, lanes)
    dfade = dtoward * (fade * step)
    dcum = dcum - dfade
    dstep = dtoward * fade
    keep_factor = jnp.exp(last) * carry_mask[0]
    kept = jnp.sum(grad_state * entering_low.astype(F32), axis=0, keepdims=True)
    kept = collapse(jnp.broadcast_to(kept, (8, width)), lanes)[0:1]
    dlast = jnp.sum(dfade, axis=0, keepdims=True) + keep_factor * kept
    back[...] = expand(keep_factor, width) * grad_state + dentering

    first = iota((1, 2 * HEAD), 1) < HEAD
    lane = iota((length, lanes), 1)
    dscores = jnp.zeros((length, length), F32)
    row_sums = jnp.zeros((length, lanes), F32)
    column_sums = []
    parts = []
    for pair in range(width // (2 * HEAD)):
        values = active[:, pair * 2 * HEAD : (pair + 1) * 2 * HEAD]
        grads = dy_low[:, pair * 2 * HEAD : (pair + 1) * 2 * HEAD]
        got = []
        for head in (2 * pair, 2 * pair + 1):
            own = jnp.where(first == (head % 2 == 0), grads, jnp.zeros_like(grads))
            steps_row = step_t[head : head + 1]
            spread = cum[:, head : head + 1] - cum_t[head : head + 1]
            decays = jnp.exp(jnp.where(allowed, spread, -1e30))
            dweights = mm_nt(own, values) * decays
            with_scores = dweights * scores
            dscores = dscores + dweights * steps_row
            column_sums.append(jnp.sum(with_scores, axis=0, keepdims=True))
            head_sum = jnp.sum(with_scores * steps_row, axis=1, keepdims=True)
            row_sums = jnp.where(lane == head, head_sum, row_sums)
            weights = (decays * scores * steps_row).astype(LOW)
            got.append(mm_tn(weights, grads))
        parts.append(jnp.where(first, got[0], got[1]))
    column_sums.append(jnp.zeros((lanes - len(column_sums), length), F32))
    columns = jnp.concatenate(column_sums, axis=0).T
    dscores_low = dscores.astype(LOW)
    dread = dread + mm(dscores_low, write)
    dwrite = dwrite + mm_tn(dscores_low, read)
    dstep = dstep + columns
    dcum = dcum + row_sums - step * columns
    dcum = dcum + jnp.where(iota((length, 1), 0) == length - 1, dlast, 0.0)
    upper = (iota((length, length), 0) <= iota((length, length), 1)).astype(F32)
    dlog = jnp.dot(upper, dcum, precision=EXACT, preferred_element_type=F32)
    dstep = dstep - dlog * rate[...]
    draw = dstep * sigmoid(shifted)
    draw_low = draw.astype(LOW)
    steps_low[...] = draw_low
    heads_out[0:1] += jnp.sum(draw, axis=0, keepdims=True)
    heads_out[1:2] += jnp.sum(dlog * log_decay, axis=0, keepdims=True)

    dactive = jnp.concatenate(parts, axis=1) + skip[...] * dy + toward_wide * from_grad
    dpre = dactive * (sig * (1.0 + pre * (1.0 - sig)))
    grad, taps_grads = conv_back(dpre, carry_z, taps_i[...], inner_v[...].astype(F32), aux)
    low = grad.astype(LOW)
    inner_low[...] = low
    inner_out[...] += mm(normed_t[...], low)
    steps_out[...] += mm(normed_t[...], draw_low)
    for tap in range(4):
        rows_out[tap : tap + 1] += taps_grads[tap]
    rows_out[4:5] += jnp.sum(dpre, axis=0, keepdims=True)
    rows_out[5:6] += jnp.sum(dy * active_wide, axis=0, keepdims=True)
    store_pieces(me_ref[0], jnp.concatenate([dwrite, dread], axis=1).T, keep, give)

    @pl.when(at == pl.num_programs(0) - 1)
    def _():
        state_out[...] = back[...]
        carry_out[...] = carry_z[...]


def return_kernel(gate_low, inner_low, steps_low, gate_w, inner_w, step_w, local):
    local[...] = (
        mm_nt(gate_w[...], gate_low[...])
        + mm_nt(inner_w[...], inner_low[...])
        + mm_nt(step_w[...], steps_low[...])
    )


def state_kernel(
    me_ref, part_a, part_b, part_c, state_c, state_v, normed_ref, local_ref, aux_ref, taps, state_w,
    keep, give, row_dot, state_w_grad, rows_out, gain_out, carry_z, total, gain_total,
):
    at = pl.program_id(0)
    me = me_ref[0]

    @pl.when(at == 0)
    def _():
        carry_z[...] = jnp.zeros_like(carry_z)
        total[...] = jnp.zeros_like(total)
        rows_out[...] = jnp.zeros_like(rows_out)
        gain_total[...] = jnp.zeros_like(gain_total)

    def own(values):
        values = values.astype(F32)
        width = values.shape[1] // 4
        picked = jnp.where((me & 2) == 2, values[:, 2 * width :], values[:, : 2 * width])
        return jnp.where((me & 1) == 1, picked[:, width:], picked[:, :width])

    dpairs = (part_a[0].astype(F32) + part_b[0].astype(F32) + part_c[...].astype(F32)).T
    pre = own(state_c[...])
    sig = sigmoid(pre)
    dpre = dpairs * (sig * (1.0 + pre * (1.0 - sig)))
    grad, taps_grads = conv_back(dpre, carry_z, taps[...], own(state_v[...]), aux_ref[...])
    low = grad.astype(LOW)
    for tap in range(4):
        rows_out[tap : tap + 1] += taps_grads[tap]
    rows_out[4:5] += jnp.sum(dpre, axis=0, keepdims=True)
    normed_t = normed_ref[...]
    total[...] += mm(normed_t, low)
    values = local_ref[...] + mm_nt(state_w[...], low)
    store_pieces(me, values, keep, give)
    product = values * normed_t.astype(F32)
    row_dot[0] = jnp.sum(product, axis=0, keepdims=True)
    gain_total[...] += sum(
        product[:, at : at + 128] for at in range(0, product.shape[1], 128)
    )

    @pl.when(at == pl.num_programs(0) - 1)
    def _():
        state_w_grad[...] = total[...].T
        column = jnp.sum(gain_total[...], axis=1, keepdims=True)
        gain_out[...] = jnp.broadcast_to(column, gain_total.shape).T[0:8]


def rows(columns, index):
    return pl.BlockSpec((BLOCK, columns), lambda i: (index(i), 0))


def slab(shape, index):
    return pl.BlockSpec((1, *shape), lambda i: (index(i),) + (0,) * len(shape))


def whole(shape):
    return pl.BlockSpec(shape, lambda i: (0,) * len(shape))


def flat(features, index):
    return pl.BlockSpec((features, BLOCK), lambda i: (0, index(i)))


def packed(count, features, index):
    return pl.BlockSpec((count, features, BLOCK), lambda i: (0, 0, index(i)))


SCALAR = pl.BlockSpec(memory_space=pltpu.SMEM)


def call(kernel, blocks, ins, outs, scratch, flops, fill=()):
    count = len(ins)
    ins = [*ins, *((array, pl.BlockSpec(memory_space=pl.ANY)) for _, array in fill)]
    aliases = {count + at: out for at, (out, _) in enumerate(fill)}
    if fill:
        inner_kernel = kernel

        def kernel(*refs):
            return inner_kernel(*refs[:count], *refs[count + len(fill) :])

    arrays = [array for array, _ in ins]
    shapes = [jax.ShapeDtypeStruct(shape, dtype) for shape, dtype, _ in outs]
    return pl.pallas_call(
        kernel,
        grid=(blocks,),
        in_specs=[spec for _, spec in ins],
        out_specs=[spec for _, _, spec in outs],
        out_shape=shapes,
        scratch_shapes=scratch,
        input_output_aliases=aliases,
        compiler_params=pltpu.CompilerParams(
            dimension_semantics=("arbitrary",), vmem_limit_bytes=VMEM_BYTES
        ),
        cost_estimate=pl.CostEstimate(flops=flops, bytes_accessed=1, transcendentals=0),
    )(*arrays)


def swap(values, axis, bit):
    size = lax.axis_size(axis)
    return lax.ppermute(values, axis, [(i, i ^ bit) for i in range(size)])


def small_sum(values, axis):
    size = lax.axis_size(axis)
    if size & (size - 1):
        return lax.psum(values, axis)
    bit = 1
    while bit < size:
        values = values + swap(values, axis, bit)
        bit *= 2
    return values


def split_half(values, axis, bit):
    half = values.shape[0] // 2
    upper = (lax.axis_index(axis) & bit) // bit
    kept = lax.dynamic_slice_in_dim(values, upper * half, half, 0)
    given = lax.dynamic_slice_in_dim(values, (1 - upper) * half, half, 0)
    return kept, swap(given, axis, bit)


def join_half(values, axis, bit):
    return place_half(values, swap(values, axis, bit), axis, bit)


def place_half(values, got, axis, bit):
    upper = (lax.axis_index(axis) & bit) > 0
    return jnp.concatenate(
        [jnp.where(upper, got, values), jnp.where(upper, values, got)], axis=0
    )


def add_low(left, right):
    return (left.astype(F32) + right.astype(F32)).astype(LOW)


def axis_bits(axis):
    size = lax.axis_size(axis)
    return [] if size & (size - 1) else [1 << k for k in range(size.bit_length() - 1)]


def in_order(index, pieces):
    one, two = (index & 1) == 1, (index & 2) == 2
    a, b, c, d = pieces
    a, b, c, d = (
        jnp.where(one, b, a), jnp.where(one, a, b), jnp.where(one, d, c), jnp.where(one, c, d)
    )
    return (
        jnp.where(two, c, a), jnp.where(two, d, b), jnp.where(two, a, c), jnp.where(two, b, d)
    )


def gather_pieces(values):
    across = swap(values, "tensor", 2)
    return values, swap(values, "tensor", 1), across, swap(across, "tensor", 1)


def after(values, *earlier):
    return lax.optimization_barrier((values, *earlier))


def scatter_sum(keep, give):
    got = swap(give, "tensor", 1)
    middle = (keep[1].astype(F32) + got[1].astype(F32)).astype(LOW)
    return keep, got, middle


def body(
    hidden, segments, norm_gain, gate_weight, inner_weight, state_weight, step_weight, inner_taps,
    inner_offset, state_taps, state_offset, step_bias, decay_log, skip_weight, out_gain, out_weight,
    cotangent,
):
    tensor_index = lax.axis_index("tensor")
    me = tensor_index.astype(jnp.int32)[None]
    own_hidden, own_upstream, segment = hidden[0].T, cotangent[0].T, segments[0]
    part, tokens = own_hidden.shape
    features, channels = gate_weight.shape
    heads = step_weight.shape[1]
    states = state_weight.shape[1]
    half = states // 2
    own_states = states // 4
    blocks = tokens // BLOCK
    lanes = 128
    full_width = channels * lax.axis_size("tensor")
    ahead = lambda i: i
    behind = lambda i: blocks - 1 - i
    zero = lambda i: 0

    hidden_pieces = gather_pieces(own_hidden)
    upstream_start, _ = after(own_upstream, hidden_pieces[2])
    upstream_across = swap(upstream_start, "tensor", 2)

    seg_blocks = segment.reshape(blocks, BLOCK)
    last_seg = seg_blocks[:, -1]
    previous = jnp.concatenate([jnp.full((1,), -1, jnp.int32), last_seg[:-1]])
    columns = []
    for back in range(1, 4):
        padded = jnp.pad(segment, (back, 0), constant_values=-1)[:tokens]
        columns.append(padded == segment)
    columns.append((seg_blocks == last_seg[:, None]).reshape(tokens))
    columns.append((seg_blocks == previous[:, None]).reshape(tokens))
    columns.append(segment)
    aux = jnp.stack([c.astype(F32) for c in columns] + [jnp.zeros((tokens,), F32)] * 2, axis=1)
    seg_rows = seg_blocks.astype(F32)[:, None, :]
    carry_mask = jnp.broadcast_to(
        (last_seg == previous).astype(F32)[:, None, None], (blocks, 1, lanes)
    )
    pad_heads = lambda v: jnp.pad(v, (0, lanes - heads))[None]
    step_w = jnp.pad(step_weight, ((0, 0), (0, lanes - heads)))
    bias_row = pad_heads(step_bias)
    rate_row = pad_heads(jnp.exp(decay_log))
    skip_row = jnp.repeat(skip_weight, HEAD)[None]
    gain_column = norm_gain[:, None]
    out_w_t = out_weight.T
    out_gain_row = out_gain[None]

    weight_spec = whole((features, channels))
    (
        normed, gate, inner_v, inner_c, state_v, state_c, pairs, raw, y, entering, scale, _, _, _,
    ) = call(
        forward_kernel,
        blocks,
        [
            (me, SCALAR),
            *[(piece, flat(part, ahead)) for piece in hidden_pieces],
            (gain_column, whole((features, 1))),
            (gate_weight, weight_spec),
            (inner_weight, weight_spec),
            (state_weight, whole((features, states))),
            (step_w, whole((features, lanes))),
            (inner_taps, whole((4, channels))),
            (inner_offset[None], whole((1, channels))),
            (state_taps, whole((4, states))),
            (state_offset[None], whole((1, states))),
            (bias_row, whole((1, lanes))),
            (rate_row, whole((1, lanes))),
            (skip_row, whole((1, channels))),
            (aux, rows(8, ahead)),
            (seg_rows, slab((1, BLOCK), ahead)),
            (carry_mask, slab((1, lanes), ahead)),
            (jnp.zeros((half, channels), F32), whole((half, channels))),
            (jnp.zeros((8, channels), F32), whole((8, channels))),
            (jnp.zeros((8, states), F32), whole((8, states))),
        ],
        [
            ((features, tokens), LOW, flat(features, ahead)),
            ((tokens, channels), F32, rows(channels, ahead)),
            ((tokens, channels), LOW, rows(channels, ahead)),
            ((tokens, channels), F32, rows(channels, ahead)),
            ((tokens, states), LOW, rows(states, ahead)),
            ((tokens, states), F32, rows(states, ahead)),
            ((tokens, states), LOW, rows(states, ahead)),
            ((tokens, lanes), F32, rows(lanes, ahead)),
            ((tokens, channels), F32, rows(channels, ahead)),
            ((blocks, half, channels), LOW, slab((half, channels), ahead)),
            ((blocks, 1, BLOCK), F32, slab((1, BLOCK), ahead)),
            ((half, channels), F32, whole((half, channels))),
            ((8, channels), F32, whole((8, channels))),
            ((8, states), F32, whole((8, states))),
        ],
        [
            pltpu.VMEM((half, channels), F32),
            pltpu.VMEM((8, channels), F32),
            pltpu.VMEM((8, states), F32),
            pltpu.VMEM((4, part, BLOCK), LOW),
        ],
        1,
    )

    upstream_across, y = after(upstream_across, y)
    upstream_own, y = after(own_upstream, y)
    upstream_pieces = (
        own_upstream,
        swap(upstream_own, "tensor", 1),
        upstream_across,
        swap(upstream_across, "tensor", 1),
    )
    upstream, normal_grad, sums = call(
        sums_kernel,
        blocks,
        [
            (me, SCALAR),
            *[(piece, flat(part, ahead)) for piece in upstream_pieces],
            (gate, rows(channels, ahead)),
            (y, rows(channels, ahead)),
            (out_w_t, weight_spec),
            (out_gain_row, whole((1, channels))),
        ],
        [
            ((features, tokens), LOW, flat(features, ahead)),
            ((tokens, channels), F32, rows(channels, ahead)),
            ((blocks, 2, BLOCK), F32, slab((2, BLOCK), ahead)),
        ],
        [pltpu.VMEM((4, part, BLOCK), LOW)],
        1,
    )
    sums = small_sum(sums, "tensor")

    piece_shape = (2, part, tokens)
    keep_o, give_o, early_grad, out_gain_grad, gate_low, dy = call(
        functools.partial(output_kernel, full_width),
        blocks,
        [
            (me, SCALAR),
            (sums, slab((2, BLOCK), ahead)),
            (upstream, flat(features, ahead)),
            (gate, rows(channels, ahead)),
            (y, rows(channels, ahead)),
            (normal_grad, rows(channels, ahead)),
            (normed, flat(features, ahead)),
            (out_w_t, weight_spec),
            (out_gain_row, whole((1, channels))),
        ],
        [
            (piece_shape, LOW, packed(2, part, ahead)),
            (piece_shape, LOW, packed(2, part, ahead)),
            ((2 * features, channels), LOW, whole((2 * features, channels))),
            ((1, channels), F32, whole((1, channels))),
            ((tokens, channels), LOW, rows(channels, ahead)),
            ((tokens, channels), F32, rows(channels, ahead)),
        ],
        [pltpu.VMEM((features, channels), F32)] * 2,
        1,
    )
    keep_o, got_o, middle_o = scatter_sum(keep_o, give_o)
    bits = axis_bits("dp")
    by_steps = len(bits) > 2 and features % (1 << len(bits)) == 0
    early = []
    if by_steps:
        early = list(split_half(early_grad, "dp", bits[0]))
    else:
        early_grad = lax.psum(early_grad, "dp")
    dy, middle_o = after(dy, middle_o)
    branch_parts = (keep_o, got_o, swap(middle_o, "tensor", 2))

    pair_shape = (2, own_states, tokens)
    sums_shapes = [
        (half, channels), (3, 8, channels), (8, channels), (8, lanes), (features, channels),
        (features, lanes),
    ]
    carried = [jnp.zeros(shape, F32) for shape in sums_shapes]
    filled = []
    parts_of_scan = 2 if blocks % 2 == 0 else 1
    for section in range(parts_of_scan):
        count = blocks // parts_of_scan
        top = blocks - 1 - section * count
        back_from = lambda i, top=top: top - i
        got_all = call(
            backward_kernel,
            count,
            [
                (me, SCALAR),
                (pairs, rows(states, back_from)),
                (inner_c, rows(channels, back_from)),
                (inner_v, rows(channels, back_from)),
                (raw, rows(lanes, back_from)),
                (dy, rows(channels, back_from)),
                (entering, slab((half, channels), back_from)),
                (aux, rows(8, back_from)),
                (seg_rows, slab((1, BLOCK), back_from)),
                (carry_mask, slab((1, lanes), back_from)),
                (inner_taps, whole((4, channels))),
                (bias_row, whole((1, lanes))),
                (rate_row, whole((1, lanes))),
                (skip_row, whole((1, channels))),
                (normed, flat(features, back_from)),
                *[(array, whole(array.shape)) for array in carried],
            ],
            [
                ((tokens, channels), LOW, rows(channels, back_from)),
                (pair_shape, LOW, packed(2, own_states, back_from)),
                (pair_shape, LOW, packed(2, own_states, back_from)),
                ((tokens, lanes), LOW, rows(lanes, back_from)),
                *[(shape, F32, whole(shape)) for shape in sums_shapes],
            ],
            [pltpu.VMEM((half, channels), F32), pltpu.VMEM((3, 8, channels), F32)],
            1,
            list(enumerate(filled)),
        )
        if section == 0 and by_steps:
            *got_all, kept, given = after(*got_all, *early)
            early = [kept, given]
            early_grad = add_low(*early)
            early = list(split_half(early_grad, "dp", bits[1]))
        filled, carried = got_all[:4], got_all[4:]
    got_branch, *held = after(branch_parts[2], *filled, *carried, *early)
    branch_parts = (*branch_parts[:2], got_branch)
    inner_low, keep_p, give_p, steps_low, _, _, row_grads, head_grads, inner_w_grad, step_w_grad = held[:10]
    early = held[10:]
    keep_p, got_p, middle_p = scatter_sum(keep_p, give_p)
    inner_w_grad = inner_w_grad.astype(LOW)
    late_i = []
    if by_steps:
        early_grad = add_low(*early)
        early = list(split_half(early_grad, "dp", bits[2]))
        late_i = list(split_half(inner_w_grad, "dp", bits[0]))
    else:
        inner_w_grad = lax.psum(inner_w_grad, "dp")
    inner_low, middle_p = after(inner_low, middle_p)
    pair_parts = (keep_p, got_p, swap(middle_p, "tensor", 2))

    local = call(
        return_kernel,
        blocks,
        [
            (gate_low, rows(channels, ahead)),
            (inner_low, rows(channels, ahead)),
            (steps_low, rows(lanes, ahead)),
            (gate_weight, weight_spec),
            (inner_weight, weight_spec),
            (step_w, whole((features, lanes))),
        ],
        [
            ((features, tokens), F32, flat(features, ahead)),
        ],
        [],
        1,
    )[0]

    if by_steps:
        local, *moved = after(local, *early, *late_i)
        early_grad = add_low(*moved[:2])
        for bit in bits[3:]:
            early_grad = add_low(*split_half(early_grad, "dp", bit))
        for bit in reversed(bits[3:]):
            early_grad = join_half(early_grad, "dp", bit)
        early_got = swap(early_grad, "dp", bits[2])
        inner_w_grad = add_low(*moved[2:])
        late_i = list(split_half(inner_w_grad, "dp", bits[1]))
    own_start = tensor_index * own_states
    own_taps = lax.dynamic_slice_in_dim(state_taps, own_start, own_states, 1)
    own_state_w = lax.dynamic_slice_in_dim(state_weight, own_start, own_states, 1)
    keep_n, give_n, row_dot, state_w_grad, state_rows, gain_sum = call(
        state_kernel,
        blocks,
        [
            (me, SCALAR),
            (pair_parts[0], packed(1, own_states, behind)),
            (pair_parts[1], packed(1, own_states, behind)),
            (pair_parts[2], flat(own_states, behind)),
            (state_c, rows(states, behind)),
            (state_v, rows(states, behind)),
            (normed, flat(features, behind)),
            (local, flat(features, behind)),
            (aux, rows(8, behind)),
            (own_taps, whole((4, own_states))),
            (own_state_w, whole((features, own_states))),
        ],
        [
            (piece_shape, LOW, packed(2, part, behind)),
            (piece_shape, LOW, packed(2, part, behind)),
            ((blocks, 1, BLOCK), F32, slab((1, BLOCK), behind)),
            ((own_states, features), F32, whole((own_states, features))),
            ((8, own_states), F32, whole((8, own_states))),
            ((8, features), F32, whole((8, features))),
        ],
        [
            pltpu.VMEM((3, 8, own_states), F32),
            pltpu.VMEM((features, own_states), F32),
            pltpu.VMEM((features, lanes), F32),
        ],
        1,
    )
    if by_steps:
        early_got, *late_i, keep_n, give_n, row_dot, state_w_grad, state_rows, gain_sum = after(
            early_got, *late_i, keep_n, give_n, row_dot, state_w_grad, state_rows, gain_sum
        )
        early_grad = place_half(early_grad, early_got, "dp", bits[2])
        inner_w_grad = add_low(*late_i)
    keep_n, got_n, middle_n = scatter_sum(keep_n, give_n)
    row_dot, state_w_grad, middle_n = after(row_dot, state_w_grad, middle_n)
    grad_parts = (keep_n, got_n, swap(middle_n, "tensor", 2))
    row_dot = small_sum(row_dot, "tensor")
    if by_steps:
        early_grad, inner_w_grad, middle_n = after(early_grad, inner_w_grad, middle_n)
        for bit in bits[2:]:
            inner_w_grad = add_low(*split_half(inner_w_grad, "dp", bit))
        for bit in reversed(bits[:2]):
            early_grad = join_half(early_grad, "dp", bit)
        for bit in reversed(bits):
            inner_w_grad = join_half(inner_w_grad, "dp", bit)
    out_w_grad = early_grad[:features].T.astype(F32)
    gate_w_grad = early_grad[features:].astype(F32)

    def total_of(parts):
        keep, got, last = parts
        return keep[0].astype(F32) + got[0].astype(F32) + last.astype(F32)

    output = (own_hidden.astype(F32) + total_of(branch_parts)).astype(LOW).T
    own_gain = lax.dynamic_slice_in_dim(norm_gain, tensor_index * part, part, 0)
    factor = scale.reshape(1, tokens)
    shrink = factor * factor * row_dot.reshape(1, tokens) / features
    input_grad = (
        own_upstream.astype(F32)
        + factor * (total_of(grad_parts) * own_gain[:, None])
        - own_hidden.astype(F32) * shrink
    ).T

    flat_size = 6 * channels + channels + 2 * lanes
    mine = jnp.concatenate(
        [row_grads[:6].reshape(-1), out_gain_grad.reshape(-1), head_grads[:2].reshape(-1)]
    )
    mine = jnp.pad(mine, (0, -flat_size % features)).reshape(-1, features)
    shared = jnp.concatenate([state_rows[:5].reshape(-1), jnp.zeros((-5 * own_states % features,), F32)])
    step_rows = step_w_grad[:, :8].T
    mine = jnp.concatenate([step_rows, mine], axis=0)
    shared = jnp.concatenate([state_w_grad, shared.reshape(-1, features), gain_sum[:1]], axis=0)
    count = shared.shape[0]
    both = small_sum(jnp.concatenate([shared, mine], axis=0), "dp")
    shared, step_w_grad, mine = both[:count], both[count : count + 8], both[count + 8 :].reshape(-1)
    cut = 6 * channels
    row_grads = mine[:cut].reshape(6, channels)
    out_gain_grad = mine[cut : cut + channels]
    head_grads = mine[cut + channels : flat_size].reshape(2, lanes)

    members = in_order(tensor_index, gather_pieces(shared))
    state_w_grad = jnp.concatenate([m[:own_states] for m in members], axis=0).T
    state_rows = jnp.concatenate(
        [m[own_states:-1].reshape(-1)[: 5 * own_states].reshape(5, own_states) for m in members],
        axis=1,
    )
    norm_gain_grad = sum(m[-1] for m in members) / norm_gain

    return (
        output[None],
        input_grad[None],
        norm_gain_grad,
        gate_w_grad,
        inner_w_grad.astype(F32),
        state_w_grad,
        step_w_grad[:heads].T,
        row_grads[:4],
        row_grads[4],
        state_rows[:4],
        state_rows[4],
        head_grads[0, :heads],
        head_grads[1, :heads],
        jnp.sum(row_grads[5].reshape(heads, HEAD), axis=1),
        out_gain_grad,
        out_w_grad,
    )


def solution(mesh):
    rows_spec = P("dp", None, "tensor")
    columns_spec = P(None, "tensor")
    in_specs = (
        rows_spec, P("dp", None), P(), columns_spec, columns_spec, P(), columns_spec, columns_spec,
        P("tensor"), P(), P(), P("tensor"), P("tensor"), P("tensor"), P("tensor"),
        P("tensor", None), rows_spec,
    )
    out_specs = (
        rows_spec, rows_spec, P(), columns_spec, columns_spec, P(), columns_spec, columns_spec,
        P("tensor"), P(), P(), P("tensor"), P("tensor"), P("tensor"), P("tensor"),
        P("tensor", None),
    )
    return jax.shard_map(body, mesh=mesh, in_specs=in_specs, out_specs=out_specs, check_vma=False)
```

```python
import functools

import jax
import jax.numpy as jnp
from jax import lax
from jax.experimental import pallas as pl
from jax.experimental.pallas import tpu as pltpu
from jax.sharding import PartitionSpec as P

BLOCK = 256
EPSILON = 1e-05
HEAD = 64
F32 = jnp.float32
LOW = jnp.bfloat16
VMEM_BYTES = 48 * 1024 * 1024


def mm(left, right):
    return jnp.dot(left, right, preferred_element_type=F32)


def mm_nt(left, right):
    return lax.dot_general(left, right, (((1,), (1,)), ((), ())), preferred_element_type=F32)


def mm_tn(left, right):
    return lax.dot_general(left, right, (((0,), (0,)), ((), ())), preferred_element_type=F32)


def iota(shape, axis):
    return lax.broadcasted_iota(jnp.int32, shape, axis)


def sigmoid(values):
    return 0.5 * jnp.tanh(0.5 * values) + 0.5


def softplus(values):
    return jnp.maximum(values, 0.0) + jnp.log1p(jnp.exp(-jnp.abs(values)))


GROUP = 8


def split_lanes(columns, count):
    rest = jnp.where(iota(columns.shape, 1) < GROUP, columns, 0.0)
    total = jnp.zeros_like(rest)
    for at in range(count):
        high = rest.astype(LOW).astype(F32)
        total = total + (pltpu.roll(high, at * GROUP, 1) if at else high)
        rest = rest - high
    return total.astype(LOW)


def expand(many, width):
    lanes = many[0].shape[1]
    packed_lanes = jnp.concatenate([split_lanes(columns, 2) for columns in many], axis=0)
    row, head = iota((lanes, width), 0), iota((lanes, width), 1) // HEAD
    wide = mm(packed_lanes, ((row == head) | (row == head + GROUP)).astype(LOW))
    ends = [0]
    for columns in many:
        ends.append(ends[-1] + columns.shape[0])
    return [wide[a:b] for a, b in zip(ends, ends[1:])]


def expand_row(row, width):
    return expand([jnp.broadcast_to(row, (8, row.shape[1]))], width)[0][0:1]


def running_sum(mask, columns):
    wide = mm(mask.astype(LOW), split_lanes(columns, 3))
    lanes = columns.shape[1]
    total = wide + pltpu.roll(wide, lanes - GROUP, 1) + pltpu.roll(wide, lanes - 2 * GROUP, 1)
    return jnp.where(iota(total.shape, 1) < GROUP, total, 0.0)


def collapse(values, lanes):
    width = values.shape[1]
    pick = (iota((width, lanes), 0) // HEAD == iota((width, lanes), 1)).astype(LOW)
    high = values.astype(LOW)
    rest = (values - high.astype(F32)).astype(LOW)
    return mm(high, pick) + mm(rest, pick)


def join_pieces(me, pieces, joined):
    for relative, piece in enumerate(pieces):
        joined[pl.ds(me ^ relative, 1)] = piece[...][None]
    return joined[...].reshape(joined.shape[0] * joined.shape[1], joined.shape[2])


def store_pieces(me, values, keep_ref, give_ref):
    width = values.shape[0] // 4
    for dest in range(4):
        piece = values[dest * width : (dest + 1) * width].astype(LOW)[None]
        relative = me ^ dest

        @pl.when((relative & 1) == 0)
        def _():
            keep_ref[pl.ds(relative >> 1, 1)] = piece

        @pl.when((relative & 1) == 1)
        def _():
            give_ref[pl.ds(relative >> 1, 1)] = piece


def block_conv(ext, values, taps, offset, aux):
    rows = values.shape[0]
    total = offset + taps[3:4] * values
    for back in range(1, 4):
        total = total + taps[3 - back : 4 - back] * (
            aux[:, back - 1 : back] * ext[8 - back : 8 - back + rows]
        )
    return total


def conv_back(dpre, carry_ref, taps, values, aux):
    rows = dpre.shape[0]
    grad = taps[3:4] * dpre
    taps_grads = [jnp.sum(values * dpre, axis=0, keepdims=True)]
    for back in range(1, 4):
        masked = dpre * aux[:, back - 1 : back]
        ext = jnp.concatenate([masked, carry_ref[back - 1]], axis=0)
        carry_ref[back - 1] = masked[0:8]
        shifted = ext[back : back + rows]
        grad = grad + taps[3 - back : 4 - back] * shifted
        taps_grads.insert(0, jnp.sum(values * shifted, axis=0, keepdims=True))
    return grad, taps_grads


def scan_parts(raw, step_bias, rate, aux, seg_row, flipped):
    length, lanes = raw.shape
    shifted = raw + step_bias
    step = softplus(shifted)
    log_decay = -step * rate
    down, right = iota((length, length), 0), iota((length, length), 1)
    cum = running_sum(down >= right, log_decay)
    causal = (down <= right) if flipped else (down >= right)
    allowed = causal & (aux[:, 5:6] == seg_row)
    last = cum[length - 1 : length]
    reach = jnp.exp(cum) * aux[:, 4:5]
    fade = jnp.exp(last - cum) * aux[:, 3:4]
    return shifted, step, log_decay, cum, allowed, last, reach, fade


def forward_kernel(
    me_ref, x0, x1, x2, x3, gain, gate_w, inner_w, state_w, step_w, taps_i, off_i, taps_s, off_s,
    step_bias, rate, skip, aux_ref, seg_row, carry_mask, run_in, ci_in, cs_in,
    normed_out, gate_out, inner_v, inner_c, state_v, state_c, pairs_out, raw_out, y_out, enter_out,
    scale_out, run_out, ci_out, cs_out,
    run, carry_i, carry_s, joined,
):
    at = pl.program_id(0)

    @pl.when(at == 0)
    def _():
        run[...] = run_in[...]
        carry_i[...] = ci_in[...]
        carry_s[...] = cs_in[...]

    aux = aux_ref[...]
    rows = join_pieces(me_ref[0], (x0, x1, x2, x3), joined).astype(F32)
    factor = lax.rsqrt(jnp.mean(rows * rows, axis=0, keepdims=True) + EPSILON)
    normed_t = (rows * factor * gain[...]).astype(LOW)
    normed_out[...] = normed_t
    scale_out[0] = factor
    normed = normed_t.T
    gate_out[...] = mm(normed, gate_w[...])
    inner = mm(normed, inner_w[...])
    state = mm(normed, state_w[...])
    raw = mm(normed, step_w[...])
    raw_out[...] = raw
    inner_v[...] = inner.astype(LOW)
    state_v[...] = state.astype(LOW)
    inner_pre = block_conv(
        jnp.concatenate([carry_i[...], inner], axis=0), inner, taps_i[...], off_i[...], aux
    )
    state_pre = block_conv(
        jnp.concatenate([carry_s[...], state], axis=0), state, taps_s[...], off_s[...], aux
    )
    carry_i[...] = inner[-8:]
    carry_s[...] = state[-8:]
    inner_c[...] = inner_pre
    state_c[...] = state_pre
    active = (inner_pre * sigmoid(inner_pre)).astype(LOW)
    pairs = (state_pre * sigmoid(state_pre)).astype(LOW)
    pairs_out[...] = pairs
    half = pairs.shape[1] // 2
    write, read = pairs[:, :half], pairs[:, half:]
    shifted, step, log_decay, cum, allowed, last, reach, fade = scan_parts(
        raw, step_bias[...], rate[...], aux, seg_row[0], False
    )
    cum_t = cum.T
    scores = mm_nt(read, write)
    width = active.shape[1]
    active_wide = active.astype(F32)
    step_wide, reach_wide, fade_wide = expand([step, reach, fade], width)
    scaled = (step_wide * active_wide).astype(LOW)
    first = iota((1, 2 * HEAD), 1) < HEAD
    parts = []
    for pair in range(width // (2 * HEAD)):
        values = scaled[:, pair * 2 * HEAD : (pair + 1) * 2 * HEAD]
        got = []
        for head in (2 * pair, 2 * pair + 1):
            spread = cum[:, head : head + 1] - cum_t[head : head + 1]
            decays = jnp.exp(jnp.where(allowed, spread, -1e30))
            got.append(mm((decays * scores).astype(LOW), values))
        parts.append(jnp.where(first, got[0], got[1]))
    within = jnp.concatenate(parts, axis=1)
    entering = run[...]
    entering_low = entering.astype(LOW)
    enter_out[0] = entering_low
    across = mm(read, entering_low) * reach_wide
    y_out[...] = within + across + skip[...] * active_wide
    fresh = mm_tn(write, (fade_wide * step_wide * active_wide).astype(LOW))
    run[...] = expand_row(jnp.exp(last) * carry_mask[0], width) * entering + fresh

    @pl.when(at == pl.num_programs(0) - 1)
    def _():
        run_out[...] = run[...]
        ci_out[...] = carry_i[...]
        cs_out[...] = carry_s[...]


def sums_kernel(
    me_ref, u0, u1, u2, u3, gate, y, out_w_t, out_gain, up_out, grad_out, sums_out, joined
):
    upstream_t = join_pieces(me_ref[0], (u0, u1, u2, u3), joined)
    up_out[...] = upstream_t
    z = gate[...]
    gated = y[...] * (z * sigmoid(z))
    normal_grad = mm(upstream_t.T, out_w_t[...])
    grad_out[...] = normal_grad
    square = jnp.sum(gated * gated, axis=1, keepdims=True)
    cross = jnp.sum(normal_grad * out_gain[...] * gated, axis=1, keepdims=True)
    lane = iota((gated.shape[0], 128), 1)
    sums_out[0] = jnp.where(lane == 0, square, cross).T[0:2]


def output_kernel(
    full_width, me_ref, sums, upstream_t, gate, y_ref, grad_ref, normed_t, out_w_t, out_gain,
    keep, give, early_grad, out_gain_grad, gate_low, dy_out, total_o, total_g,
):
    at = pl.program_id(0)

    @pl.when(at == 0)
    def _():
        total_o[...] = jnp.zeros_like(total_o)
        total_g[...] = jnp.zeros_like(total_g)
        out_gain_grad[...] = jnp.zeros_like(out_gain_grad)

    pair = jnp.concatenate([sums[0], jnp.zeros((126, sums.shape[2]), F32)], axis=0).T
    square, cross = pair[:, 0:1], pair[:, 1:2]
    z, y = gate[...], y_ref[...]
    sig = sigmoid(z)
    swish = z * sig
    gated = y * swish
    scale = lax.rsqrt(square / full_width + EPSILON)
    gated_normed = (gated * scale * out_gain[...]).astype(LOW)
    store_pieces(me_ref[0], mm_nt(out_w_t[...], gated_normed), keep, give)
    total_o[...] += mm(upstream_t[...], gated_normed)
    normal_grad = grad_ref[...]
    out_gain_grad[...] += jnp.sum(normal_grad * gated * scale, axis=0, keepdims=True)
    weighted = normal_grad * out_gain[...]
    gated_grad = scale * weighted - gated * (scale * scale * scale * (cross / full_width))
    dy_out[...] = gated_grad * swish
    low = (gated_grad * y * (sig * (1.0 + z * (1.0 - sig)))).astype(LOW)
    gate_low[...] = low
    total_g[...] += mm(normed_t[...], low)

    @pl.when(at == pl.num_programs(0) - 1)
    def _():
        early_grad[0 : total_o.shape[0]] = total_o[...].astype(LOW)
        early_grad[total_o.shape[0] :] = total_g[...].astype(LOW)


def backward_kernel(
    me_ref, pairs_ref, inner_c, inner_v, raw_ref, dy_ref, enter_ref, aux_ref, seg_row, carry_mask,
    taps_i, step_bias, rate, skip, normed_t, state_in, carry_in, rows_in, heads_in, inner_in, steps_in,
    inner_low, keep, give, steps_low, state_out, carry_out, rows_out, heads_out, inner_out, steps_out,
    back, carry_z,
):
    at = pl.program_id(0)

    @pl.when(at == 0)
    def _():
        back[...] = state_in[...]
        carry_z[...] = carry_in[...]
        rows_out[...] = rows_in[...]
        heads_out[...] = heads_in[...]
        inner_out[...] = inner_in[...]
        steps_out[...] = steps_in[...]

    aux = aux_ref[...]
    pre = inner_c[...]
    sig = sigmoid(pre)
    active = (pre * sig).astype(LOW)
    active_wide = active.astype(F32)
    width = active.shape[1]
    pairs = pairs_ref[...]
    half = pairs.shape[1] // 2
    write, read = pairs[:, :half], pairs[:, half:]
    shifted, step, log_decay, cum, allowed, last, reach, fade = scan_parts(
        raw_ref[...], step_bias[...], rate[...], aux, seg_row[0], True
    )
    length, lanes = cum.shape
    cum_t = cum.T
    scores_t = mm_nt(write, read)
    dy = dy_ref[...]
    dy_low = dy.astype(LOW)
    entering_low = enter_ref[0]
    step_wide, reach_wide, fade_wide = expand([step, reach, fade], width)
    toward_wide = fade_wide * step_wide
    scaled = (step_wide * active_wide).astype(LOW)
    dy_reach = dy * reach_wide
    dy_reach_low = dy_reach.astype(LOW)
    from_state = mm(read, entering_low)
    dcum = collapse(dy_reach * from_state, lanes)
    dread = mm_nt(dy_reach_low, entering_low)
    dentering = mm_tn(read, dy_reach_low)
    grad_state = back[...]
    grad_low = grad_state.astype(LOW)
    from_grad = mm(write, grad_low)
    dwrite = mm_nt((toward_wide * active_wide).astype(LOW), grad_low)
    dtoward = collapse(active_wide * from_grad, lanes)
    dfade = dtoward * (fade * step)
    dcum = dcum - dfade
    dstep = dtoward * fade
    keep_factor = jnp.exp(last) * carry_mask[0]
    kept = jnp.sum(grad_state * entering_low.astype(F32), axis=0, keepdims=True)
    kept = collapse(jnp.broadcast_to(kept, (8, width)), lanes)[0:1]
    dlast = jnp.sum(dfade, axis=0, keepdims=True) + keep_factor * kept
    back[...] = expand_row(keep_factor, width) * grad_state + dentering

    first = iota((1, 2 * HEAD), 1) < HEAD
    lane = iota((length, lanes), 1)
    dscores = jnp.zeros((length, length), F32)
    source_sums = jnp.zeros((length, lanes), F32)
    target_sums = []
    parts = []
    for pair in range(width // (2 * HEAD)):
        values = scaled[:, pair * 2 * HEAD : (pair + 1) * 2 * HEAD]
        grads = dy_low[:, pair * 2 * HEAD : (pair + 1) * 2 * HEAD]
        got = []
        for head in (2 * pair, 2 * pair + 1):
            own = jnp.where(first == (head % 2 == 0), grads, jnp.zeros_like(grads))
            spread = cum_t[head : head + 1] - cum[:, head : head + 1]
            decays = jnp.exp(jnp.where(allowed, spread, -1e30))
            graded = mm_nt(values, own) * decays
            dscores = dscores + graded
            scored = graded * scores_t
            source = jnp.sum(scored, axis=1, keepdims=True)
            source_sums = jnp.where(lane == head, source, source_sums)
            target_sums.append(jnp.sum(scored, axis=0, keepdims=True))
            got.append(mm((decays * scores_t).astype(LOW), grads))
        parts.append(jnp.where(first, got[0], got[1]))
    target_sums.append(jnp.zeros((lanes - len(target_sums), length), F32))
    target_sums = jnp.concatenate(target_sums, axis=0).T
    dscores_low = dscores.astype(LOW)
    dread = dread + mm_tn(dscores_low, write)
    dwrite = dwrite + mm(dscores_low, read)
    dstep = dstep + source_sums / jnp.maximum(step, 1e-30)
    dcum = dcum + target_sums - source_sums
    dcum = dcum + jnp.where(iota((length, 1), 0) == length - 1, dlast, 0.0)
    dlog = running_sum(iota((length, length), 0) <= iota((length, length), 1), dcum)
    dstep = dstep - dlog * rate[...]
    draw = dstep * sigmoid(shifted)
    draw_low = draw.astype(LOW)
    steps_low[...] = draw_low
    heads_out[0:1] += jnp.sum(draw, axis=0, keepdims=True)
    heads_out[1:2] += jnp.sum(dlog * log_decay, axis=0, keepdims=True)

    dactive = step_wide * jnp.concatenate(parts, axis=1) + skip[...] * dy + toward_wide * from_grad
    dpre = dactive * (sig * (1.0 + pre * (1.0 - sig)))
    grad, taps_grads = conv_back(dpre, carry_z, taps_i[...], inner_v[...].astype(F32), aux)
    low = grad.astype(LOW)
    inner_low[...] = low
    inner_out[...] += mm(normed_t[...], low)
    steps_out[...] += mm(normed_t[...], draw_low)
    for tap in range(4):
        rows_out[tap : tap + 1] += taps_grads[tap]
    rows_out[4:5] += jnp.sum(dpre, axis=0, keepdims=True)
    rows_out[5:6] += jnp.sum(dy * active_wide, axis=0, keepdims=True)
    store_pieces(me_ref[0], jnp.concatenate([dwrite, dread], axis=1).T, keep, give)

    @pl.when(at == pl.num_programs(0) - 1)
    def _():
        state_out[...] = back[...]
        carry_out[...] = carry_z[...]


def return_kernel(gate_low, inner_low, steps_low, gate_w, inner_w, step_w, local):
    local[...] = (
        mm_nt(gate_w[...], gate_low[...])
        + mm_nt(inner_w[...], inner_low[...])
        + mm_nt(step_w[...], steps_low[...])
    )


def state_kernel(
    me_ref, part_a, part_b, part_c, state_c, state_v, normed_ref, local_ref, aux_ref, taps, state_w,
    steps_in, rows_in, heads_in,
    keep, give, row_dot, late, carry_z, total, gain_total, rows_out,
):
    at = pl.program_id(0)
    me = me_ref[0]

    @pl.when(at == 0)
    def _():
        carry_z[...] = jnp.zeros_like(carry_z)
        total[...] = jnp.zeros_like(total)
        rows_out[...] = jnp.zeros_like(rows_out)
        gain_total[...] = jnp.zeros_like(gain_total)

    def own(values):
        values = values.astype(F32)
        width = values.shape[1] // 4
        picked = jnp.where((me & 2) == 2, values[:, 2 * width :], values[:, : 2 * width])
        return jnp.where((me & 1) == 1, picked[:, width:], picked[:, :width])

    dpairs = (part_a[0].astype(F32) + part_b[0].astype(F32) + part_c[...].astype(F32)).T
    pre = own(state_c[...])
    sig = sigmoid(pre)
    dpre = dpairs * (sig * (1.0 + pre * (1.0 - sig)))
    grad, taps_grads = conv_back(dpre, carry_z, taps[...], own(state_v[...]), aux_ref[...])
    low = grad.astype(LOW)
    for tap in range(4):
        rows_out[tap : tap + 1] += taps_grads[tap]
    rows_out[4:5] += jnp.sum(dpre, axis=0, keepdims=True)
    normed_t = normed_ref[...]
    total[...] += mm(normed_t, low)
    values = local_ref[...] + mm_nt(state_w[...], low)
    store_pieces(me, values, keep, give)
    product = values * normed_t.astype(F32)
    row_dot[0] = jnp.sum(product, axis=0, keepdims=True)
    gain_total[...] += sum(
        product[:, at : at + 128] for at in range(0, product.shape[1], 128)
    )

    @pl.when(at == pl.num_programs(0) - 1)
    def _():
        states, channels, heads = total.shape[1], rows_in.shape[1], heads_in.shape[1]
        width = total.shape[0]
        column = jnp.sum(gain_total[...], axis=1, keepdims=True)
        taps_row = [rows_out[row : row + 1] for row in range(5)]
        taps_row = jnp.concatenate([*taps_row, jnp.zeros((1, width - 5 * states), F32)], axis=1)
        lists = jnp.concatenate(
            [rows_in[...], heads_in[...], jnp.zeros((8, width - channels - heads), F32)], axis=1
        )
        late[...] = jnp.concatenate(
            [
                total[...].T,
                taps_row,
                jnp.broadcast_to(column, gain_total.shape).T[0:1],
                jnp.zeros((14, width), F32),
                steps_in[...].T[0:8],
                lists,
            ],
            axis=0,
        ).astype(LOW)


def lists_kernel(own, step_grad, taps_grad, offset_grad, out_gain_grad, skip_grad, head_grads):
    channels = taps_grad.shape[1]
    values = own[...].astype(F32)
    steps = values[0:8]
    step_grad[...] = jnp.concatenate([steps, jnp.zeros((120, steps.shape[1]), F32)], axis=0).T
    rows = values[8:16, 0:channels]
    taps_grad[...] = rows[0:4]
    offset_grad[...] = rows[4:5]
    out_gain_grad[...] = rows[6:7]
    skip_grad[...] = collapse(rows, 128)
    head_grads[...] = values[8:16, channels : channels + 128]


def state_grads_kernel(me_ref, m0, m1, m2, m3, gain, state_w_grad, state_rows, gain_grad, gathered):
    states = gathered.shape[1]
    total = jnp.zeros(gain.shape, F32)
    for relative, member in enumerate((m0, m1, m2, m3)):
        dest = me_ref[0] ^ relative
        values = member[...].astype(F32)
        gathered[pl.ds(dest, 1)] = values[0:states][None]
        state_rows[pl.ds(dest, 1)] = values[states : states + 1][None]
        total = total + values[states + 1 : states + 2]
    state_w_grad[...] = gathered[...].reshape(4 * states, gain.shape[1]).T
    gain_grad[...] = total / gain[...]


def rows(columns, index, size=BLOCK):
    return pl.BlockSpec((size, columns), lambda i: (index(i), 0))


def slab(shape, index):
    return pl.BlockSpec((1, *shape), lambda i: (index(i),) + (0,) * len(shape))


def whole(shape):
    return pl.BlockSpec(shape, lambda i: (0,) * len(shape))


def flat(features, index, size=BLOCK):
    return pl.BlockSpec((features, size), lambda i: (0, index(i)))


def packed(count, features, index, size=BLOCK):
    return pl.BlockSpec((count, features, size), lambda i: (0, 0, index(i)))


SCALAR = pl.BlockSpec(memory_space=pltpu.SMEM)


def call(kernel, blocks, ins, outs, scratch, flops, fill=()):
    count = len(ins)
    ins = [*ins, *((array, pl.BlockSpec(memory_space=pl.ANY)) for _, array in fill)]
    aliases = {count + at: out for at, (out, _) in enumerate(fill)}
    if fill:
        inner_kernel = kernel

        def kernel(*refs):
            return inner_kernel(*refs[:count], *refs[count + len(fill) :])

    arrays = [array for array, _ in ins]
    shapes = [jax.ShapeDtypeStruct(shape, dtype) for shape, dtype, _ in outs]
    return pl.pallas_call(
        kernel,
        grid=(blocks,),
        in_specs=[spec for _, spec in ins],
        out_specs=[spec for _, _, spec in outs],
        out_shape=shapes,
        scratch_shapes=scratch,
        input_output_aliases=aliases,
        compiler_params=pltpu.CompilerParams(
            dimension_semantics=("arbitrary",), vmem_limit_bytes=VMEM_BYTES
        ),
        cost_estimate=pl.CostEstimate(flops=flops, bytes_accessed=1, transcendentals=0),
    )(*arrays)


def swap(values, axis, bit):
    size = lax.axis_size(axis)
    return lax.ppermute(values, axis, [(i, i ^ bit) for i in range(size)])


def small_sum(values, axis):
    size = lax.axis_size(axis)
    if size & (size - 1):
        return lax.psum(values, axis)
    bit = 1
    while bit < size:
        values = values + swap(values, axis, bit)
        bit *= 2
    return values


def split_half(values, axis, bit):
    half = values.shape[0] // 2
    upper = (lax.axis_index(axis) & bit) // bit
    kept = lax.dynamic_slice_in_dim(values, upper * half, half, 0)
    given = lax.dynamic_slice_in_dim(values, (1 - upper) * half, half, 0)
    return kept, swap(given, axis, bit)


def join_half(values, axis, bit):
    return place_half(values, swap(values, axis, bit), axis, bit)


def place_half(values, got, axis, bit):
    upper = (lax.axis_index(axis) & bit) > 0
    return jnp.concatenate(
        [jnp.where(upper, got, values), jnp.where(upper, values, got)], axis=0
    )


def add_low(left, right):
    return (left.astype(F32) + right.astype(F32)).astype(LOW)


def axis_bits(axis):
    size = lax.axis_size(axis)
    return [] if size & (size - 1) else [1 << k for k in range(size.bit_length() - 1)]


def in_order(index, pieces):
    one, two = (index & 1) == 1, (index & 2) == 2
    a, b, c, d = pieces
    a, b, c, d = (
        jnp.where(one, b, a), jnp.where(one, a, b), jnp.where(one, d, c), jnp.where(one, c, d)
    )
    return (
        jnp.where(two, c, a), jnp.where(two, d, b), jnp.where(two, a, c), jnp.where(two, b, d)
    )


def gather_pieces(values):
    across = swap(values, "tensor", 2)
    return values, swap(values, "tensor", 1), across, swap(across, "tensor", 1)


def after(values, *earlier):
    return lax.optimization_barrier((values, *earlier))


def scatter_sum(keep, give):
    got = swap(give, "tensor", 1)
    middle = (keep[1].astype(F32) + got[1].astype(F32)).astype(LOW)
    return keep, got, middle


def body(
    hidden, segments, norm_gain, gate_weight, inner_weight, state_weight, step_weight, inner_taps,
    inner_offset, state_taps, state_offset, step_bias, decay_log, skip_weight, out_gain, out_weight,
    cotangent,
):
    tensor_index = lax.axis_index("tensor")
    me = tensor_index.astype(jnp.int32)[None]
    own_hidden, own_upstream, segment = hidden[0].T, cotangent[0].T, segments[0]
    part, tokens = own_hidden.shape
    features, channels = gate_weight.shape
    heads = step_weight.shape[1]
    states = state_weight.shape[1]
    half = states // 2
    own_states = states // 4
    blocks = tokens // BLOCK
    lanes = 128
    full_width = channels * lax.axis_size("tensor")
    ahead = lambda i: i
    behind = lambda i: blocks - 1 - i
    wide = 2 * BLOCK if tokens % (2 * BLOCK) == 0 else BLOCK
    behind_wide = lambda i: tokens // wide - 1 - i

    sections = 2 if blocks % 2 == 0 else 1
    cut = tokens // sections
    starts = [own_hidden[:, at * cut : (at + 1) * cut] for at in range(sections)]
    crossed = []
    for start in starts:
        if crossed:
            start, crossed[-1] = after(start, crossed[-1])
        crossed.append(swap(start, "tensor", 2))
    upstream_start, crossed[0] = after(own_upstream, crossed[0])
    upstream_across = swap(upstream_start, "tensor", 2)

    seg_blocks = segment.reshape(blocks, BLOCK)
    last_seg = seg_blocks[:, -1]
    previous = jnp.concatenate([jnp.full((1,), -1, jnp.int32), last_seg[:-1]])
    columns = []
    for back in range(1, 4):
        padded = jnp.pad(segment, (back, 0), constant_values=-1)[:tokens]
        columns.append(padded == segment)
    columns.append((seg_blocks == last_seg[:, None]).reshape(tokens))
    columns.append((seg_blocks == previous[:, None]).reshape(tokens))
    columns.append(segment)
    aux = jnp.stack([c.astype(F32) for c in columns] + [jnp.zeros((tokens,), F32)] * 2, axis=1)
    seg_rows = seg_blocks.astype(F32)[:, None, :]
    carry_mask = jnp.broadcast_to(
        (last_seg == previous).astype(F32)[:, None, None], (blocks, 1, lanes)
    )
    pad_heads = lambda v: jnp.pad(v, (0, lanes - heads))[None]
    step_w = jnp.pad(step_weight, ((0, 0), (0, lanes - heads)))
    bias_row = pad_heads(step_bias)
    rate_row = pad_heads(jnp.exp(decay_log))
    skip_row = jnp.repeat(skip_weight, HEAD)[None]
    gain_column = norm_gain[:, None]
    out_w_t = out_weight.T
    out_gain_row = out_gain[None]

    weight_spec = whole((features, channels))
    states_shapes = [(half, channels), (8, channels), (8, states)]
    carried = [jnp.zeros(shape, F32) for shape in states_shapes]
    filled = []
    for section in range(sections):
        count = blocks // sections
        onward = lambda i, base=section * count: base + i
        pieces = (
            starts[section],
            swap(starts[section], "tensor", 1),
            crossed[section],
            swap(crossed[section], "tensor", 1),
        )
        got_all = call(
            forward_kernel,
            count,
            [
                (me, SCALAR),
                *[(piece, flat(part, ahead)) for piece in pieces],
                (gain_column, whole((features, 1))),
                (gate_weight, weight_spec),
                (inner_weight, weight_spec),
                (state_weight, whole((features, states))),
                (step_w, whole((features, lanes))),
                (inner_taps, whole((4, channels))),
                (inner_offset[None], whole((1, channels))),
                (state_taps, whole((4, states))),
                (state_offset[None], whole((1, states))),
                (bias_row, whole((1, lanes))),
                (rate_row, whole((1, lanes))),
                (skip_row, whole((1, channels))),
                (aux, rows(8, onward)),
                (seg_rows, slab((1, BLOCK), onward)),
                (carry_mask, slab((1, lanes), onward)),
                *[(array, whole(array.shape)) for array in carried],
            ],
            [
                ((features, tokens), LOW, flat(features, onward)),
                ((tokens, channels), F32, rows(channels, onward)),
                ((tokens, channels), LOW, rows(channels, onward)),
                ((tokens, channels), F32, rows(channels, onward)),
                ((tokens, states), LOW, rows(states, onward)),
                ((tokens, states), F32, rows(states, onward)),
                ((tokens, states), LOW, rows(states, onward)),
                ((tokens, lanes), F32, rows(lanes, onward)),
                ((tokens, channels), F32, rows(channels, onward)),
                ((blocks, half, channels), LOW, slab((half, channels), onward)),
                ((blocks, 1, BLOCK), F32, slab((1, BLOCK), onward)),
                *[(shape, F32, whole(shape)) for shape in states_shapes],
            ],
            [
                *[pltpu.VMEM(shape, F32) for shape in states_shapes],
                pltpu.VMEM((4, part, BLOCK), LOW),
            ],
            1,
            list(enumerate(filled)),
        )
        if section + 1 < sections:
            crossed[section + 1], *got_all = after(crossed[section + 1], *got_all)
        filled, carried = got_all[:11], got_all[11:]
    normed, gate, inner_v, inner_c, state_v, state_c, pairs, raw, y, entering, scale = filled

    upstream_across, y = after(upstream_across, y)
    upstream_own, y = after(own_upstream, y)
    upstream_pieces = (
        own_upstream,
        swap(upstream_own, "tensor", 1),
        upstream_across,
        swap(upstream_across, "tensor", 1),
    )
    upstream, normal_grad, sums = call(
        sums_kernel,
        tokens // wide,
        [
            (me, SCALAR),
            *[(piece, flat(part, ahead, wide)) for piece in upstream_pieces],
            (gate, rows(channels, ahead, wide)),
            (y, rows(channels, ahead, wide)),
            (out_w_t, weight_spec),
            (out_gain_row, whole((1, channels))),
        ],
        [
            ((features, tokens), LOW, flat(features, ahead, wide)),
            ((tokens, channels), F32, rows(channels, ahead, wide)),
            ((tokens // wide, 2, wide), F32, slab((2, wide), ahead)),
        ],
        [pltpu.VMEM((4, part, wide), LOW)],
        1,
    )
    sums = small_sum(sums, "tensor")

    piece_shape = (2, part, tokens)
    keep_o, give_o, early_grad, out_gain_grad, gate_low, dy = call(
        functools.partial(output_kernel, full_width),
        tokens // wide,
        [
            (me, SCALAR),
            (sums, slab((2, wide), ahead)),
            (upstream, flat(features, ahead, wide)),
            (gate, rows(channels, ahead, wide)),
            (y, rows(channels, ahead, wide)),
            (normal_grad, rows(channels, ahead, wide)),
            (normed, flat(features, ahead, wide)),
            (out_w_t, weight_spec),
            (out_gain_row, whole((1, channels))),
        ],
        [
            (piece_shape, LOW, packed(2, part, ahead, wide)),
            (piece_shape, LOW, packed(2, part, ahead, wide)),
            ((2 * features, channels), LOW, whole((2 * features, channels))),
            ((1, channels), F32, whole((1, channels))),
            ((tokens, channels), LOW, rows(channels, ahead, wide)),
            ((tokens, channels), F32, rows(channels, ahead, wide)),
        ],
        [pltpu.VMEM((features, channels), F32)] * 2,
        1,
    )
    keep_o, got_o, middle_o = scatter_sum(keep_o, give_o)
    bits = axis_bits("dp")
    by_steps = len(bits) > 2 and features % (1 << len(bits)) == 0
    early = []
    if by_steps:
        early = list(split_half(early_grad, "dp", bits[0]))
    else:
        early_grad = lax.psum(early_grad, "dp")
    dy, middle_o = after(dy, middle_o)
    branch_parts = (keep_o, got_o, swap(middle_o, "tensor", 2))

    pair_shape = (2, own_states, tokens)
    sums_shapes = [
        (half, channels), (3, 8, channels), (8, channels), (8, lanes), (features, channels),
        (features, lanes),
    ]
    carried = [jnp.zeros(shape, F32) for shape in sums_shapes]
    carried[2] = jnp.pad(out_gain_grad, ((6, 1), (0, 0)))
    filled = []
    parts_of_scan = 2 if blocks % 2 == 0 else 1
    for section in range(parts_of_scan):
        count = blocks // parts_of_scan
        top = blocks - 1 - section * count
        back_from = lambda i, top=top: top - i
        got_all = call(
            backward_kernel,
            count,
            [
                (me, SCALAR),
                (pairs, rows(states, back_from)),
                (inner_c, rows(channels, back_from)),
                (inner_v, rows(channels, back_from)),
                (raw, rows(lanes, back_from)),
                (dy, rows(channels, back_from)),
                (entering, slab((half, channels), back_from)),
                (aux, rows(8, back_from)),
                (seg_rows, slab((1, BLOCK), back_from)),
                (carry_mask, slab((1, lanes), back_from)),
                (inner_taps, whole((4, channels))),
                (bias_row, whole((1, lanes))),
                (rate_row, whole((1, lanes))),
                (skip_row, whole((1, channels))),
                (normed, flat(features, back_from)),
                *[(array, whole(array.shape)) for array in carried],
            ],
            [
                ((tokens, channels), LOW, rows(channels, back_from)),
                (pair_shape, LOW, packed(2, own_states, back_from)),
                (pair_shape, LOW, packed(2, own_states, back_from)),
                ((tokens, lanes), LOW, rows(lanes, back_from)),
                *[(shape, F32, whole(shape)) for shape in sums_shapes],
            ],
            [pltpu.VMEM((half, channels), F32), pltpu.VMEM((3, 8, channels), F32)],
            1,
            list(enumerate(filled)),
        )
        if section == 0 and by_steps:
            *got_all, kept, given = after(*got_all, *early)
            early = [kept, given]
            early_grad = add_low(*early)
            early = list(split_half(early_grad, "dp", bits[1]))
        filled, carried = got_all[:4], got_all[4:]
    got_branch, *held = after(branch_parts[2], *filled, *carried, *early)
    branch_parts = (*branch_parts[:2], got_branch)
    inner_low, keep_p, give_p, steps_low, _, _, row_grads, head_grads, inner_w_grad, step_w_grad = held[:10]
    early = held[10:]
    keep_p, got_p, middle_p = scatter_sum(keep_p, give_p)
    inner_w_grad = inner_w_grad.astype(LOW)
    late_i = []
    if by_steps:
        early_grad = add_low(*early)
        early = list(split_half(early_grad, "dp", bits[2]))
        late_i = list(split_half(inner_w_grad, "dp", bits[0]))
    else:
        inner_w_grad = lax.psum(inner_w_grad, "dp")
    inner_low, middle_p = after(inner_low, middle_p)
    pair_parts = (keep_p, got_p, swap(middle_p, "tensor", 2))

    local = call(
        return_kernel,
        tokens // wide,
        [
            (gate_low, rows(channels, ahead, wide)),
            (inner_low, rows(channels, ahead, wide)),
            (steps_low, rows(lanes, ahead, wide)),
            (gate_weight, weight_spec),
            (inner_weight, weight_spec),
            (step_w, whole((features, lanes))),
        ],
        [
            ((features, tokens), F32, flat(features, ahead, wide)),
        ],
        [],
        1,
    )[0]

    if by_steps:
        local, *moved = after(local, *early, *late_i)
        early_grad = add_low(*moved[:2])
        for bit in bits[3:]:
            early_grad = add_low(*split_half(early_grad, "dp", bit))
        for bit in reversed(bits[3:]):
            early_grad = join_half(early_grad, "dp", bit)
        early_got = swap(early_grad, "dp", bits[2])
        inner_w_grad = add_low(*moved[2:])
        late_i = list(split_half(inner_w_grad, "dp", bits[1]))
    own_start = tensor_index * own_states
    own_taps = lax.dynamic_slice_in_dim(state_taps, own_start, own_states, 1)
    own_state_w = lax.dynamic_slice_in_dim(state_weight, own_start, own_states, 1)
    keep_n, give_n, row_dot, late = call(
        state_kernel,
        tokens // wide,
        [
            (me, SCALAR),
            (pair_parts[0], packed(1, own_states, behind_wide, wide)),
            (pair_parts[1], packed(1, own_states, behind_wide, wide)),
            (pair_parts[2], flat(own_states, behind_wide, wide)),
            (state_c, rows(states, behind_wide, wide)),
            (state_v, rows(states, behind_wide, wide)),
            (normed, flat(features, behind_wide, wide)),
            (local, flat(features, behind_wide, wide)),
            (aux, rows(8, behind_wide, wide)),
            (own_taps, whole((4, own_states))),
            (own_state_w, whole((features, own_states))),
            (step_w_grad, whole((features, lanes))),
            (row_grads, whole((8, channels))),
            (head_grads, whole((8, lanes))),
        ],
        [
            (piece_shape, LOW, packed(2, part, behind_wide, wide)),
            (piece_shape, LOW, packed(2, part, behind_wide, wide)),
            ((tokens // wide, 1, wide), F32, slab((1, wide), behind_wide)),
            ((own_states + 32, features), LOW, whole((own_states + 32, features))),
        ],
        [
            pltpu.VMEM((3, 8, own_states), F32),
            pltpu.VMEM((features, own_states), F32),
            pltpu.VMEM((features, lanes), F32),
            pltpu.VMEM((8, own_states), F32),
        ],
        1,
    )
    if by_steps:
        early_got, *late_i, keep_n, give_n, row_dot, late = after(
            early_got, *late_i, keep_n, give_n, row_dot, late
        )
        early_grad = place_half(early_grad, early_got, "dp", bits[2])
        inner_w_grad = add_low(*late_i)
    keep_n, got_n, middle_n = scatter_sum(keep_n, give_n)
    crossed_dot = swap(row_dot, "tensor", 2)
    row_dot, crossed_dot, middle_n = after(row_dot, crossed_dot, middle_n)
    row_dot = row_dot + crossed_dot
    late, middle_n = after(late, middle_n)
    grad_parts = (keep_n, got_n, swap(middle_n, "tensor", 2))
    row_dot = row_dot + swap(row_dot, "tensor", 1)
    if by_steps:
        early_grad, inner_w_grad, middle_n = after(early_grad, inner_w_grad, middle_n)
        for bit in bits[2:]:
            inner_w_grad = add_low(*split_half(inner_w_grad, "dp", bit))
        for bit in reversed(bits[:2]):
            early_grad = join_half(early_grad, "dp", bit)
        for bit in reversed(bits):
            inner_w_grad = join_half(inner_w_grad, "dp", bit)
    out_w_grad = early_grad[:features].T.astype(F32)
    gate_w_grad = early_grad[features:].astype(F32)

    def total_of(parts):
        keep, got, last = parts
        return keep[0].astype(F32) + got[0].astype(F32) + last.astype(F32)

    own_gain = lax.dynamic_slice_in_dim(norm_gain, tensor_index * part, part, 0)
    hidden_again, late = after(own_hidden, late)
    output = (hidden_again.astype(F32) + total_of(branch_parts)).astype(LOW).T
    if by_steps:
        late = add_low(late, swap(late, "dp", bits[0]))
        output, late = after(output, late)
        late = add_low(late, swap(late, "dp", bits[1]))
        out_w_grad, gate_w_grad, late = after(out_w_grad, gate_w_grad, late)
        for bit in bits[2:]:
            late = add_low(late, swap(late, "dp", bit))
    else:
        late = lax.psum(late, "dp")
    factor = scale.reshape(1, tokens)
    shrink = factor * factor * row_dot.reshape(1, tokens) / features
    input_grad = (
        own_upstream.astype(F32)
        + factor * (total_of(grad_parts) * own_gain[:, None])
        - own_hidden.astype(F32) * shrink
    ).T
    input_grad, late = after(input_grad, late)

    top = own_states + 16
    members = gather_pieces(late[:top])
    row_384 = ((1, channels), F32, whole((1, channels)))
    row_lanes = ((8, lanes), F32, whole((8, lanes)))
    step_grad, taps_grad, offset_grad, out_gain_grad, skip_grad, head_grads = call(
        lists_kernel,
        1,
        [(late[top:], whole((16, features)))],
        [
            ((features, lanes), F32, whole((features, lanes))),
            ((4, channels), F32, whole((4, channels))),
            row_384,
            row_384,
            row_lanes,
            row_lanes,
        ],
        [],
        1,
    )
    state_w_grad, state_rows, norm_gain_grad = call(
        state_grads_kernel,
        1,
        [
            (me, SCALAR),
            *[(member, whole(member.shape)) for member in members],
            (norm_gain[None], whole((1, features))),
        ],
        [
            ((features, states), F32, whole((features, states))),
            ((4, 1, features), F32, whole((4, 1, features))),
            ((1, features), F32, whole((1, features))),
        ],
        [pltpu.VMEM((4, own_states, features), F32)],
        1,
    )
    state_rows = state_rows[:, 0, : 5 * own_states].reshape(4, 5, own_states)
    state_rows = state_rows.transpose(1, 0, 2).reshape(5, states)

    return (
        output[None],
        input_grad[None],
        norm_gain_grad[0],
        gate_w_grad,
        inner_w_grad.astype(F32),
        state_w_grad,
        step_grad[:, :heads],
        taps_grad,
        offset_grad[0],
        state_rows[:4],
        state_rows[4],
        head_grads[0, :heads],
        head_grads[1, :heads],
        skip_grad[5, :heads],
        out_gain_grad[0],
        out_w_grad,
    )


def solution(mesh):
    rows_spec = P("dp", None, "tensor")
    columns_spec = P(None, "tensor")
    in_specs = (
        rows_spec, P("dp", None), P(), columns_spec, columns_spec, P(), columns_spec, columns_spec,
        P("tensor"), P(), P(), P("tensor"), P("tensor"), P("tensor"), P("tensor"),
        P("tensor", None), rows_spec,
    )
    out_specs = (
        rows_spec, rows_spec, P(), columns_spec, columns_spec, P(), columns_spec, columns_spec,
        P("tensor"), P(), P(), P("tensor"), P("tensor"), P("tensor"), P("tensor"),
        P("tensor", None),
    )
    return jax.shard_map(body, mesh=mesh, in_specs=in_specs, out_specs=out_specs, check_vma=False)
```

```python
import functools

import jax
import jax.numpy as jnp
from jax import lax
from jax.experimental import pallas as pl
from jax.experimental.pallas import tpu as pltpu
from jax.sharding import PartitionSpec as P

BLOCK = 256
EPSILON = 1e-05
HEAD = 64
F32 = jnp.float32
LOW = jnp.bfloat16
VMEM_BYTES = 48 * 1024 * 1024


def mm(left, right):
    return jnp.dot(left, right, preferred_element_type=F32)


def mm_nt(left, right):
    return lax.dot_general(left, right, (((1,), (1,)), ((), ())), preferred_element_type=F32)


def mm_tn(left, right):
    return lax.dot_general(left, right, (((0,), (0,)), ((), ())), preferred_element_type=F32)


def iota(shape, axis):
    return lax.broadcasted_iota(jnp.int32, shape, axis)


def sigmoid(values):
    return 0.5 * jnp.tanh(0.5 * values) + 0.5


def softplus(values):
    return jnp.maximum(values, 0.0) + jnp.log1p(jnp.exp(-jnp.abs(values)))


GROUP = 8


def split_lanes(columns, count):
    rest = jnp.where(iota(columns.shape, 1) < GROUP, columns, 0.0)
    total = jnp.zeros_like(rest)
    for at in range(count):
        high = rest.astype(LOW).astype(F32)
        total = total + (pltpu.roll(high, at * GROUP, 1) if at else high)
        rest = rest - high
    return total.astype(LOW)


def expand(many, width):
    lanes = many[0].shape[1]
    packed_lanes = jnp.concatenate([split_lanes(columns, 2) for columns in many], axis=0)
    row, head = iota((lanes, width), 0), iota((lanes, width), 1) // HEAD
    wide = mm(packed_lanes, ((row == head) | (row == head + GROUP)).astype(LOW))
    ends = [0]
    for columns in many:
        ends.append(ends[-1] + columns.shape[0])
    return [wide[a:b] for a, b in zip(ends, ends[1:])]


def expand_row(row, width):
    return expand([jnp.broadcast_to(row, (8, row.shape[1]))], width)[0][0:1]


def running_sum(mask, columns):
    wide = mm(mask.astype(LOW), split_lanes(columns, 3))
    lanes = columns.shape[1]
    total = wide + pltpu.roll(wide, lanes - GROUP, 1) + pltpu.roll(wide, lanes - 2 * GROUP, 1)
    return jnp.where(iota(total.shape, 1) < GROUP, total, 0.0)


def collapse(values, lanes):
    width = values.shape[1]
    pick = (iota((width, lanes), 0) // HEAD == iota((width, lanes), 1)).astype(LOW)
    high = values.astype(LOW)
    rest = (values - high.astype(F32)).astype(LOW)
    return mm(high, pick) + mm(rest, pick)


def join_pieces(me, pieces, joined):
    for relative, piece in enumerate(pieces):
        joined[pl.ds(me ^ relative, 1)] = piece[...][None]
    return joined[...].reshape(joined.shape[0] * joined.shape[1], joined.shape[2])


def store_pieces(me, values, keep_ref, give_ref):
    width = values.shape[0] // 4
    for dest in range(4):
        piece = values[dest * width : (dest + 1) * width].astype(LOW)[None]
        relative = me ^ dest

        @pl.when((relative & 1) == 0)
        def _():
            keep_ref[pl.ds(relative >> 1, 1)] = piece

        @pl.when((relative & 1) == 1)
        def _():
            give_ref[pl.ds(relative >> 1, 1)] = piece


def block_conv(ext, values, taps, offset, aux):
    rows = values.shape[0]
    total = offset + taps[3:4] * values
    for back in range(1, 4):
        total = total + taps[3 - back : 4 - back] * (
            aux[:, back - 1 : back] * ext[8 - back : 8 - back + rows]
        )
    return total


def conv_back(dpre, carry_ref, taps, values, aux):
    rows = dpre.shape[0]
    grad = taps[3:4] * dpre
    taps_grads = [jnp.sum(values * dpre, axis=0, keepdims=True)]
    for back in range(1, 4):
        masked = dpre * aux[:, back - 1 : back]
        ext = jnp.concatenate([masked, carry_ref[back - 1]], axis=0)
        carry_ref[back - 1] = masked[0:8]
        shifted = ext[back : back + rows]
        grad = grad + taps[3 - back : 4 - back] * shifted
        taps_grads.insert(0, jnp.sum(values * shifted, axis=0, keepdims=True))
    return grad, taps_grads


def scan_parts(raw, step_bias, rate, aux, seg_row, flipped):
    length, lanes = raw.shape
    shifted = raw + step_bias
    step = softplus(shifted)
    log_decay = -step * rate
    down, right = iota((length, length), 0), iota((length, length), 1)
    cum = running_sum(down >= right, log_decay)
    causal = (down <= right) if flipped else (down >= right)
    allowed = causal & (aux[:, 5:6] == seg_row)
    last = cum[length - 1 : length]
    reach = jnp.exp(cum) * aux[:, 4:5]
    fade = jnp.exp(last - cum) * aux[:, 3:4]
    return shifted, step, log_decay, cum, allowed, last, reach, fade


def forward_kernel(
    me_ref, x0, x1, x2, x3, gain, gate_w, inner_w, state_w, step_w, taps_i, off_i, taps_s, off_s,
    step_bias, rate, skip, aux_ref, seg_row, carry_mask, run_in, ci_in, cs_in,
    normed_out, gate_out, inner_v, inner_c, state_v, state_c, pairs_out, raw_out, y_out, enter_out,
    scale_out, run_out, ci_out, cs_out,
    run, carry_i, carry_s, joined,
):
    at = pl.program_id(0)

    @pl.when(at == 0)
    def _():
        run[...] = run_in[...]
        carry_i[...] = ci_in[...]
        carry_s[...] = cs_in[...]

    aux = aux_ref[...]
    rows = join_pieces(me_ref[0], (x0, x1, x2, x3), joined).astype(F32)
    factor = lax.rsqrt(jnp.mean(rows * rows, axis=0, keepdims=True) + EPSILON)
    normed_t = (rows * factor * gain[...]).astype(LOW)
    normed_out[...] = normed_t
    scale_out[0] = factor
    normed = normed_t.T
    gate_out[...] = mm(normed, gate_w[...])
    inner = mm(normed, inner_w[...])
    state = mm(normed, state_w[...])
    raw = mm(normed, step_w[...])
    raw_out[...] = raw
    inner_v[...] = inner.astype(LOW)
    state_v[...] = state.astype(LOW)
    inner_pre = block_conv(
        jnp.concatenate([carry_i[...], inner], axis=0), inner, taps_i[...], off_i[...], aux
    )
    state_pre = block_conv(
        jnp.concatenate([carry_s[...], state], axis=0), state, taps_s[...], off_s[...], aux
    )
    carry_i[...] = inner[-8:]
    carry_s[...] = state[-8:]
    inner_c[...] = inner_pre
    state_c[...] = state_pre
    active = (inner_pre * sigmoid(inner_pre)).astype(LOW)
    pairs = (state_pre * sigmoid(state_pre)).astype(LOW)
    pairs_out[...] = pairs
    half = pairs.shape[1] // 2
    write, read = pairs[:, :half], pairs[:, half:]
    shifted, step, log_decay, cum, allowed, last, reach, fade = scan_parts(
        raw, step_bias[...], rate[...], aux, seg_row[0], False
    )
    cum_t = cum.T
    scores = mm_nt(read, write)
    width = active.shape[1]
    active_wide = active.astype(F32)
    step_wide, reach_wide, fade_wide = expand([step, reach, fade], width)
    scaled = (step_wide * active_wide).astype(LOW)
    first = iota((1, 2 * HEAD), 1) < HEAD
    parts = []
    for pair in range(width // (2 * HEAD)):
        values = scaled[:, pair * 2 * HEAD : (pair + 1) * 2 * HEAD]
        got = []
        for head in (2 * pair, 2 * pair + 1):
            spread = cum[:, head : head + 1] - cum_t[head : head + 1]
            decays = jnp.exp(jnp.where(allowed, spread, -1e30))
            got.append(mm((decays * scores).astype(LOW), values))
        parts.append(jnp.where(first, got[0], got[1]))
    within = jnp.concatenate(parts, axis=1)
    entering = run[...]
    entering_low = entering.astype(LOW)
    enter_out[0] = entering_low
    across = mm(read, entering_low) * reach_wide
    y_out[...] = within + across + skip[...] * active_wide
    fresh = mm_tn(write, (fade_wide * step_wide * active_wide).astype(LOW))
    run[...] = expand_row(jnp.exp(last) * carry_mask[0], width) * entering + fresh

    @pl.when(at == pl.num_programs(0) - 1)
    def _():
        run_out[...] = run[...]
        ci_out[...] = carry_i[...]
        cs_out[...] = carry_s[...]


def sums_kernel(
    me_ref, u0, u1, u2, u3, gate, y, out_w_t, out_gain, up_out, grad_out, sums_out, joined
):
    upstream_t = join_pieces(me_ref[0], (u0, u1, u2, u3), joined)
    up_out[...] = upstream_t
    z = gate[...]
    gated = y[...] * (z * sigmoid(z))
    normal_grad = mm(upstream_t.T, out_w_t[...])
    grad_out[...] = normal_grad
    square = jnp.sum(gated * gated, axis=1, keepdims=True)
    cross = jnp.sum(normal_grad * out_gain[...] * gated, axis=1, keepdims=True)
    lane = iota((gated.shape[0], 128), 1)
    sums_out[0] = jnp.where(lane == 0, square, cross).T[0:2]


def output_kernel(
    full_width, me_ref, sums, upstream_t, gate, y_ref, grad_ref, normed_t, out_w_t, out_gain,
    keep, give, kept_grad, given_grad, out_gain_grad, gate_low, dy_out, total_o, total_g,
):
    at = pl.program_id(0)

    @pl.when(at == 0)
    def _():
        total_o[...] = jnp.zeros_like(total_o)
        total_g[...] = jnp.zeros_like(total_g)
        out_gain_grad[...] = jnp.zeros_like(out_gain_grad)

    pair = jnp.concatenate([sums[0], jnp.zeros((126, sums.shape[2]), F32)], axis=0).T
    square, cross = pair[:, 0:1], pair[:, 1:2]
    z, y = gate[...], y_ref[...]
    sig = sigmoid(z)
    swish = z * sig
    gated = y * swish
    scale = lax.rsqrt(square / full_width + EPSILON)
    gated_normed = (gated * scale * out_gain[...]).astype(LOW)
    store_pieces(me_ref[0], mm_nt(out_w_t[...], gated_normed), keep, give)
    total_o[...] += mm(upstream_t[...], gated_normed)
    normal_grad = grad_ref[...]
    out_gain_grad[...] += jnp.sum(normal_grad * gated * scale, axis=0, keepdims=True)
    weighted = normal_grad * out_gain[...]
    gated_grad = scale * weighted - gated * (scale * scale * scale * (cross / full_width))
    dy_out[...] = gated_grad * swish
    low = (gated_grad * y * (sig * (1.0 + z * (1.0 - sig)))).astype(LOW)
    gate_low[...] = low
    total_g[...] += mm(normed_t[...], low)

    @pl.when(at == pl.num_programs(0) - 1)
    def _():
        upper = me_ref[1] == 1
        kept_grad[...] = jnp.where(upper, total_g[...], total_o[...]).astype(LOW)
        given_grad[...] = jnp.where(upper, total_o[...], total_g[...]).astype(LOW)


def backward_kernel(
    carried, me_ref, pairs_ref, inner_c, inner_v, raw_ref, dy_ref, enter_ref, aux_ref, seg_row,
    carry_mask, taps_i, step_bias, rate, skip, normed_t, rows_in, *refs,
):
    starts = refs[:carried]
    (
        inner_low, keep, give, steps_low, state_out, carry_out, heads_out, inner_out, steps_out,
        rows_out, inner_sum, back, carry_z,
    ) = refs[carried:]
    at = pl.program_id(0)

    @pl.when(at == 0)
    def _():
        rows_out[...] = rows_in[...]
        targets = (back, carry_z, heads_out, inner_out, steps_out)
        for target, start in zip(targets, starts or targets):
            target[...] = start[...] if starts else jnp.zeros_like(target)

    aux = aux_ref[...]
    pre = inner_c[...]
    sig = sigmoid(pre)
    active = (pre * sig).astype(LOW)
    active_wide = active.astype(F32)
    width = active.shape[1]
    pairs = pairs_ref[...]
    half = pairs.shape[1] // 2
    write, read = pairs[:, :half], pairs[:, half:]
    shifted, step, log_decay, cum, allowed, last, reach, fade = scan_parts(
        raw_ref[...], step_bias[...], rate[...], aux, seg_row[0], True
    )
    length, lanes = cum.shape
    cum_t = cum.T
    scores_t = mm_nt(write, read)
    dy = dy_ref[...]
    dy_low = dy.astype(LOW)
    entering_low = enter_ref[0]
    step_wide, reach_wide, fade_wide = expand([step, reach, fade], width)
    toward_wide = fade_wide * step_wide
    scaled = (step_wide * active_wide).astype(LOW)
    dy_reach = dy * reach_wide
    dy_reach_low = dy_reach.astype(LOW)
    from_state = mm(read, entering_low)
    dcum = collapse(dy_reach * from_state, lanes)
    dread = mm_nt(dy_reach_low, entering_low)
    dentering = mm_tn(read, dy_reach_low)
    grad_state = back[...]
    grad_low = grad_state.astype(LOW)
    from_grad = mm(write, grad_low)
    dwrite = mm_nt((toward_wide * active_wide).astype(LOW), grad_low)
    dtoward = collapse(active_wide * from_grad, lanes)
    dfade = dtoward * (fade * step)
    dcum = dcum - dfade
    dstep = dtoward * fade
    keep_factor = jnp.exp(last) * carry_mask[0]
    kept = jnp.sum(grad_state * entering_low.astype(F32), axis=0, keepdims=True)
    kept = collapse(jnp.broadcast_to(kept, (8, width)), lanes)[0:1]
    dlast = jnp.sum(dfade, axis=0, keepdims=True) + keep_factor * kept
    back[...] = expand_row(keep_factor, width) * grad_state + dentering

    first = iota((1, 2 * HEAD), 1) < HEAD
    lane = iota((length, lanes), 1)
    dscores = jnp.zeros((length, length), F32)
    source_sums = jnp.zeros((length, lanes), F32)
    target_sums = []
    parts = []
    for pair in range(width // (2 * HEAD)):
        values = scaled[:, pair * 2 * HEAD : (pair + 1) * 2 * HEAD]
        grads = dy_low[:, pair * 2 * HEAD : (pair + 1) * 2 * HEAD]
        got = []
        for head in (2 * pair, 2 * pair + 1):
            own = jnp.where(first == (head % 2 == 0), grads, jnp.zeros_like(grads))
            spread = cum_t[head : head + 1] - cum[:, head : head + 1]
            decays = jnp.exp(jnp.where(allowed, spread, -1e30))
            graded = mm_nt(values, own) * decays
            dscores = dscores + graded
            scored = graded * scores_t
            source = jnp.sum(scored, axis=1, keepdims=True)
            source_sums = jnp.where(lane == head, source, source_sums)
            target_sums.append(jnp.sum(scored, axis=0, keepdims=True))
            got.append(mm((decays * scores_t).astype(LOW), grads))
        parts.append(jnp.where(first, got[0], got[1]))
    target_sums.append(jnp.zeros((lanes - len(target_sums), length), F32))
    target_sums = jnp.concatenate(target_sums, axis=0).T
    dscores_low = dscores.astype(LOW)
    dread = dread + mm_tn(dscores_low, write)
    dwrite = dwrite + mm(dscores_low, read)
    dstep = dstep + source_sums / jnp.maximum(step, 1e-30)
    dcum = dcum + target_sums - source_sums
    dcum = dcum + jnp.where(iota((length, 1), 0) == length - 1, dlast, 0.0)
    dlog = running_sum(iota((length, length), 0) <= iota((length, length), 1), dcum)
    dstep = dstep - dlog * rate[...]
    draw = dstep * sigmoid(shifted)
    draw_low = draw.astype(LOW)
    steps_low[...] = draw_low
    heads_out[0:1] += jnp.sum(draw, axis=0, keepdims=True)
    heads_out[1:2] += jnp.sum(dlog * log_decay, axis=0, keepdims=True)

    dactive = step_wide * jnp.concatenate(parts, axis=1) + skip[...] * dy + toward_wide * from_grad
    dpre = dactive * (sig * (1.0 + pre * (1.0 - sig)))
    grad, taps_grads = conv_back(dpre, carry_z, taps_i[...], inner_v[...].astype(F32), aux)
    low = grad.astype(LOW)
    inner_low[...] = low
    inner_out[...] += mm(normed_t[...], low)
    steps_out[...] += mm(normed_t[...], draw_low)
    for tap in range(4):
        rows_out[tap : tap + 1] += taps_grads[tap]
    rows_out[4:5] += jnp.sum(dpre, axis=0, keepdims=True)
    rows_out[5:6] += jnp.sum(dy * active_wide, axis=0, keepdims=True)
    store_pieces(me_ref[0], jnp.concatenate([dwrite, dread], axis=1).T, keep, give)

    @pl.when(at == pl.num_programs(0) - 1)
    def _():
        inner_sum[...] = inner_out[...].astype(LOW)
        state_out[...] = back[...]
        carry_out[...] = carry_z[...]


def return_kernel(gate_low, inner_low, steps_low, gate_w, inner_w, step_w, local):
    local[...] = (
        mm_nt(gate_w[...], gate_low[...])
        + mm_nt(inner_w[...], inner_low[...])
        + mm_nt(step_w[...], steps_low[...])
    )


def state_kernel(
    me_ref, part_a, part_b, part_c, state_c, state_v, normed_ref, local_ref, aux_ref, taps, state_w,
    steps_in, rows_in, heads_in,
    keep, give, row_dot, late, carry_z, total, gain_total, rows_out,
):
    at = pl.program_id(0)
    me = me_ref[0]

    @pl.when(at == 0)
    def _():
        carry_z[...] = jnp.zeros_like(carry_z)
        total[...] = jnp.zeros_like(total)
        rows_out[...] = jnp.zeros_like(rows_out)
        gain_total[...] = jnp.zeros_like(gain_total)

    def own(values):
        values = values.astype(F32)
        width = values.shape[1] // 4
        picked = jnp.where((me & 2) == 2, values[:, 2 * width :], values[:, : 2 * width])
        return jnp.where((me & 1) == 1, picked[:, width:], picked[:, :width])

    dpairs = (part_a[0].astype(F32) + part_b[0].astype(F32) + part_c[...].astype(F32)).T
    pre = own(state_c[...])
    sig = sigmoid(pre)
    dpre = dpairs * (sig * (1.0 + pre * (1.0 - sig)))
    grad, taps_grads = conv_back(dpre, carry_z, taps[...], own(state_v[...]), aux_ref[...])
    low = grad.astype(LOW)
    for tap in range(4):
        rows_out[tap : tap + 1] += taps_grads[tap]
    rows_out[4:5] += jnp.sum(dpre, axis=0, keepdims=True)
    normed_t = normed_ref[...]
    total[...] += mm(normed_t, low)
    values = local_ref[...] + mm_nt(state_w[...], low)
    store_pieces(me, values, keep, give)
    product = values * normed_t.astype(F32)
    row_dot[0] = jnp.sum(product, axis=0, keepdims=True)
    gain_total[...] += sum(
        product[:, at : at + 128] for at in range(0, product.shape[1], 128)
    )

    @pl.when(at == pl.num_programs(0) - 1)
    def _():
        states, channels, heads = total.shape[1], rows_in.shape[1], heads_in.shape[1]
        width = total.shape[0]
        column = jnp.sum(gain_total[...], axis=1, keepdims=True)
        taps_row = [rows_out[row : row + 1] for row in range(5)]
        taps_row = jnp.concatenate([*taps_row, jnp.zeros((1, width - 5 * states), F32)], axis=1)
        lists = jnp.concatenate(
            [rows_in[...], heads_in[...], jnp.zeros((8, width - channels - heads), F32)], axis=1
        )
        late[...] = jnp.concatenate(
            [
                total[...].T,
                taps_row,
                jnp.broadcast_to(column, gain_total.shape).T[0:1],
                jnp.zeros((14, width), F32),
                steps_in[...].T[0:8],
                lists,
            ],
            axis=0,
        ).astype(LOW)


def lists_kernel(own, step_grad, taps_grad, offset_grad, out_gain_grad, skip_grad, head_grads):
    channels = taps_grad.shape[1]
    values = own[...].astype(F32)
    steps = values[0:8]
    step_grad[...] = jnp.concatenate([steps, jnp.zeros((120, steps.shape[1]), F32)], axis=0).T
    rows = values[8:16, 0:channels]
    taps_grad[...] = rows[0:4]
    offset_grad[...] = rows[4:5]
    out_gain_grad[...] = rows[6:7]
    skip_grad[...] = collapse(rows, 128)
    head_grads[...] = values[8:16, channels : channels + 128]


def state_grads_kernel(
    me_ref, m0, m1, m2, m3, gain, state_w_grad, taps_grad, offset_grad, gain_grad, gathered, rows
):
    states = gathered.shape[1]
    total = jnp.zeros(gain.shape, F32)
    for relative, member in enumerate((m0, m1, m2, m3)):
        dest = me_ref[0] ^ relative
        values = member[...].astype(F32)
        gathered[pl.ds(dest, 1)] = values[0:states][None]
        rows[pl.ds(dest, 1)] = values[states : states + 1][None]
        total = total + values[states + 1 : states + 2]
    state_w_grad[...] = gathered[...].reshape(4 * states, gain.shape[1]).T
    gain_grad[...] = total / gain[...]
    for tap in range(5):
        cut = slice(tap * states, (tap + 1) * states)
        row = jnp.concatenate([rows[dest][:, cut] for dest in range(4)], axis=1)
        if tap < 4:
            taps_grad[tap : tap + 1] = row
        else:
            offset_grad[...] = row


def weight_grads_kernel(
    me_ref, early_own, early_got, inner_own, inner_got, out_w_grad, gate_w_grad, inner_w_grad
):
    upper = me_ref[1] == 1
    own, got = early_own[...].astype(F32), early_got[...].astype(F32)
    out_w_grad[...] = jnp.where(upper, got, own).T
    gate_w_grad[...] = jnp.where(upper, own, got)
    own, got = inner_own[...].astype(F32), inner_got[...].astype(F32)
    half = own.shape[0]
    inner_w_grad[0:half] = jnp.where(upper, got, own)
    inner_w_grad[half:] = jnp.where(upper, own, got)


def rows(columns, index, size=BLOCK):
    return pl.BlockSpec((size, columns), lambda i: (index(i), 0))


def slab(shape, index):
    return pl.BlockSpec((1, *shape), lambda i: (index(i),) + (0,) * len(shape))


def whole(shape):
    return pl.BlockSpec(shape, lambda i: (0,) * len(shape))


def flat(features, index, size=BLOCK):
    return pl.BlockSpec((features, size), lambda i: (0, index(i)))


def packed(count, features, index, size=BLOCK):
    return pl.BlockSpec((count, features, size), lambda i: (0, 0, index(i)))


SCALAR = pl.BlockSpec(memory_space=pltpu.SMEM)


def call(kernel, blocks, ins, outs, scratch, flops, fill=()):
    count = len(ins)
    ins = [*ins, *((array, pl.BlockSpec(memory_space=pl.ANY)) for _, array in fill)]
    aliases = {count + at: out for at, (out, _) in enumerate(fill)}
    if fill:
        inner_kernel = kernel

        def kernel(*refs):
            return inner_kernel(*refs[:count], *refs[count + len(fill) :])

    arrays = [array for array, _ in ins]
    shapes = [jax.ShapeDtypeStruct(shape, dtype) for shape, dtype, _ in outs]
    return pl.pallas_call(
        kernel,
        grid=(blocks,),
        in_specs=[spec for _, spec in ins],
        out_specs=[spec for _, _, spec in outs],
        out_shape=shapes,
        scratch_shapes=scratch,
        input_output_aliases=aliases,
        compiler_params=pltpu.CompilerParams(
            dimension_semantics=("arbitrary",), vmem_limit_bytes=VMEM_BYTES
        ),
        cost_estimate=pl.CostEstimate(flops=flops, bytes_accessed=1, transcendentals=0),
    )(*arrays)


def swap(values, axis, bit):
    size = lax.axis_size(axis)
    return lax.ppermute(values, axis, [(i, i ^ bit) for i in range(size)])


def small_sum(values, axis):
    size = lax.axis_size(axis)
    if size & (size - 1):
        return lax.psum(values, axis)
    bit = 1
    while bit < size:
        values = values + swap(values, axis, bit)
        bit *= 2
    return values


def split_half(values, axis, bit):
    half = values.shape[0] // 2
    upper = (lax.axis_index(axis) & bit) // bit
    kept = lax.dynamic_slice_in_dim(values, upper * half, half, 0)
    given = lax.dynamic_slice_in_dim(values, (1 - upper) * half, half, 0)
    return kept, swap(given, axis, bit)


def join_half(values, axis, bit):
    return place_half(values, swap(values, axis, bit), axis, bit)


def place_half(values, got, axis, bit):
    upper = (lax.axis_index(axis) & bit) > 0
    return jnp.concatenate(
        [jnp.where(upper, got, values), jnp.where(upper, values, got)], axis=0
    )


def add_low(left, right):
    return (left.astype(F32) + right.astype(F32)).astype(LOW)


def axis_bits(axis):
    size = lax.axis_size(axis)
    return [] if size & (size - 1) else [1 << k for k in range(size.bit_length() - 1)]


def in_order(index, pieces):
    one, two = (index & 1) == 1, (index & 2) == 2
    a, b, c, d = pieces
    a, b, c, d = (
        jnp.where(one, b, a), jnp.where(one, a, b), jnp.where(one, d, c), jnp.where(one, c, d)
    )
    return (
        jnp.where(two, c, a), jnp.where(two, d, b), jnp.where(two, a, c), jnp.where(two, b, d)
    )


def gather_pieces(values):
    across = swap(values, "tensor", 2)
    return values, swap(values, "tensor", 1), across, swap(across, "tensor", 1)


def after(values, *earlier):
    return lax.optimization_barrier((values, *earlier))


def scatter_sum(keep, give):
    got = swap(give, "tensor", 1)
    middle = (keep[1].astype(F32) + got[1].astype(F32)).astype(LOW)
    return keep, got, middle


def body(
    hidden, segments, norm_gain, gate_weight, inner_weight, state_weight, step_weight, inner_taps,
    inner_offset, state_taps, state_offset, step_bias, decay_log, skip_weight, out_gain, out_weight,
    cotangent,
):
    tensor_index = lax.axis_index("tensor")
    me = jnp.stack([tensor_index, lax.axis_index("dp") & 1]).astype(jnp.int32)
    own_hidden, own_upstream, segment = hidden[0].T, cotangent[0].T, segments[0]
    part, tokens = own_hidden.shape
    features, channels = gate_weight.shape
    heads = step_weight.shape[1]
    states = state_weight.shape[1]
    half = states // 2
    own_states = states // 4
    blocks = tokens // BLOCK
    lanes = 128
    full_width = channels * lax.axis_size("tensor")
    ahead = lambda i: i
    behind = lambda i: blocks - 1 - i
    wide = 2 * BLOCK if tokens % (2 * BLOCK) == 0 else BLOCK
    behind_wide = lambda i: tokens // wide - 1 - i

    sections = 2 if blocks % 2 == 0 else 1
    cut = tokens // sections
    starts = [own_hidden[:, at * cut : (at + 1) * cut] for at in range(sections)]
    crossed = []
    for start in starts:
        if crossed:
            start, crossed[-1] = after(start, crossed[-1])
        crossed.append(swap(start, "tensor", 2))
    upstream_start, crossed[0] = after(own_upstream, crossed[0])
    upstream_across = swap(upstream_start, "tensor", 2)

    seg_blocks = segment.reshape(blocks, BLOCK)
    last_seg = seg_blocks[:, -1]
    previous = jnp.concatenate([jnp.full((1,), -1, jnp.int32), last_seg[:-1]])
    columns = []
    for back in range(1, 4):
        padded = jnp.pad(segment, (back, 0), constant_values=-1)[:tokens]
        columns.append(padded == segment)
    columns.append((seg_blocks == last_seg[:, None]).reshape(tokens))
    columns.append((seg_blocks == previous[:, None]).reshape(tokens))
    columns.append(segment)
    aux = jnp.stack([c.astype(F32) for c in columns] + [jnp.zeros((tokens,), F32)] * 2, axis=1)
    seg_rows = seg_blocks.astype(F32)[:, None, :]
    carry_mask = jnp.broadcast_to(
        (last_seg == previous).astype(F32)[:, None, None], (blocks, 1, lanes)
    )
    pad_heads = lambda v: jnp.pad(v, (0, lanes - heads))[None]
    step_w = jnp.pad(step_weight, ((0, 0), (0, lanes - heads)))
    bias_row = pad_heads(step_bias)
    rate_row = pad_heads(jnp.exp(decay_log))
    skip_row = jnp.repeat(skip_weight, HEAD)[None]
    gain_column = norm_gain[:, None]
    out_w_t = out_weight.T
    out_gain_row = out_gain[None]

    weight_spec = whole((features, channels))
    states_shapes = [(half, channels), (8, channels), (8, states)]
    carried = [jnp.zeros(shape, F32) for shape in states_shapes]
    filled = []
    for section in range(sections):
        count = blocks // sections
        onward = lambda i, base=section * count: base + i
        pieces = (
            starts[section],
            swap(starts[section], "tensor", 1),
            crossed[section],
            swap(crossed[section], "tensor", 1),
        )
        got_all = call(
            forward_kernel,
            count,
            [
                (me, SCALAR),
                *[(piece, flat(part, ahead)) for piece in pieces],
                (gain_column, whole((features, 1))),
                (gate_weight, weight_spec),
                (inner_weight, weight_spec),
                (state_weight, whole((features, states))),
                (step_w, whole((features, lanes))),
                (inner_taps, whole((4, channels))),
                (inner_offset[None], whole((1, channels))),
                (state_taps, whole((4, states))),
                (state_offset[None], whole((1, states))),
                (bias_row, whole((1, lanes))),
                (rate_row, whole((1, lanes))),
                (skip_row, whole((1, channels))),
                (aux, rows(8, onward)),
                (seg_rows, slab((1, BLOCK), onward)),
                (carry_mask, slab((1, lanes), onward)),
                *[(array, whole(array.shape)) for array in carried],
            ],
            [
                ((features, tokens), LOW, flat(features, onward)),
                ((tokens, channels), F32, rows(channels, onward)),
                ((tokens, channels), LOW, rows(channels, onward)),
                ((tokens, channels), F32, rows(channels, onward)),
                ((tokens, states), LOW, rows(states, onward)),
                ((tokens, states), F32, rows(states, onward)),
                ((tokens, states), LOW, rows(states, onward)),
                ((tokens, lanes), F32, rows(lanes, onward)),
                ((tokens, channels), F32, rows(channels, onward)),
                ((blocks, half, channels), LOW, slab((half, channels), onward)),
                ((blocks, 1, BLOCK), F32, slab((1, BLOCK), onward)),
                *[(shape, F32, whole(shape)) for shape in states_shapes],
            ],
            [
                *[pltpu.VMEM(shape, F32) for shape in states_shapes],
                pltpu.VMEM((4, part, BLOCK), LOW),
            ],
            1,
            list(enumerate(filled)),
        )
        if section + 1 < sections:
            crossed[section + 1], *got_all = after(crossed[section + 1], *got_all)
        filled, carried = got_all[:11], got_all[11:]
    normed, gate, inner_v, inner_c, state_v, state_c, pairs, raw, y, entering, scale = filled

    upstream_across, y = after(upstream_across, y)
    upstream_own, y = after(own_upstream, y)
    upstream_pieces = (
        own_upstream,
        swap(upstream_own, "tensor", 1),
        upstream_across,
        swap(upstream_across, "tensor", 1),
    )
    upstream, normal_grad, sums = call(
        sums_kernel,
        tokens // wide,
        [
            (me, SCALAR),
            *[(piece, flat(part, ahead, wide)) for piece in upstream_pieces],
            (gate, rows(channels, ahead, wide)),
            (y, rows(channels, ahead, wide)),
            (out_w_t, weight_spec),
            (out_gain_row, whole((1, channels))),
        ],
        [
            ((features, tokens), LOW, flat(features, ahead, wide)),
            ((tokens, channels), F32, rows(channels, ahead, wide)),
            ((tokens // wide, 2, wide), F32, slab((2, wide), ahead)),
        ],
        [pltpu.VMEM((4, part, wide), LOW)],
        1,
    )
    sums = small_sum(sums, "tensor")

    piece_shape = (2, part, tokens)
    keep_o, give_o, early_kept, early_given, out_gain_grad, gate_low, dy = call(
        functools.partial(output_kernel, full_width),
        tokens // wide,
        [
            (me, SCALAR),
            (sums, slab((2, wide), ahead)),
            (upstream, flat(features, ahead, wide)),
            (gate, rows(channels, ahead, wide)),
            (y, rows(channels, ahead, wide)),
            (normal_grad, rows(channels, ahead, wide)),
            (normed, flat(features, ahead, wide)),
            (out_w_t, weight_spec),
            (out_gain_row, whole((1, channels))),
        ],
        [
            (piece_shape, LOW, packed(2, part, ahead, wide)),
            (piece_shape, LOW, packed(2, part, ahead, wide)),
            ((features, channels), LOW, weight_spec),
            ((features, channels), LOW, weight_spec),
            ((1, channels), F32, whole((1, channels))),
            ((tokens, channels), LOW, rows(channels, ahead, wide)),
            ((tokens, channels), F32, rows(channels, ahead, wide)),
        ],
        [pltpu.VMEM((features, channels), F32)] * 2,
        1,
    )
    keep_o, got_o, middle_o = scatter_sum(keep_o, give_o)
    bits = axis_bits("dp")
    by_steps = len(bits) > 2 and features % (1 << len(bits)) == 0
    early = []
    if by_steps:
        early = [early_kept, swap(early_given, "dp", bits[0])]
    else:
        flipped = (lax.axis_index("dp") & 1) > 0
        early_grad = jnp.concatenate(
            [
                jnp.where(flipped, early_given, early_kept),
                jnp.where(flipped, early_kept, early_given),
            ],
            axis=0,
        )
        early_grad = lax.psum(early_grad, "dp")
    dy, middle_o = after(dy, middle_o)
    branch_parts = (keep_o, got_o, swap(middle_o, "tensor", 2))

    pair_shape = (2, own_states, tokens)
    sums_shapes = [
        (half, channels), (3, 8, channels), (8, lanes), (features, channels), (features, lanes),
    ]
    carried = []
    row_grads = jnp.pad(out_gain_grad, ((6, 1), (0, 0)))
    filled = []
    parts_of_scan = 2 if blocks % 2 == 0 else 1
    for section in range(parts_of_scan):
        count = blocks // parts_of_scan
        top = blocks - 1 - section * count
        back_from = lambda i, top=top: top - i
        got_all = call(
            functools.partial(backward_kernel, len(carried)),
            count,
            [
                (me, SCALAR),
                (pairs, rows(states, back_from)),
                (inner_c, rows(channels, back_from)),
                (inner_v, rows(channels, back_from)),
                (raw, rows(lanes, back_from)),
                (dy, rows(channels, back_from)),
                (entering, slab((half, channels), back_from)),
                (aux, rows(8, back_from)),
                (seg_rows, slab((1, BLOCK), back_from)),
                (carry_mask, slab((1, lanes), back_from)),
                (inner_taps, whole((4, channels))),
                (bias_row, whole((1, lanes))),
                (rate_row, whole((1, lanes))),
                (skip_row, whole((1, channels))),
                (normed, flat(features, back_from)),
                (row_grads, whole((8, channels))),
                *[(array, whole(array.shape)) for array in carried],
            ],
            [
                ((tokens, channels), LOW, rows(channels, back_from)),
                (pair_shape, LOW, packed(2, own_states, back_from)),
                (pair_shape, LOW, packed(2, own_states, back_from)),
                ((tokens, lanes), LOW, rows(lanes, back_from)),
                *[(shape, F32, whole(shape)) for shape in sums_shapes],
                ((8, channels), F32, whole((8, channels))),
                ((features, channels), LOW, weight_spec),
            ],
            [pltpu.VMEM((half, channels), F32), pltpu.VMEM((3, 8, channels), F32)],
            1,
            list(enumerate(filled)),
        )
        if section == 0 and by_steps:
            *got_all, kept, given = after(*got_all, *early)
            early = [kept, given]
            early_grad = add_low(*early)
            early = list(split_half(early_grad, "dp", bits[1]))
        filled, carried, row_grads, inner_w_grad = (
            got_all[:4], got_all[4:9], got_all[9], got_all[10]
        )
    got_branch, *held = after(branch_parts[2], *filled, *carried[2:], row_grads, inner_w_grad, *early)
    branch_parts = (*branch_parts[:2], got_branch)
    inner_low, keep_p, give_p, steps_low, head_grads, _, step_w_grad, row_grads, inner_w_grad = held[:9]
    early = held[9:]
    keep_p, got_p, middle_p = scatter_sum(keep_p, give_p)
    late_i = []
    if by_steps:
        early_grad = add_low(*early)
        early = list(split_half(early_grad, "dp", bits[2]))
        late_i = list(split_half(inner_w_grad, "dp", bits[0]))
    else:
        inner_w_grad = lax.psum(inner_w_grad, "dp")
    inner_low, middle_p = after(inner_low, middle_p)
    pair_parts = (keep_p, got_p, swap(middle_p, "tensor", 2))

    local = call(
        return_kernel,
        tokens // wide,
        [
            (gate_low, rows(channels, ahead, wide)),
            (inner_low, rows(channels, ahead, wide)),
            (steps_low, rows(lanes, ahead, wide)),
            (gate_weight, weight_spec),
            (inner_weight, weight_spec),
            (step_w, whole((features, lanes))),
        ],
        [
            ((features, tokens), F32, flat(features, ahead, wide)),
        ],
        [],
        1,
    )[0]

    if by_steps:
        local, *moved = after(local, *early, *late_i)
        early_grad = add_low(*moved[:2])
        for bit in bits[3:]:
            early_grad = add_low(*split_half(early_grad, "dp", bit))
        for bit in reversed(bits[3:]):
            early_grad = join_half(early_grad, "dp", bit)
        early_got = swap(early_grad, "dp", bits[2])
        inner_w_grad = add_low(*moved[2:])
        late_i = list(split_half(inner_w_grad, "dp", bits[1]))
    own_start = tensor_index * own_states
    own_taps = lax.dynamic_slice_in_dim(state_taps, own_start, own_states, 1)
    own_state_w = lax.dynamic_slice_in_dim(state_weight, own_start, own_states, 1)
    keep_n, give_n, row_dot, late = call(
        state_kernel,
        tokens // wide,
        [
            (me, SCALAR),
            (pair_parts[0], packed(1, own_states, behind_wide, wide)),
            (pair_parts[1], packed(1, own_states, behind_wide, wide)),
            (pair_parts[2], flat(own_states, behind_wide, wide)),
            (state_c, rows(states, behind_wide, wide)),
            (state_v, rows(states, behind_wide, wide)),
            (normed, flat(features, behind_wide, wide)),
            (local, flat(features, behind_wide, wide)),
            (aux, rows(8, behind_wide, wide)),
            (own_taps, whole((4, own_states))),
            (own_state_w, whole((features, own_states))),
            (step_w_grad, whole((features, lanes))),
            (row_grads, whole((8, channels))),
            (head_grads, whole((8, lanes))),
        ],
        [
            (piece_shape, LOW, packed(2, part, behind_wide, wide)),
            (piece_shape, LOW, packed(2, part, behind_wide, wide)),
            ((tokens // wide, 1, wide), F32, slab((1, wide), behind_wide)),
            ((own_states + 32, features), LOW, whole((own_states + 32, features))),
        ],
        [
            pltpu.VMEM((3, 8, own_states), F32),
            pltpu.VMEM((features, own_states), F32),
            pltpu.VMEM((features, lanes), F32),
            pltpu.VMEM((8, own_states), F32),
        ],
        1,
    )
    if by_steps:
        early_got, *late_i, keep_n, give_n, row_dot, late = after(
            early_got, *late_i, keep_n, give_n, row_dot, late
        )
        early_grad = place_half(early_grad, early_got, "dp", bits[2])
        early_got = swap(early_grad, "dp", bits[1])
        inner_w_grad = add_low(*late_i)
    keep_n, got_n, middle_n = scatter_sum(keep_n, give_n)
    crossed_dot = swap(row_dot, "tensor", 2)
    row_dot, crossed_dot, middle_n = after(row_dot, crossed_dot, middle_n)
    row_dot = row_dot + crossed_dot
    late, middle_n = after(late, middle_n)
    grad_parts = (keep_n, got_n, swap(middle_n, "tensor", 2))
    row_dot = row_dot + swap(row_dot, "tensor", 1)
    if by_steps:
        for bit in bits[2:]:
            inner_w_grad = add_low(*split_half(inner_w_grad, "dp", bit))
        inner_got = swap(inner_w_grad, "dp", bits[-1])

    def total_of(parts):
        keep, got, last = parts
        return keep[0].astype(F32) + got[0].astype(F32) + last.astype(F32)

    own_gain = lax.dynamic_slice_in_dim(norm_gain, tensor_index * part, part, 0)
    if by_steps:
        late_got = swap(late, "dp", bits[0])
        early_got, late_got = after(early_got, late_got)
        early_grad = place_half(early_grad, early_got, "dp", bits[1])
        early_grad, late_got, inner_got = after(early_grad, late_got, inner_got)
        early_got = swap(early_grad, "dp", bits[0])
        late = add_low(late, late_got)
        late_got = swap(late, "dp", bits[1])
        inner_w_grad = place_half(inner_w_grad, inner_got, "dp", bits[-1])
        for bit in reversed(bits[1:-1]):
            inner_w_grad = join_half(inner_w_grad, "dp", bit)
        inner_got = swap(inner_w_grad, "dp", bits[0])
        hidden_again, late_got = after(own_hidden, late_got)
        late = add_low(late, late_got)
    else:
        late = lax.psum(late, "dp")
        hidden_again = own_hidden
    output = (hidden_again.astype(F32) + total_of(branch_parts)).astype(LOW).T
    if by_steps:
        for bit in bits[2:]:
            late_got = swap(late, "dp", bit)
            output, late_got = after(output, late_got)
            late = add_low(late, late_got)
    factor = scale.reshape(1, tokens)
    shrink = factor * factor * row_dot.reshape(1, tokens) / features
    input_grad = (
        own_upstream.astype(F32)
        + factor * (total_of(grad_parts) * own_gain[:, None])
        - own_hidden.astype(F32) * shrink
    ).T
    top = own_states + 16
    members = list(gather_pieces(late[:top]))
    if by_steps:
        early_got, inner_got, members[2] = after(early_got, inner_got, members[2])
        out_w_grad, gate_w_grad, inner_w_grad = call(
            weight_grads_kernel,
            1,
            [
                (me, SCALAR),
                (early_grad, weight_spec),
                (early_got, weight_spec),
                (inner_w_grad, whole(inner_w_grad.shape)),
                (inner_got, whole(inner_got.shape)),
            ],
            [
                ((channels, features), F32, whole((channels, features))),
                ((features, channels), F32, weight_spec),
                ((features, channels), F32, weight_spec),
            ],
            [],
            1,
        )
    else:
        out_w_grad = early_grad[:features].T.astype(F32)
        gate_w_grad = early_grad[features:].astype(F32)
        inner_w_grad = inner_w_grad.astype(F32)
    input_grad, out_w_grad, *members = after(input_grad, out_w_grad, *members)
    row_384 = ((1, channels), F32, whole((1, channels)))
    row_lanes = ((8, lanes), F32, whole((8, lanes)))
    step_grad, taps_grad, offset_grad, out_gain_grad, skip_grad, head_grads = call(
        lists_kernel,
        1,
        [(late[top:], whole((16, features)))],
        [
            ((features, lanes), F32, whole((features, lanes))),
            ((4, channels), F32, whole((4, channels))),
            row_384,
            row_384,
            row_lanes,
            row_lanes,
        ],
        [],
        1,
    )
    state_w_grad, state_taps_grad, state_offset_grad, norm_gain_grad = call(
        state_grads_kernel,
        1,
        [
            (me, SCALAR),
            *[(member, whole(member.shape)) for member in members],
            (norm_gain[None], whole((1, features))),
        ],
        [
            ((features, states), F32, whole((features, states))),
            ((4, states), F32, whole((4, states))),
            ((1, states), F32, whole((1, states))),
            ((1, features), F32, whole((1, features))),
        ],
        [pltpu.VMEM((4, own_states, features), F32), pltpu.VMEM((4, 1, features), F32)],
        1,
    )

    return (
        output[None],
        input_grad[None],
        norm_gain_grad[0],
        gate_w_grad,
        inner_w_grad,
        state_w_grad,
        step_grad[:, :heads],
        taps_grad,
        offset_grad[0],
        state_taps_grad,
        state_offset_grad[0],
        head_grads[0, :heads],
        head_grads[1, :heads],
        skip_grad[5, :heads],
        out_gain_grad[0],
        out_w_grad,
    )


def solution(mesh):
    rows_spec = P("dp", None, "tensor")
    columns_spec = P(None, "tensor")
    in_specs = (
        rows_spec, P("dp", None), P(), columns_spec, columns_spec, P(), columns_spec, columns_spec,
        P("tensor"), P(), P(), P("tensor"), P("tensor"), P("tensor"), P("tensor"),
        P("tensor", None), rows_spec,
    )
    out_specs = (
        rows_spec, rows_spec, P(), columns_spec, columns_spec, P(), columns_spec, columns_spec,
        P("tensor"), P(), P(), P("tensor"), P("tensor"), P("tensor"), P("tensor"),
        P("tensor", None),
    )
    return jax.shard_map(body, mesh=mesh, in_specs=in_specs, out_specs=out_specs, check_vma=False)
```

```python
import functools

import jax
import jax.numpy as jnp
from jax import lax
from jax.experimental import pallas as pl
from jax.experimental.pallas import tpu as pltpu
from jax.sharding import PartitionSpec as P

BLOCK = 256
EPSILON = 1e-05
HEAD = 64
F32 = jnp.float32
LOW = jnp.bfloat16
VMEM_BYTES = 48 * 1024 * 1024


def mm(left, right):
    return jnp.dot(left, right, preferred_element_type=F32)


def mm_nt(left, right):
    return lax.dot_general(left, right, (((1,), (1,)), ((), ())), preferred_element_type=F32)


def mm_tn(left, right):
    return lax.dot_general(left, right, (((0,), (0,)), ((), ())), preferred_element_type=F32)


def iota(shape, axis):
    return lax.broadcasted_iota(jnp.int32, shape, axis)


def sigmoid(values):
    return 0.5 * jnp.tanh(0.5 * values) + 0.5


def softplus(values):
    return jnp.maximum(values, 0.0) + jnp.log1p(jnp.exp(-jnp.abs(values)))


GROUP = 8


def split_lanes(columns, count):
    rest = jnp.where(iota(columns.shape, 1) < GROUP, columns, 0.0)
    total = jnp.zeros_like(rest)
    for at in range(count):
        high = rest.astype(LOW).astype(F32)
        total = total + (pltpu.roll(high, at * GROUP, 1) if at else high)
        rest = rest - high
    return total.astype(LOW)


def expand(many, width):
    lanes = many[0].shape[1]
    packed_lanes = jnp.concatenate([split_lanes(columns, 2) for columns in many], axis=0)
    row, head = iota((lanes, width), 0), iota((lanes, width), 1) // HEAD
    wide = mm(packed_lanes, ((row == head) | (row == head + GROUP)).astype(LOW))
    ends = [0]
    for columns in many:
        ends.append(ends[-1] + columns.shape[0])
    return [wide[a:b] for a, b in zip(ends, ends[1:])]


def expand_row(row, width):
    return expand([jnp.broadcast_to(row, (8, row.shape[1]))], width)[0][0:1]


def running_sum(mask, columns):
    wide = mm(mask.astype(LOW), split_lanes(columns, 3))
    lanes = columns.shape[1]
    total = wide + pltpu.roll(wide, lanes - GROUP, 1) + pltpu.roll(wide, lanes - 2 * GROUP, 1)
    return jnp.where(iota(total.shape, 1) < GROUP, total, 0.0)


def collapse(values, lanes):
    width = values.shape[1]
    pick = (iota((width, lanes), 0) // HEAD == iota((width, lanes), 1)).astype(LOW)
    high = values.astype(LOW)
    rest = (values - high.astype(F32)).astype(LOW)
    return mm(high, pick) + mm(rest, pick)


def join_pieces(me, pieces, joined):
    for relative, piece in enumerate(pieces):
        joined[pl.ds(me ^ relative, 1)] = piece[...][None]
    return joined[...].reshape(joined.shape[0] * joined.shape[1], joined.shape[2])


def store_pieces(me, values, keep_ref, give_ref):
    width = values.shape[0] // 4
    for dest in range(4):
        piece = values[dest * width : (dest + 1) * width].astype(LOW)[None]
        relative = me ^ dest

        @pl.when((relative & 1) == 0)
        def _():
            keep_ref[pl.ds(relative >> 1, 1)] = piece

        @pl.when((relative & 1) == 1)
        def _():
            give_ref[pl.ds(relative >> 1, 1)] = piece


def block_conv(ext, values, taps, offset, aux):
    rows = values.shape[0]
    total = offset + taps[3:4] * values
    for back in range(1, 4):
        total = total + taps[3 - back : 4 - back] * (
            aux[:, back - 1 : back] * ext[8 - back : 8 - back + rows]
        )
    return total


def conv_back(dpre, carry_ref, taps, values, aux):
    rows = dpre.shape[0]
    grad = taps[3:4] * dpre
    taps_grads = [jnp.sum(values * dpre, axis=0, keepdims=True)]
    for back in range(1, 4):
        masked = dpre * aux[:, back - 1 : back]
        ext = jnp.concatenate([masked, carry_ref[back - 1]], axis=0)
        carry_ref[back - 1] = masked[0:8]
        shifted = ext[back : back + rows]
        grad = grad + taps[3 - back : 4 - back] * shifted
        taps_grads.insert(0, jnp.sum(values * shifted, axis=0, keepdims=True))
    return grad, taps_grads


def scan_parts(raw, step_bias, rate, aux, seg_row, flipped):
    length, lanes = raw.shape
    shifted = raw + step_bias
    step = softplus(shifted)
    log_decay = -step * rate
    down, right = iota((length, length), 0), iota((length, length), 1)
    cum = running_sum(down >= right, log_decay)
    causal = (down <= right) if flipped else (down >= right)
    allowed = causal & (aux[:, 5:6] == seg_row)
    last = cum[length - 1 : length]
    reach = jnp.exp(cum) * aux[:, 4:5]
    fade = jnp.exp(last - cum) * aux[:, 3:4]
    return shifted, step, log_decay, cum, allowed, last, reach, fade


def forward_kernel(
    me_ref, x0, x1, x2, x3, gain, gate_w, inner_w, state_w, step_w, taps_i, off_i, taps_s, off_s,
    step_bias, rate, skip, aux_ref, seg_row, carry_mask, run_in, ci_in, cs_in,
    normed_out, gate_out, inner_v, inner_c, state_v, state_c, pairs_out, raw_out, y_out, enter_out,
    scale_out, run_out, ci_out, cs_out,
    run, carry_i, carry_s, joined,
):
    at = pl.program_id(0)

    @pl.when(at == 0)
    def _():
        run[...] = run_in[...]
        carry_i[...] = ci_in[...]
        carry_s[...] = cs_in[...]

    aux = aux_ref[...]
    rows = join_pieces(me_ref[0], (x0, x1, x2, x3), joined).astype(F32)
    factor = lax.rsqrt(jnp.mean(rows * rows, axis=0, keepdims=True) + EPSILON)
    normed_t = (rows * factor * gain[...]).astype(LOW)
    normed_out[...] = normed_t
    scale_out[0] = factor
    normed = normed_t.T
    gate_out[...] = mm(normed, gate_w[...])
    inner = mm(normed, inner_w[...])
    state = mm(normed, state_w[...])
    raw = mm(normed, step_w[...])
    raw_out[...] = raw
    inner_v[...] = inner.astype(LOW)
    state_v[...] = state.astype(LOW)
    inner_pre = block_conv(
        jnp.concatenate([carry_i[...], inner], axis=0), inner, taps_i[...], off_i[...], aux
    )
    state_pre = block_conv(
        jnp.concatenate([carry_s[...], state], axis=0), state, taps_s[...], off_s[...], aux
    )
    carry_i[...] = inner[-8:]
    carry_s[...] = state[-8:]
    inner_c[...] = inner_pre
    state_c[...] = state_pre
    active = (inner_pre * sigmoid(inner_pre)).astype(LOW)
    pairs = (state_pre * sigmoid(state_pre)).astype(LOW)
    pairs_out[...] = pairs
    half = pairs.shape[1] // 2
    write, read = pairs[:, :half], pairs[:, half:]
    shifted, step, log_decay, cum, allowed, last, reach, fade = scan_parts(
        raw, step_bias[...], rate[...], aux, seg_row[0], False
    )
    cum_t = cum.T
    scores = mm_nt(read, write)
    width = active.shape[1]
    active_wide = active.astype(F32)
    step_wide, reach_wide, fade_wide = expand([step, reach, fade], width)
    scaled = (step_wide * active_wide).astype(LOW)
    first = iota((1, 2 * HEAD), 1) < HEAD
    parts = []
    for pair in range(width // (2 * HEAD)):
        values = scaled[:, pair * 2 * HEAD : (pair + 1) * 2 * HEAD]
        got = []
        for head in (2 * pair, 2 * pair + 1):
            spread = cum[:, head : head + 1] - cum_t[head : head + 1]
            decays = jnp.exp(jnp.where(allowed, spread, -1e30))
            got.append(mm((decays * scores).astype(LOW), values))
        parts.append(jnp.where(first, got[0], got[1]))
    within = jnp.concatenate(parts, axis=1)
    entering = run[...]
    entering_low = entering.astype(LOW)
    enter_out[0] = entering_low
    across = mm(read, entering_low) * reach_wide
    y_out[...] = within + across + skip[...] * active_wide
    fresh = mm_tn(write, (fade_wide * step_wide * active_wide).astype(LOW))
    run[...] = expand_row(jnp.exp(last) * carry_mask[0], width) * entering + fresh

    @pl.when(at == pl.num_programs(0) - 1)
    def _():
        run_out[...] = run[...]
        ci_out[...] = carry_i[...]
        cs_out[...] = carry_s[...]


def sums_kernel(
    me_ref, u0, u1, u2, u3, gate, y, out_w_t, out_gain, up_out, grad_out, sums_out, joined
):
    upstream_t = join_pieces(me_ref[0], (u0, u1, u2, u3), joined)
    up_out[...] = upstream_t
    z = gate[...]
    gated = y[...] * (z * sigmoid(z))
    normal_grad = mm(upstream_t.T, out_w_t[...])
    grad_out[...] = normal_grad
    square = jnp.sum(gated * gated, axis=1, keepdims=True)
    cross = jnp.sum(normal_grad * out_gain[...] * gated, axis=1, keepdims=True)
    lane = iota((gated.shape[0], 128), 1)
    sums_out[0] = jnp.where(lane == 0, square, cross).T[0:2]


def output_kernel(
    full_width, me_ref, sums, upstream_t, gate, y_ref, grad_ref, normed_t, out_w_t, out_gain,
    keep, give, kept_grad, given_grad, out_gain_grad, gate_low, dy_out, total_o, total_g,
):
    at = pl.program_id(0)

    @pl.when(at == 0)
    def _():
        total_o[...] = jnp.zeros_like(total_o)
        total_g[...] = jnp.zeros_like(total_g)
        out_gain_grad[...] = jnp.zeros_like(out_gain_grad)

    pair = jnp.concatenate([sums[0], jnp.zeros((126, sums.shape[2]), F32)], axis=0).T
    square, cross = pair[:, 0:1], pair[:, 1:2]
    z, y = gate[...], y_ref[...]
    sig = sigmoid(z)
    swish = z * sig
    gated = y * swish
    scale = lax.rsqrt(square / full_width + EPSILON)
    gated_normed = (gated * scale * out_gain[...]).astype(LOW)
    store_pieces(me_ref[0], mm_nt(out_w_t[...], gated_normed), keep, give)
    total_o[...] += mm(upstream_t[...], gated_normed)
    normal_grad = grad_ref[...]
    out_gain_grad[...] += jnp.sum(normal_grad * gated * scale, axis=0, keepdims=True)
    weighted = normal_grad * out_gain[...]
    gated_grad = scale * weighted - gated * (scale * scale * scale * (cross / full_width))
    dy_out[...] = gated_grad * swish
    low = (gated_grad * y * (sig * (1.0 + z * (1.0 - sig)))).astype(LOW)
    gate_low[...] = low
    total_g[...] += mm(normed_t[...], low)

    @pl.when(at == pl.num_programs(0) - 1)
    def _():
        upper = me_ref[1] == 1
        kept_grad[...] = jnp.where(upper, total_g[...], total_o[...]).astype(LOW)
        given_grad[...] = jnp.where(upper, total_o[...], total_g[...]).astype(LOW)


def backward_kernel(
    carried, me_ref, pairs_ref, inner_c, inner_v, raw_ref, dy_ref, enter_ref, aux_ref, seg_row,
    carry_mask, taps_i, step_bias, rate, skip, normed_t, rows_in, *refs,
):
    starts = refs[:carried]
    (
        inner_low, keep, give, steps_low, state_out, carry_out, heads_out, inner_out, steps_out,
        rows_out, inner_sum, back, carry_z,
    ) = refs[carried:]
    at = pl.program_id(0)

    @pl.when(at == 0)
    def _():
        rows_out[...] = rows_in[...]
        targets = (back, carry_z, heads_out, inner_out, steps_out)
        for target, start in zip(targets, starts or targets):
            target[...] = start[...] if starts else jnp.zeros_like(target)

    aux = aux_ref[...]
    pre = inner_c[...]
    sig = sigmoid(pre)
    active = (pre * sig).astype(LOW)
    active_wide = active.astype(F32)
    width = active.shape[1]
    pairs = pairs_ref[...]
    half = pairs.shape[1] // 2
    write, read = pairs[:, :half], pairs[:, half:]
    shifted, step, log_decay, cum, allowed, last, reach, fade = scan_parts(
        raw_ref[...], step_bias[...], rate[...], aux, seg_row[0], True
    )
    length, lanes = cum.shape
    cum_t = cum.T
    scores_t = mm_nt(write, read)
    dy = dy_ref[...]
    dy_low = dy.astype(LOW)
    entering_low = enter_ref[0]
    step_wide, reach_wide, fade_wide = expand([step, reach, fade], width)
    toward_wide = fade_wide * step_wide
    scaled = (step_wide * active_wide).astype(LOW)
    dy_reach = dy * reach_wide
    dy_reach_low = dy_reach.astype(LOW)
    from_state = mm(read, entering_low)
    dcum = collapse(dy_reach * from_state, lanes)
    dread = mm_nt(dy_reach_low, entering_low)
    dentering = mm_tn(read, dy_reach_low)
    grad_state = back[...]
    grad_low = grad_state.astype(LOW)
    from_grad = mm(write, grad_low)
    dwrite = mm_nt((toward_wide * active_wide).astype(LOW), grad_low)
    dtoward = collapse(active_wide * from_grad, lanes)
    dfade = dtoward * (fade * step)
    dcum = dcum - dfade
    dstep = dtoward * fade
    keep_factor = jnp.exp(last) * carry_mask[0]
    kept = jnp.sum(grad_state * entering_low.astype(F32), axis=0, keepdims=True)
    kept = collapse(jnp.broadcast_to(kept, (8, width)), lanes)[0:1]
    dlast = jnp.sum(dfade, axis=0, keepdims=True) + keep_factor * kept
    back[...] = expand_row(keep_factor, width) * grad_state + dentering

    first = iota((1, 2 * HEAD), 1) < HEAD
    lane = iota((length, lanes), 1)
    dscores = jnp.zeros((length, length), F32)
    source_sums = jnp.zeros((length, lanes), F32)
    target_sums = []
    parts = []
    for pair in range(width // (2 * HEAD)):
        values = scaled[:, pair * 2 * HEAD : (pair + 1) * 2 * HEAD]
        grads = dy_low[:, pair * 2 * HEAD : (pair + 1) * 2 * HEAD]
        got = []
        for head in (2 * pair, 2 * pair + 1):
            own = jnp.where(first == (head % 2 == 0), grads, jnp.zeros_like(grads))
            spread = cum_t[head : head + 1] - cum[:, head : head + 1]
            decays = jnp.exp(jnp.where(allowed, spread, -1e30))
            graded = mm_nt(values, own) * decays
            dscores = dscores + graded
            scored = graded * scores_t
            source = jnp.sum(scored, axis=1, keepdims=True)
            source_sums = jnp.where(lane == head, source, source_sums)
            target_sums.append(jnp.sum(scored, axis=0, keepdims=True))
            got.append(mm((decays * scores_t).astype(LOW), grads))
        parts.append(jnp.where(first, got[0], got[1]))
    target_sums.append(jnp.zeros((lanes - len(target_sums), length), F32))
    target_sums = jnp.concatenate(target_sums, axis=0).T
    dscores_low = dscores.astype(LOW)
    dread = dread + mm_tn(dscores_low, write)
    dwrite = dwrite + mm(dscores_low, read)
    dstep = dstep + source_sums / jnp.maximum(step, 1e-30)
    dcum = dcum + target_sums - source_sums
    dcum = dcum + jnp.where(iota((length, 1), 0) == length - 1, dlast, 0.0)
    dlog = running_sum(iota((length, length), 0) <= iota((length, length), 1), dcum)
    dstep = dstep - dlog * rate[...]
    draw = dstep * sigmoid(shifted)
    draw_low = draw.astype(LOW)
    steps_low[...] = draw_low
    heads_out[0:1] += jnp.sum(draw, axis=0, keepdims=True)
    heads_out[1:2] += jnp.sum(dlog * log_decay, axis=0, keepdims=True)

    dactive = step_wide * jnp.concatenate(parts, axis=1) + skip[...] * dy + toward_wide * from_grad
    dpre = dactive * (sig * (1.0 + pre * (1.0 - sig)))
    grad, taps_grads = conv_back(dpre, carry_z, taps_i[...], inner_v[...].astype(F32), aux)
    low = grad.astype(LOW)
    inner_low[...] = low
    inner_out[...] += mm(normed_t[...], low)
    steps_out[...] += mm(normed_t[...], draw_low)
    for tap in range(4):
        rows_out[tap : tap + 1] += taps_grads[tap]
    rows_out[4:5] += jnp.sum(dpre, axis=0, keepdims=True)
    rows_out[5:6] += jnp.sum(dy * active_wide, axis=0, keepdims=True)
    store_pieces(me_ref[0], jnp.concatenate([dwrite, dread], axis=1).T, keep, give)

    @pl.when(at == pl.num_programs(0) - 1)
    def _():
        inner_sum[...] = inner_out[...].astype(LOW)
        state_out[...] = back[...]
        carry_out[...] = carry_z[...]


def return_kernel(gate_low, inner_low, steps_low, gate_w, inner_w, step_w, local):
    local[...] = (
        mm_nt(gate_w[...], gate_low[...])
        + mm_nt(inner_w[...], inner_low[...])
        + mm_nt(step_w[...], steps_low[...])
    )


def state_kernel(
    me_ref, part_a, part_b, part_c, state_c, state_v, normed_ref, local_ref, aux_ref, taps, state_w,
    steps_in, rows_in, heads_in,
    keep, give, row_dot, late, carry_z, total, gain_total, rows_out,
):
    at = pl.program_id(0)
    me = me_ref[0]

    @pl.when(at == 0)
    def _():
        carry_z[...] = jnp.zeros_like(carry_z)
        total[...] = jnp.zeros_like(total)
        rows_out[...] = jnp.zeros_like(rows_out)
        gain_total[...] = jnp.zeros_like(gain_total)

    def own(values):
        values = values.astype(F32)
        width = values.shape[1] // 4
        picked = jnp.where((me & 2) == 2, values[:, 2 * width :], values[:, : 2 * width])
        return jnp.where((me & 1) == 1, picked[:, width:], picked[:, :width])

    dpairs = (part_a[0].astype(F32) + part_b[0].astype(F32) + part_c[...].astype(F32)).T
    pre = own(state_c[...])
    sig = sigmoid(pre)
    dpre = dpairs * (sig * (1.0 + pre * (1.0 - sig)))
    grad, taps_grads = conv_back(dpre, carry_z, taps[...], own(state_v[...]), aux_ref[...])
    low = grad.astype(LOW)
    for tap in range(4):
        rows_out[tap : tap + 1] += taps_grads[tap]
    rows_out[4:5] += jnp.sum(dpre, axis=0, keepdims=True)
    normed_t = normed_ref[...]
    total[...] += mm(normed_t, low)
    values = local_ref[...] + mm_nt(state_w[...], low)
    store_pieces(me, values, keep, give)
    product = values * normed_t.astype(F32)
    row_dot[0] = jnp.sum(product, axis=0, keepdims=True)
    gain_total[...] += sum(
        product[:, at : at + 128] for at in range(0, product.shape[1], 128)
    )

    @pl.when(at == pl.num_programs(0) - 1)
    def _():
        states, channels, heads = total.shape[1], rows_in.shape[1], heads_in.shape[1]
        width = total.shape[0]
        column = jnp.sum(gain_total[...], axis=1, keepdims=True)
        taps_row = [rows_out[row : row + 1] for row in range(5)]
        taps_row = jnp.concatenate([*taps_row, jnp.zeros((1, width - 5 * states), F32)], axis=1)
        lists = jnp.concatenate(
            [rows_in[...], heads_in[...], jnp.zeros((8, width - channels - heads), F32)], axis=1
        )
        late[...] = jnp.concatenate(
            [
                total[...].T,
                taps_row,
                jnp.broadcast_to(column, gain_total.shape).T[0:1],
                jnp.zeros((14, width), F32),
                steps_in[...].T[0:8],
                lists,
            ],
            axis=0,
        ).astype(LOW)


def lists_kernel(own, step_grad, taps_grad, offset_grad, out_gain_grad, skip_grad, head_grads):
    channels = taps_grad.shape[1]
    values = own[...].astype(F32)
    step_grad[...] = values[0:8]
    rows = values[8:16, 0:channels]
    taps_grad[...] = rows[0:4]
    offset_grad[...] = rows[4:5]
    out_gain_grad[...] = rows[6:7]
    skip_grad[...] = collapse(rows, 128)
    head_grads[...] = values[8:16, channels : channels + 128]


def state_grads_kernel(
    me_ref, m0, m1, m2, m3, gain, state_w_grad, taps_grad, offset_grad, gain_grad, gathered, rows
):
    states = gathered.shape[1]
    total = jnp.zeros(gain.shape, F32)
    for relative, member in enumerate((m0, m1, m2, m3)):
        dest = me_ref[0] ^ relative
        values = member[...].astype(F32)
        gathered[pl.ds(dest, 1)] = values[0:states][None]
        rows[pl.ds(dest, 1)] = values[states : states + 1][None]
        total = total + values[states + 1 : states + 2]
    state_w_grad[...] = gathered[...].reshape(4 * states, gain.shape[1]).T
    gain_grad[...] = total / gain[...]
    for tap in range(5):
        cut = slice(tap * states, (tap + 1) * states)
        row = jnp.concatenate([rows[dest][:, cut] for dest in range(4)], axis=1)
        if tap < 4:
            taps_grad[tap : tap + 1] = row
        else:
            offset_grad[...] = row


def weight_grads_kernel(
    me_ref, early_own, early_got, inner_own, inner_got, out_w_grad, gate_w_grad, inner_w_grad
):
    upper = me_ref[1] == 1
    own, got = early_own[...].astype(F32), early_got[...].astype(F32)
    out_w_grad[...] = jnp.where(upper, got, own).T
    gate_w_grad[...] = jnp.where(upper, own, got)
    own, got = inner_own[...].astype(F32), inner_got[...].astype(F32)
    half = own.shape[0]
    inner_w_grad[0:half] = jnp.where(upper, got, own)
    inner_w_grad[half:] = jnp.where(upper, own, got)


def rows(columns, index, size=BLOCK):
    return pl.BlockSpec((size, columns), lambda i: (index(i), 0))


def slab(shape, index):
    return pl.BlockSpec((1, *shape), lambda i: (index(i),) + (0,) * len(shape))


def whole(shape):
    return pl.BlockSpec(shape, lambda i: (0,) * len(shape))


def flat(features, index, size=BLOCK):
    return pl.BlockSpec((features, size), lambda i: (0, index(i)))


def packed(count, features, index, size=BLOCK):
    return pl.BlockSpec((count, features, size), lambda i: (0, 0, index(i)))


SCALAR = pl.BlockSpec(memory_space=pltpu.SMEM)


def call(kernel, blocks, ins, outs, scratch, flops, fill=()):
    count = len(ins)
    ins = [*ins, *((array, pl.BlockSpec(memory_space=pl.ANY)) for _, array in fill)]
    aliases = {count + at: out for at, (out, _) in enumerate(fill)}
    if fill:
        inner_kernel = kernel

        def kernel(*refs):
            return inner_kernel(*refs[:count], *refs[count + len(fill) :])

    arrays = [array for array, _ in ins]
    shapes = [jax.ShapeDtypeStruct(shape, dtype) for shape, dtype, _ in outs]
    return pl.pallas_call(
        kernel,
        grid=(blocks,),
        in_specs=[spec for _, spec in ins],
        out_specs=[spec for _, _, spec in outs],
        out_shape=shapes,
        scratch_shapes=scratch,
        input_output_aliases=aliases,
        compiler_params=pltpu.CompilerParams(
            dimension_semantics=("arbitrary",), vmem_limit_bytes=VMEM_BYTES
        ),
        cost_estimate=pl.CostEstimate(flops=flops, bytes_accessed=1, transcendentals=0),
    )(*arrays)


def swap(values, axis, bit):
    size = lax.axis_size(axis)
    return lax.ppermute(values, axis, [(i, i ^ bit) for i in range(size)])


def small_sum(values, axis):
    size = lax.axis_size(axis)
    if size & (size - 1):
        return lax.psum(values, axis)
    bit = 1
    while bit < size:
        values = values + swap(values, axis, bit)
        bit *= 2
    return values


def split_half(values, axis, bit):
    half = values.shape[0] // 2
    upper = (lax.axis_index(axis) & bit) // bit
    kept = lax.dynamic_slice_in_dim(values, upper * half, half, 0)
    given = lax.dynamic_slice_in_dim(values, (1 - upper) * half, half, 0)
    return kept, swap(given, axis, bit)


def join_half(values, axis, bit):
    return place_half(values, swap(values, axis, bit), axis, bit)


def place_half(values, got, axis, bit):
    upper = (lax.axis_index(axis) & bit) > 0
    return jnp.concatenate(
        [jnp.where(upper, got, values), jnp.where(upper, values, got)], axis=0
    )


def add_low(left, right):
    return (left.astype(F32) + right.astype(F32)).astype(LOW)


def axis_bits(axis):
    size = lax.axis_size(axis)
    return [] if size & (size - 1) else [1 << k for k in range(size.bit_length() - 1)]


def in_order(index, pieces):
    one, two = (index & 1) == 1, (index & 2) == 2
    a, b, c, d = pieces
    a, b, c, d = (
        jnp.where(one, b, a), jnp.where(one, a, b), jnp.where(one, d, c), jnp.where(one, c, d)
    )
    return (
        jnp.where(two, c, a), jnp.where(two, d, b), jnp.where(two, a, c), jnp.where(two, b, d)
    )


def gather_pieces(values):
    across = swap(values, "tensor", 2)
    return values, swap(values, "tensor", 1), across, swap(across, "tensor", 1)


def after(values, *earlier):
    return lax.optimization_barrier((values, *earlier))


def scatter_sum(keep, give):
    got = swap(give, "tensor", 1)
    middle = (keep[1].astype(F32) + got[1].astype(F32)).astype(LOW)
    return keep, got, middle


def body(
    hidden, segments, norm_gain, gate_weight, inner_weight, state_weight, step_weight, inner_taps,
    inner_offset, state_taps, state_offset, step_bias, decay_log, skip_weight, out_gain, out_weight,
    cotangent,
):
    tensor_index = lax.axis_index("tensor")
    me = jnp.stack([tensor_index, lax.axis_index("dp") & 1]).astype(jnp.int32)
    own_hidden, own_upstream, segment = hidden[0].T, cotangent[0].T, segments[0]
    part, tokens = own_hidden.shape
    features, channels = gate_weight.shape
    heads = step_weight.shape[1]
    states = state_weight.shape[1]
    half = states // 2
    own_states = states // 4
    blocks = tokens // BLOCK
    lanes = 128
    full_width = channels * lax.axis_size("tensor")
    ahead = lambda i: i
    behind = lambda i: blocks - 1 - i
    wide = 2 * BLOCK if tokens % (2 * BLOCK) == 0 else BLOCK
    longer = 2 * wide if tokens % (2 * wide) == 0 else wide
    behind_wide = lambda i: tokens // wide - 1 - i

    sections = 2 if blocks % 2 == 0 else 1
    cut = tokens // sections
    starts = [own_hidden[:, at * cut : (at + 1) * cut] for at in range(sections)]
    crossed = []
    for start in starts:
        if crossed:
            start, crossed[-1] = after(start, crossed[-1])
        crossed.append(swap(start, "tensor", 2))
    upstream_start, crossed[0] = after(own_upstream, crossed[0])
    upstream_across = swap(upstream_start, "tensor", 2)

    seg_blocks = segment.reshape(blocks, BLOCK)
    last_seg = seg_blocks[:, -1]
    previous = jnp.concatenate([jnp.full((1,), -1, jnp.int32), last_seg[:-1]])
    columns = []
    for back in range(1, 4):
        padded = jnp.pad(segment, (back, 0), constant_values=-1)[:tokens]
        columns.append(padded == segment)
    columns.append((seg_blocks == last_seg[:, None]).reshape(tokens))
    columns.append((seg_blocks == previous[:, None]).reshape(tokens))
    columns.append(segment)
    aux = jnp.stack([c.astype(F32) for c in columns] + [jnp.zeros((tokens,), F32)] * 2, axis=1)
    seg_rows = seg_blocks.astype(F32)[:, None, :]
    carry_mask = jnp.broadcast_to(
        (last_seg == previous).astype(F32)[:, None, None], (blocks, 1, lanes)
    )
    pad_heads = lambda v: jnp.pad(v, (0, lanes - heads))[None]
    step_w = jnp.pad(step_weight, ((0, 0), (0, lanes - heads)))
    bias_row = pad_heads(step_bias)
    rate_row = pad_heads(jnp.exp(decay_log))
    skip_row = jnp.repeat(skip_weight, HEAD)[None]
    gain_column = norm_gain[:, None]
    out_w_t = out_weight.T
    out_gain_row = out_gain[None]

    weight_spec = whole((features, channels))
    states_shapes = [(half, channels), (8, channels), (8, states)]
    carried = [jnp.zeros(shape, F32) for shape in states_shapes]
    filled = []
    for section in range(sections):
        count = blocks // sections
        onward = lambda i, base=section * count: base + i
        pieces = (
            starts[section],
            swap(starts[section], "tensor", 1),
            crossed[section],
            swap(crossed[section], "tensor", 1),
        )
        got_all = call(
            forward_kernel,
            count,
            [
                (me, SCALAR),
                *[(piece, flat(part, ahead)) for piece in pieces],
                (gain_column, whole((features, 1))),
                (gate_weight, weight_spec),
                (inner_weight, weight_spec),
                (state_weight, whole((features, states))),
                (step_w, whole((features, lanes))),
                (inner_taps, whole((4, channels))),
                (inner_offset[None], whole((1, channels))),
                (state_taps, whole((4, states))),
                (state_offset[None], whole((1, states))),
                (bias_row, whole((1, lanes))),
                (rate_row, whole((1, lanes))),
                (skip_row, whole((1, channels))),
                (aux, rows(8, onward)),
                (seg_rows, slab((1, BLOCK), onward)),
                (carry_mask, slab((1, lanes), onward)),
                *[(array, whole(array.shape)) for array in carried],
            ],
            [
                ((features, tokens), LOW, flat(features, onward)),
                ((tokens, channels), F32, rows(channels, onward)),
                ((tokens, channels), LOW, rows(channels, onward)),
                ((tokens, channels), F32, rows(channels, onward)),
                ((tokens, states), LOW, rows(states, onward)),
                ((tokens, states), F32, rows(states, onward)),
                ((tokens, states), LOW, rows(states, onward)),
                ((tokens, lanes), F32, rows(lanes, onward)),
                ((tokens, channels), F32, rows(channels, onward)),
                ((blocks, half, channels), LOW, slab((half, channels), onward)),
                ((blocks, 1, BLOCK), F32, slab((1, BLOCK), onward)),
                *[(shape, F32, whole(shape)) for shape in states_shapes],
            ],
            [
                *[pltpu.VMEM(shape, F32) for shape in states_shapes],
                pltpu.VMEM((4, part, BLOCK), LOW),
            ],
            1,
            list(enumerate(filled)),
        )
        if section + 1 < sections:
            crossed[section + 1], *got_all = after(crossed[section + 1], *got_all)
        filled, carried = got_all[:11], got_all[11:]
    normed, gate, inner_v, inner_c, state_v, state_c, pairs, raw, y, entering, scale = filled

    upstream_across, y = after(upstream_across, y)
    upstream_own, y = after(own_upstream, y)
    upstream_pieces = (
        own_upstream,
        swap(upstream_own, "tensor", 1),
        upstream_across,
        swap(upstream_across, "tensor", 1),
    )
    upstream, normal_grad, sums = call(
        sums_kernel,
        tokens // longer,
        [
            (me, SCALAR),
            *[(piece, flat(part, ahead, longer)) for piece in upstream_pieces],
            (gate, rows(channels, ahead, longer)),
            (y, rows(channels, ahead, longer)),
            (out_w_t, weight_spec),
            (out_gain_row, whole((1, channels))),
        ],
        [
            ((features, tokens), LOW, flat(features, ahead, longer)),
            ((tokens, channels), F32, rows(channels, ahead, longer)),
            ((tokens // longer, 2, longer), F32, slab((2, longer), ahead)),
        ],
        [pltpu.VMEM((4, part, longer), LOW)],
        1,
    )
    sums = small_sum(sums, "tensor")

    piece_shape = (2, part, tokens)
    keep_o, give_o, early_kept, early_given, out_gain_grad, gate_low, dy = call(
        functools.partial(output_kernel, full_width),
        tokens // wide,
        [
            (me, SCALAR),
            (sums, pl.BlockSpec((1, 2, wide), lambda i: (i * wide // longer, 0, i % (longer // wide)))),
            (upstream, flat(features, ahead, wide)),
            (gate, rows(channels, ahead, wide)),
            (y, rows(channels, ahead, wide)),
            (normal_grad, rows(channels, ahead, wide)),
            (normed, flat(features, ahead, wide)),
            (out_w_t, weight_spec),
            (out_gain_row, whole((1, channels))),
        ],
        [
            (piece_shape, LOW, packed(2, part, ahead, wide)),
            (piece_shape, LOW, packed(2, part, ahead, wide)),
            ((features, channels), LOW, weight_spec),
            ((features, channels), LOW, weight_spec),
            ((1, channels), F32, whole((1, channels))),
            ((tokens, channels), LOW, rows(channels, ahead, wide)),
            ((tokens, channels), F32, rows(channels, ahead, wide)),
        ],
        [pltpu.VMEM((features, channels), F32)] * 2,
        1,
    )
    keep_o, got_o, middle_o = scatter_sum(keep_o, give_o)
    bits = axis_bits("dp")
    by_steps = len(bits) > 2 and features % (1 << len(bits)) == 0
    early = []
    if by_steps:
        early = [early_kept, swap(early_given, "dp", bits[0])]
    else:
        flipped = (lax.axis_index("dp") & 1) > 0
        early_grad = jnp.concatenate(
            [
                jnp.where(flipped, early_given, early_kept),
                jnp.where(flipped, early_kept, early_given),
            ],
            axis=0,
        )
        early_grad = lax.psum(early_grad, "dp")
    dy, middle_o = after(dy, middle_o)
    branch_parts = (keep_o, got_o, swap(middle_o, "tensor", 2))

    pair_shape = (2, own_states, tokens)
    sums_shapes = [
        (half, channels), (3, 8, channels), (8, lanes), (features, channels), (features, lanes),
    ]
    carried = []
    row_grads = jnp.pad(out_gain_grad, ((6, 1), (0, 0)))
    filled = []
    parts_of_scan = 2 if blocks % 2 == 0 else 1
    for section in range(parts_of_scan):
        count = blocks // parts_of_scan
        top = blocks - 1 - section * count
        back_from = lambda i, top=top: top - i
        got_all = call(
            functools.partial(backward_kernel, len(carried)),
            count,
            [
                (me, SCALAR),
                (pairs, rows(states, back_from)),
                (inner_c, rows(channels, back_from)),
                (inner_v, rows(channels, back_from)),
                (raw, rows(lanes, back_from)),
                (dy, rows(channels, back_from)),
                (entering, slab((half, channels), back_from)),
                (aux, rows(8, back_from)),
                (seg_rows, slab((1, BLOCK), back_from)),
                (carry_mask, slab((1, lanes), back_from)),
                (inner_taps, whole((4, channels))),
                (bias_row, whole((1, lanes))),
                (rate_row, whole((1, lanes))),
                (skip_row, whole((1, channels))),
                (normed, flat(features, back_from)),
                (row_grads, whole((8, channels))),
                *[(array, whole(array.shape)) for array in carried],
            ],
            [
                ((tokens, channels), LOW, rows(channels, back_from)),
                (pair_shape, LOW, packed(2, own_states, back_from)),
                (pair_shape, LOW, packed(2, own_states, back_from)),
                ((tokens, lanes), LOW, rows(lanes, back_from)),
                *[(shape, F32, whole(shape)) for shape in sums_shapes],
                ((8, channels), F32, whole((8, channels))),
                ((features, channels), LOW, weight_spec),
            ],
            [pltpu.VMEM((half, channels), F32), pltpu.VMEM((3, 8, channels), F32)],
            1,
            list(enumerate(filled)),
        )
        if section == 0 and by_steps:
            *got_all, kept, given = after(*got_all, *early)
            early = [kept, given]
            early_grad = add_low(*early)
            early = list(split_half(early_grad, "dp", bits[1]))
        filled, carried, row_grads, inner_w_grad = (
            got_all[:4], got_all[4:9], got_all[9], got_all[10]
        )
    got_branch, *held = after(branch_parts[2], *filled, *carried[2:], row_grads, inner_w_grad, *early)
    branch_parts = (*branch_parts[:2], got_branch)
    inner_low, keep_p, give_p, steps_low, head_grads, _, step_w_grad, row_grads, inner_w_grad = held[:9]
    early = held[9:]
    keep_p, got_p, middle_p = scatter_sum(keep_p, give_p)
    late_i = []
    if by_steps:
        early_grad = add_low(*early)
        early = list(split_half(early_grad, "dp", bits[2]))
        late_i = list(split_half(inner_w_grad, "dp", bits[0]))
    else:
        inner_w_grad = lax.psum(inner_w_grad, "dp")
    inner_low, middle_p = after(inner_low, middle_p)
    pair_parts = (keep_p, got_p, swap(middle_p, "tensor", 2))

    local = call(
        return_kernel,
        tokens // wide,
        [
            (gate_low, rows(channels, ahead, wide)),
            (inner_low, rows(channels, ahead, wide)),
            (steps_low, rows(lanes, ahead, wide)),
            (gate_weight, weight_spec),
            (inner_weight, weight_spec),
            (step_w, whole((features, lanes))),
        ],
        [
            ((features, tokens), F32, flat(features, ahead, wide)),
        ],
        [],
        1,
    )[0]

    if by_steps:
        local, *moved = after(local, *early, *late_i)
        early_grad = add_low(*moved[:2])
        for bit in bits[3:]:
            early_grad = add_low(*split_half(early_grad, "dp", bit))
        for bit in reversed(bits[3:]):
            early_grad = join_half(early_grad, "dp", bit)
        early_got = swap(early_grad, "dp", bits[2])
        inner_w_grad = add_low(*moved[2:])
        late_i = list(split_half(inner_w_grad, "dp", bits[1]))
    own_start = tensor_index * own_states
    own_taps = lax.dynamic_slice_in_dim(state_taps, own_start, own_states, 1)
    own_state_w = lax.dynamic_slice_in_dim(state_weight, own_start, own_states, 1)
    keep_n, give_n, row_dot, late = call(
        state_kernel,
        tokens // wide,
        [
            (me, SCALAR),
            (pair_parts[0], packed(1, own_states, behind_wide, wide)),
            (pair_parts[1], packed(1, own_states, behind_wide, wide)),
            (pair_parts[2], flat(own_states, behind_wide, wide)),
            (state_c, rows(states, behind_wide, wide)),
            (state_v, rows(states, behind_wide, wide)),
            (normed, flat(features, behind_wide, wide)),
            (local, flat(features, behind_wide, wide)),
            (aux, rows(8, behind_wide, wide)),
            (own_taps, whole((4, own_states))),
            (own_state_w, whole((features, own_states))),
            (step_w_grad, whole((features, lanes))),
            (row_grads, whole((8, channels))),
            (head_grads, whole((8, lanes))),
        ],
        [
            (piece_shape, LOW, packed(2, part, behind_wide, wide)),
            (piece_shape, LOW, packed(2, part, behind_wide, wide)),
            ((tokens // wide, 1, wide), F32, slab((1, wide), behind_wide)),
            ((own_states + 32, features), LOW, whole((own_states + 32, features))),
        ],
        [
            pltpu.VMEM((3, 8, own_states), F32),
            pltpu.VMEM((features, own_states), F32),
            pltpu.VMEM((features, lanes), F32),
            pltpu.VMEM((8, own_states), F32),
        ],
        1,
    )
    if by_steps:
        early_got, *late_i, keep_n, give_n, row_dot, late = after(
            early_got, *late_i, keep_n, give_n, row_dot, late
        )
        early_grad = place_half(early_grad, early_got, "dp", bits[2])
        early_got = swap(early_grad, "dp", bits[1])
        inner_w_grad = add_low(*late_i)
    keep_n, got_n, middle_n = scatter_sum(keep_n, give_n)
    crossed_dot = swap(row_dot, "tensor", 2)
    row_dot, crossed_dot, middle_n = after(row_dot, crossed_dot, middle_n)
    row_dot = row_dot + crossed_dot
    late, middle_n = after(late, middle_n)
    grad_parts = (keep_n, got_n, swap(middle_n, "tensor", 2))
    row_dot = row_dot + swap(row_dot, "tensor", 1)
    if by_steps:
        for bit in bits[2:]:
            inner_w_grad = add_low(*split_half(inner_w_grad, "dp", bit))
        inner_got = swap(inner_w_grad, "dp", bits[-1])

    def total_of(parts):
        keep, got, last = parts
        return keep[0].astype(F32) + got[0].astype(F32) + last.astype(F32)

    own_gain = lax.dynamic_slice_in_dim(norm_gain, tensor_index * part, part, 0)
    if by_steps:
        late_got = swap(late, "dp", bits[0])
        early_got, late_got = after(early_got, late_got)
        early_grad = place_half(early_grad, early_got, "dp", bits[1])
        early_grad, late_got, inner_got = after(early_grad, late_got, inner_got)
        early_got = swap(early_grad, "dp", bits[0])
        late = add_low(late, late_got)
        late_got = swap(late, "dp", bits[1])
        inner_w_grad = place_half(inner_w_grad, inner_got, "dp", bits[-1])
        for bit in reversed(bits[1:-1]):
            inner_w_grad = join_half(inner_w_grad, "dp", bit)
        inner_got = swap(inner_w_grad, "dp", bits[0])
        hidden_again, late_got = after(own_hidden, late_got)
        late = add_low(late, late_got)
    else:
        late = lax.psum(late, "dp")
        hidden_again = own_hidden
    output = (hidden_again.astype(F32) + total_of(branch_parts)).astype(LOW).T
    if by_steps:
        for bit in bits[2:]:
            late_got = swap(late, "dp", bit)
            output, late_got = after(output, late_got)
            late = add_low(late, late_got)
    factor = scale.reshape(1, tokens)
    shrink = factor * factor * row_dot.reshape(1, tokens) / features
    input_grad = (
        own_upstream.astype(F32)
        + factor * (total_of(grad_parts) * own_gain[:, None])
        - own_hidden.astype(F32) * shrink
    ).T
    top = own_states + 16
    members = list(gather_pieces(late[:top]))
    if by_steps:
        early_got, inner_got, members[2] = after(early_got, inner_got, members[2])
        out_w_grad, gate_w_grad, inner_w_grad = call(
            weight_grads_kernel,
            1,
            [
                (me, SCALAR),
                (early_grad, weight_spec),
                (early_got, weight_spec),
                (inner_w_grad, whole(inner_w_grad.shape)),
                (inner_got, whole(inner_got.shape)),
            ],
            [
                ((channels, features), F32, whole((channels, features))),
                ((features, channels), F32, weight_spec),
                ((features, channels), F32, weight_spec),
            ],
            [],
            1,
        )
    else:
        out_w_grad = early_grad[:features].T.astype(F32)
        gate_w_grad = early_grad[features:].astype(F32)
        inner_w_grad = inner_w_grad.astype(F32)
    input_grad, out_w_grad, *members = after(input_grad, out_w_grad, *members)
    row_384 = ((1, channels), F32, whole((1, channels)))
    row_lanes = ((8, lanes), F32, whole((8, lanes)))
    step_grad, taps_grad, offset_grad, out_gain_grad, skip_grad, head_grads = call(
        lists_kernel,
        1,
        [(late[top:], whole((16, features)))],
        [
            ((8, features), F32, whole((8, features))),
            ((4, channels), F32, whole((4, channels))),
            row_384,
            row_384,
            row_lanes,
            row_lanes,
        ],
        [],
        1,
    )
    state_w_grad, state_taps_grad, state_offset_grad, norm_gain_grad = call(
        state_grads_kernel,
        1,
        [
            (me, SCALAR),
            *[(member, whole(member.shape)) for member in members],
            (norm_gain[None], whole((1, features))),
        ],
        [
            ((features, states), F32, whole((features, states))),
            ((4, states), F32, whole((4, states))),
            ((1, states), F32, whole((1, states))),
            ((1, features), F32, whole((1, features))),
        ],
        [pltpu.VMEM((4, own_states, features), F32), pltpu.VMEM((4, 1, features), F32)],
        1,
    )

    return (
        output[None],
        input_grad[None],
        norm_gain_grad[0],
        gate_w_grad,
        inner_w_grad,
        state_w_grad,
        step_grad[:heads].T,
        taps_grad,
        offset_grad[0],
        state_taps_grad,
        state_offset_grad[0],
        head_grads[0, :heads],
        head_grads[1, :heads],
        skip_grad[5, :heads],
        out_gain_grad[0],
        out_w_grad,
    )


def solution(mesh):
    rows_spec = P("dp", None, "tensor")
    columns_spec = P(None, "tensor")
    in_specs = (
        rows_spec, P("dp", None), P(), columns_spec, columns_spec, P(), columns_spec, columns_spec,
        P("tensor"), P(), P(), P("tensor"), P("tensor"), P("tensor"), P("tensor"),
        P("tensor", None), rows_spec,
    )
    out_specs = (
        rows_spec, rows_spec, P(), columns_spec, columns_spec, P(), columns_spec, columns_spec,
        P("tensor"), P(), P(), P("tensor"), P("tensor"), P("tensor"), P("tensor"),
        P("tensor", None),
    )
    return jax.shard_map(body, mesh=mesh, in_specs=in_specs, out_specs=out_specs, check_vma=False)
```
